32 devices in a mesh: rep: 8 (over y, x, core), grp: 4 (over z).
Axes of the slice: x: 2, y: 2, z: 4, core: 2. Of those that a mesh axis runs over, the one named last changes fastest.
Arguments:
- grads: bfloat16 [32, 2, 320, 2048], P(('rep', 'grp')), may hold values from -6 to 6
- errors: float32 [32, 2, 320, 2048], P(('rep', 'grp')), may hold values from -4 to 4
- warm_start: float32 [2, 32, 2048], replicated, may hold values from -0.125 to 0.125
- vec_grads: float32 [32, 2, 2048], P(('rep', 'grp')), may hold values from -6 to 6
- owners: int32 [12], replicated, may hold values from 0 to 31, as said below
- mat_momentum: float32 [64, 64, 2048], P(('rep', 'grp')), may hold values from -0.3 to 0.3
- mat_weights: float32 [64, 64, 2048], P(('rep', 'grp')), may hold values from -0.3 to 0.3
- vec_momentum: float32 [64, 2048], P(('rep', 'grp')), may hold values from -0.3 to 0.3
- vec_weights: float32 [64, 2048], P(('rep', 'grp')), may hold values from 0.5 to 1.5
Outputs:
- new_errors: float32 [32, 2, 320, 2048], P(('rep', 'grp'))
- mat_momentum_out: float32 [64, 64, 2048], P(('rep', 'grp'))
- mat_weights_out: float32 [64, 64, 2048], P(('rep', 'grp'))
- vec_momentum_out: float32 [64, 2048], P(('rep', 'grp'))
- vec_weights_out: float32 [64, 2048], P(('rep', 'grp'))
The draws below stay inside these ranges and needn't reach their ends.
Inputs may be any that keep to these rules, and one draw needn't show every extreme that they name: `owners`: no replica owns more than 2 items, and some replica owns exactly 2. Replicas 0 and 31 each own at least one item.
All inputs are finite; a program needn't handle non-finite values.
Results may differ from the reference program's by a relative error of at most 0.0003.
Values sent between devices are 32-bit elements; how exact they have to be, the bound alone decides.
No kernel may reach another device: no remote copies, remote signals or barrier semaphores. Data moves between devices by JAX's collectives and lax.ppermute only.
A program may use at most 64 MiB of HBM per device.

```python
import jax
import jax.numpy as jnp
from jax import lax

D = 2048
KVH = 5
HD = 64
R = 32
SLOTS = 2
ROOT_ITERS = 12
KVW = 320
REPLICAS = 32
NITEM = 12


def draw_owners(key, part):
    key_perm, key_pick, key_order = jax.random.split(key, 3)
    middle = jax.random.permutation(key_perm, REPLICAS - 2)[:NITEM - 3] + 1
    ends = jnp.array([0, REPLICAS - 1], dtype=jnp.int32)
    devices = jnp.concatenate([ends, middle.astype(jnp.int32)])
    extra = devices[jax.random.randint(key_pick, (), 0, NITEM - 1)]
    full = jnp.concatenate([devices, extra[None]])
    order = jax.random.permutation(key_order, NITEM)
    return full[order].astype(jnp.int32)


def levels(rng, extent, pieces, least, largest):
    factor_of, own = 1.0, jax.random.fold_in(rng, 6)
    for position, parts in pieces:
        heights = jnp.exp(jax.random.uniform(jax.random.fold_in(own, position), (parts,), jnp.float32, least / len(pieces), largest / len(pieces)))
        factor_of = factor_of * jnp.repeat(heights, extent[position] // parts).reshape([-1 if axis == position else 1 for axis in range(len(extent))])
    return factor_of


def normal_values(key, dims, scale, bound, shards=(), kind=jnp.bfloat16):
    drawn = jax.random.normal(key, dims, jnp.float32) * scale
    if len(shards) > 0:
        drawn = levels(key, dims, shards, -0.22, 0.18) * drawn
    return jnp.clip(drawn, min=-bound, max=bound).astype(kind)


def setup_inputs(seed: int = 0) -> dict:
    key_list = jax.random.split(jax.random.key(seed), 10)
    return {
        "grads": normal_values(key_list[0], (REPLICAS, 2, KVW, D), 1.0, 6.0, ((0, 32),)),
        "errors": normal_values(key_list[1], (REPLICAS, 2, KVW, D), 0.5, 4.0, ((0, 32),), jnp.float32),
        "warm_start": normal_values(key_list[2], (2, R, D), D ** -0.5, 0.125, (), jnp.float32),
        "vec_grads": normal_values(key_list[3], (REPLICAS, 2, D), 1.0, 6.0, ((0, 32),), jnp.float32),
        "owners": draw_owners(jax.random.fold_in(key_list[9], 71), 0),
        "mat_momentum": normal_values(key_list[5], (REPLICAS * SLOTS, HD, D), 0.05, 0.3, ((0, 32),), jnp.float32),
        "mat_weights": normal_values(key_list[6], (REPLICAS * SLOTS, HD, D), 0.05, 0.3, ((0, 32),), jnp.float32),
        "vec_momentum": normal_values(key_list[7], (REPLICAS * SLOTS, D), 0.05, 0.3, ((0, 32),), jnp.float32),
        "vec_weights": jnp.clip(1.0 + 0.1 * jax.random.normal(key_list[8], (REPLICAS * SLOTS, D), jnp.float32), 0.5, 1.5),
    }


high = lax.Precision.HIGHEST

def orthonormal(factor):
    gram_matrix = jnp.einsum('mkr,mks->mrs', factor, factor, precision=high)
    spread = jnp.sqrt(lax.optimization_barrier(jnp.sum(gram_matrix * gram_matrix, axis=(1, 2))))[:, None, None]
    identity_mat = jnp.broadcast_to(jnp.eye(gram_matrix.shape[1], dtype=jnp.float32), gram_matrix.shape).astype(gram_matrix.dtype)
    root_left = gram_matrix / spread
    root_right = identity_mat
    for sweep in range(ROOT_ITERS):
        middle = 1.5 * identity_mat - 0.5 * jnp.einsum('mrs,mst->mrt', root_right, root_left, precision=high)
        root_left = jnp.einsum('mrs,mst->mrt', root_left, middle, precision=high)
        root_right = jnp.einsum('mrs,mst->mrt', middle, root_right, precision=high)
    return jnp.einsum('mkr,mrs->mks', factor, root_right, precision=high) / jnp.sqrt(spread)

def replica_sum(term, grads, errors, init):

    def step(carry, pair):
        combined = pair[0].astype(jnp.float32) + pair[1]
        return (carry + term(combined), None)
    total, unused = lax.scan(step, init, (grads, errors))
    return total

def reference(grads, errors, warm_start, vec_grads, owners, mat_momentum, mat_weights, vec_momentum, vec_weights):
    q_factor = warm_start
    p_hat = None
    for round_index in range(2):
        p_sum = replica_sum(lambda c: jnp.einsum('mkd,mrd->mkr', c, q_factor, precision=high), grads, errors, jnp.zeros((2, KVW, R), jnp.float32))
        p_hat = orthonormal(p_sum / REPLICAS)
        q_sum = replica_sum(lambda c: jnp.einsum('mks,mkd->msd', p_hat, c, precision=high), grads, errors, jnp.zeros((2, R, D), jnp.float32))
        q_factor = q_sum / REPLICAS
    approx = jnp.einsum('mks,msd->mkd', p_hat, q_factor, precision=high)
    new_errors = lax.map(lambda pair: pair[0].astype(jnp.float32) + pair[1] - approx, (grads, errors))
    vec_avg = lax.optimization_barrier(jnp.sum(vec_grads, axis=0)) / REPLICAS
    earlier = jnp.arange(NITEM)[None, :] < jnp.arange(NITEM)[:, None]
    same = owners[None, :] == owners[:, None]
    slot = lax.optimization_barrier(jnp.sum((earlier & same).astype(jnp.int32), axis=1)).astype(jnp.int32)
    rows = (owners * SLOTS + slot).astype(jnp.int32)
    blocks = approx.reshape(2 * KVH, HD, D)
    for item in range(NITEM):
        where = rows[item]
        if item < 2 * KVH:
            moment = 0.9 * mat_momentum[where] + blocks[item]
            mat_momentum = mat_momentum.at[where].set(moment)
            mat_weights = mat_weights.at[where].set(mat_weights[where] - 0.5 * moment)
        else:
            moment = 0.9 * vec_momentum[where] + vec_avg[item - 2 * KVH]
            vec_momentum = vec_momentum.at[where].set(moment)
            vec_weights = vec_weights.at[where].set(vec_weights[where] - 0.5 * moment)
    return (new_errors, mat_momentum, mat_weights, vec_momentum, vec_weights)
```

```python
import functools

import jax
import jax.numpy as jnp
from jax import lax
from jax.experimental import pallas as pl
from jax.experimental.pallas import tpu as pltpu
from jax.sharding import PartitionSpec as P

ROOT_ITERS = 12
f32 = jnp.float32
VMEM_LIMIT = 48 * 1024 * 1024
NN = ((1,), (0,))
NT = ((1,), (1,))
TN = ((0,), (0,))


def dot(a, b, dims=NN):
    return lax.dot_general(
        a, b, (dims, ((), ())), precision=lax.Precision.HIGHEST, preferred_element_type=f32
    )


def split3(a):
    high = a.astype(jnp.bfloat16)
    rest = a - high.astype(f32)
    middle = rest.astype(jnp.bfloat16)
    low = (rest - middle.astype(f32)).astype(jnp.bfloat16)
    return high, middle, low


def params():
    return pltpu.CompilerParams(vmem_limit_bytes=VMEM_LIMIT)


def cost(flops, nbytes):
    return pl.CostEstimate(flops=flops, bytes_accessed=nbytes, transcendentals=0)


def outgoing_kernel(place, g_ref, e_ref, o_ref):
    o_ref[0] = g_ref[0, 0].astype(f32) + e_ref[0, 0]


def outgoing(place, grads, errors, blocks, streams, stream):
    rows, cols = grads.shape[2:]
    width = cols // (blocks * streams)

    def source(p, place):
        return (0, 1 - place[0], 0, (place[1] ^ p) * streams + stream)

    return pl.pallas_call(
        outgoing_kernel,
        grid_spec=pltpu.PrefetchScalarGridSpec(
            num_scalar_prefetch=1,
            grid=(blocks,),
            in_specs=[pl.BlockSpec((1, 1, rows, width), source)] * 2,
            out_specs=pl.BlockSpec((1, rows, width), lambda p, place: (p, 0, 0)),
        ),
        out_shape=jax.ShapeDtypeStruct((blocks, rows, width), f32),
        compiler_params=params(),
        cost_estimate=cost(blocks * rows * width, blocks * rows * width * 10),
        name=f"outgoing{stream}",
    )(place, grads, errors)


def pair_kernel(place, g_ref, e_ref, r_ref, w_ref, send_ref, keep_ref, p_ref, *, half):
    step = pl.program_id(0)
    total = g_ref[0, 0].astype(f32) + e_ref[0, 0] + r_ref[0]
    term = dot(w_ref[0], total, NT)

    @pl.when(step < half)
    def _():
        send_ref[0] = total

    @pl.when(step >= half)
    def _():
        keep_ref[0] = total

    @pl.when(step == 0)
    def _():
        p_ref[...] = term

    @pl.when(step > 0)
    def _():
        p_ref[...] += term


def pair(place, grads, errors, received, warm_start, blocks, streams, stream, bit):
    rows, cols = grads.shape[2:]
    rank = warm_start.shape[1]
    width = cols // (blocks * streams)
    half = blocks // 2

    def position(i):
        goes = jnp.where(i < half, 1, 0)
        h = lax.rem(i, half)
        low = h & ((1 << bit) - 1)
        return ((h >> bit) << (bit + 1)) | (goes << bit) | low

    def column(i, place):
        return (place[1] ^ position(i)) * streams + stream

    def source(i, place):
        return (0, place[0], 0, column(i, place))

    return pl.pallas_call(
        functools.partial(pair_kernel, half=half),
        grid_spec=pltpu.PrefetchScalarGridSpec(
            num_scalar_prefetch=1,
            grid=(blocks,),
            in_specs=[
                pl.BlockSpec((1, 1, rows, width), source),
                pl.BlockSpec((1, 1, rows, width), source),
                pl.BlockSpec((1, rows, width), lambda i, place: (position(i), 0, 0)),
                pl.BlockSpec((1, rank, width), lambda i, place: (place[0], 0, column(i, place))),
            ],
            out_specs=[
                pl.BlockSpec((1, rows, width), lambda i, place: (jnp.minimum(i, half - 1), 0, 0)),
                pl.BlockSpec((1, rows, width), lambda i, place: (jnp.maximum(i - half, 0), 0, 0)),
                pl.BlockSpec((rank, rows), lambda i, place: (0, 0)),
            ],
        ),
        out_shape=[
            jax.ShapeDtypeStruct((half, rows, width), f32),
            jax.ShapeDtypeStruct((half, rows, width), f32),
            jax.ShapeDtypeStruct((rank, rows), f32),
        ],
        compiler_params=params(),
        cost_estimate=cost(12 * rank * rows * cols // streams, blocks * rows * width * 14),
        name=f"pair{stream}",
    )(place, grads, errors, received, warm_start)


def whole_call(kernel, shapes, name, flops, *operands):
    nbytes = 4 * sum(o.size for o in operands)
    return pl.pallas_call(
        kernel,
        out_shape=[jax.ShapeDtypeStruct(s, f32) for s in shapes],
        compiler_params=params(),
        cost_estimate=cost(flops, nbytes),
        name=name,
    )(*operands)


def project_kernel(*refs, streams, count):
    x_ref, parts, (s_ref, v_ref) = refs[0], refs[1 : 1 + 2 * streams], refs[1 + 2 * streams :]
    rows = s_ref.shape[0]
    width = s_ref.shape[1] // streams
    factor = x_ref[:, :rows] / count
    for s in range(streams):
        block = parts[2 * s][...] + parts[2 * s + 1][...]
        where = slice(s * width, (s + 1) * width)
        s_ref[:, where] = block
        v_ref[:, where] = dot(factor, block) / count


def lift_kernel(v_ref, s_ref, u_ref, *, count):
    u_ref[...] = dot(v_ref[...], s_ref[...], NT) / count


def lower_kernel(u_ref, s_ref, v_ref, *, count):
    v_ref[...] = dot(u_ref[...], s_ref[...]) / count


def inverse_root(gram):
    rank = gram.shape[0]
    eye = (
        lax.broadcasted_iota(jnp.int32, (rank, rank), 0)
        == lax.broadcasted_iota(jnp.int32, (rank, rank), 1)
    ).astype(f32)
    spread = jnp.sqrt(jnp.sum(gram * gram, keepdims=True))
    left = gram / spread
    right = eye
    for sweep in range(ROOT_ITERS):
        if sweep == 0:
            middle = 1.5 * eye - 0.5 * left
            right = middle
        else:
            middle = 1.5 * eye - 0.5 * dot(right, left)
            right = dot(middle, right)
        if sweep + 1 < ROOT_ITERS:
            left = dot(left, middle)
    return right / jnp.sqrt(spread)


def first_root_kernel(x_ref, a_ref, *, rows, count):
    factor = x_ref[:, :rows] / count
    a_ref[...] = inverse_root(dot(factor, factor, NT))


def second_root_kernel(a_ref, u_ref, f_ref):
    a = a_ref[...]
    u = u_ref[...]
    rank, rows = u.shape
    gram = dot(a, dot(dot(u, u, NT), a), TN)
    both = dot(a, inverse_root(gram))
    f_ref[...] = jnp.zeros(f_ref.shape, f32)
    f_ref[:, :rows] = dot(both, u, TN)
    f_ref[:, rows : rows + rank] = both


def final_kernel(place, g_ref, e_ref, v0_ref, v1_ref, f0_ref, f1_ref, mm_ref, mw_ref,
                 n_ref, mo_ref, wo_ref, approx, left, *, head):
    rows, width = g_ref.shape[2:]
    rank = f0_ref.shape[0]

    @pl.when(pl.program_id(0) == 0)
    def _():
        for i, f_ref in enumerate((f0_ref, f1_ref)):
            high, middle, low = split3(f_ref[:, :rows].T)
            left[i] = jnp.concatenate([high, high, middle, high, low, middle], axis=1)

    for i, (v_ref, f_ref) in enumerate(((v0_ref, f0_ref), (v1_ref, f1_ref))):
        m = place[0] if i == 0 else 1 - place[0]
        q = dot(f_ref[:, rows : rows + rank], v_ref[0], TN)
        high, middle, low = split3(q)
        right = jnp.concatenate([high, middle, high, low, high, middle], axis=0)
        product = jnp.dot(left[i], right, preferred_element_type=f32)
        approx[pl.ds(m * rows, rows), :] = product
        n_ref[0, m] = g_ref[0, m].astype(f32) + e_ref[0, m] - product
    for slot in range(mm_ref.shape[0]):
        item = place[2 + slot]

        @pl.when(item >= 0)
        def _():
            block = approx[pl.ds(jnp.maximum(item, 0) * head, head), :]
            moment = 0.9 * mm_ref[slot] + block
            mo_ref[slot] = moment
            wo_ref[slot] = mw_ref[slot] - 0.5 * moment

        @pl.when(item < 0)
        def _():
            mo_ref[slot] = mm_ref[slot]
            wo_ref[slot] = mw_ref[slot]


def final(place, grads, errors, own_v, other_v, own_f, other_f, mat_momentum, mat_weights):
    blocks, rank, width = own_v.shape
    matrices, rows, cols = grads.shape[1:]
    slots, head = mat_momentum.shape[:2]

    def here(b, place):
        return (0, 0, 0, b)

    def there(b, place):
        return (place[1] ^ b, 0, 0)

    def whole(b, place):
        return (0, 0)

    def bank(b, place):
        return (0, 0, b)

    big = pl.BlockSpec((1, matrices, rows, width), here)
    small = pl.BlockSpec((slots, head, width), bank)
    return pl.pallas_call(
        functools.partial(final_kernel, head=head),
        grid_spec=pltpu.PrefetchScalarGridSpec(
            num_scalar_prefetch=1,
            grid=(blocks,),
            in_specs=[
                big,
                big,
                pl.BlockSpec((1, rank, width), there),
                pl.BlockSpec((1, rank, width), there),
                pl.BlockSpec(own_f.shape, whole),
                pl.BlockSpec(other_f.shape, whole),
                small,
                small,
            ],
            out_specs=[big, small, small],
            scratch_shapes=[
                pltpu.VMEM((matrices * rows, width), f32),
                pltpu.VMEM((matrices, rows, 6 * rank), jnp.bfloat16),
            ],
        ),
        out_shape=[
            jax.ShapeDtypeStruct(errors.shape, f32),
            jax.ShapeDtypeStruct(mat_momentum.shape, f32),
            jax.ShapeDtypeStruct(mat_weights.shape, f32),
        ],
        compiler_params=params(),
        cost_estimate=cost(2 * matrices * rows * cols * 6 * rank, 18_000_000),
        name="final",
    )(place, grads, errors, own_v, other_v, own_f, other_f, mat_momentum, mat_weights)


def exchange(a, axis, mask):
    return lax.ppermute(a, axis, [(i, i ^ mask) for i in range(lax.axis_size(axis))])


def local(grads, errors, warm_start, vec_grads, owners, mat_momentum, mat_weights, vec_momentum, vec_weights):
    reps, groups = lax.axis_size("rep"), lax.axis_size("grp")
    count = float(reps * groups)
    blocks = reps // 2
    bits = blocks.bit_length() - 1
    matrices, rows, cols = grads.shape[1:]
    rank = warm_start.shape[1]
    streams = 2 if (cols // blocks) % 256 == 0 else 1
    rep = lax.axis_index("rep")
    core, spot = rep % 2, rep // 2
    device = rep * groups + lax.axis_index("grp")

    items = owners.shape[0]
    slots, head = mat_momentum.shape[:2]
    earlier = jnp.arange(items)[None, :] < jnp.arange(items)[:, None]
    same = owners[None, :] == owners[:, None]
    slot = jnp.sum((earlier & same).astype(jnp.int32), axis=1)
    match = (owners[None, :] == device) & (slot[None, :] == jnp.arange(slots)[:, None])
    head_items = matrices * (rows // head)
    mat_match = match[:, :head_items]
    chosen = jnp.max(jnp.where(mat_match, jnp.arange(head_items)[None, :], -1), axis=1)
    place = jnp.concatenate([jnp.stack([core, spot]), chosen]).astype(jnp.int32)

    def z_sum(a):
        mask = 1
        while mask < groups:
            a = a + exchange(a, "grp", mask)
            mask *= 2
        return a

    def plane_sum(a):
        for bit in range(bits):
            a = a + exchange(a, "rep", 2 << bit)
        return a

    sent = [outgoing(place, grads, errors, blocks, streams, s) for s in range(streams)]
    received = [exchange(a, "rep", 1) for a in sent]
    vec_own = lax.dynamic_index_in_dim(vec_grads[0], core, 0, keepdims=False)
    vec_out = lax.dynamic_index_in_dim(vec_grads[0], 1 - core, 0, keepdims=False)
    vec_pair = vec_own + exchange(vec_out, "rep", 1)

    factor = None
    kept = []
    for s in range(streams):
        order = list(range(bits)) if s == 0 else list(range(bits))[::-1]
        send, keep, term = pair(
            place, grads, errors, received[s], warm_start, blocks, streams, s, order[0]
        )
        factor = term if factor is None else factor + term
        kept.append((order, keep, exchange(send, "rep", 2 << order[0])))
    packed = jnp.concatenate([factor, vec_pair.reshape(rank, cols // rank)], axis=1)
    packed = plane_sum(z_sum(packed))
    parts = []
    for order, keep, arrived in kept:
        left = sorted(order[1:])
        for bit in order[1:]:
            where = left.index(bit)
            left.remove(bit)
            shape = keep.shape
            view = (-1, 2, 1 << where) + shape[1:]
            a, b = keep.reshape(view), arrived.reshape(view)
            goes = a[:, 1] + b[:, 1]
            keep = (a[:, 0] + b[:, 0]).reshape((-1,) + shape[1:])
            arrived = exchange(goes.reshape((-1,) + shape[1:]), "rep", 2 << bit)
        parts += [keep[0], arrived[0]]

    width = cols // blocks
    kept_sum, v = whole_call(
        functools.partial(project_kernel, streams=streams, count=count),
        [(rows, width), (rank, width)], "project", 12 * rank * rows * width, packed, *parts,
    )
    (first_root,) = whole_call(
        functools.partial(first_root_kernel, rows=rows, count=count),
        [(rank, rank)], "root1", 24 * 12 * rank**3, packed,
    )
    v = z_sum(v)
    (u,) = whole_call(
        functools.partial(lift_kernel, count=count), [(rank, rows)], "lift", 12 * rank * rows * width, v, kept_sum,
    )
    u = plane_sum(z_sum(u))
    (v,) = whole_call(
        functools.partial(lower_kernel, count=count), [(rank, width)], "lower", 12 * rank * rows * width, u, kept_sum,
    )
    (own_f,) = whole_call(
        second_root_kernel, [packed.shape], "root2", 24 * 12 * rank**3, first_root, u,
    )
    v = z_sum(v)[None]
    for bit in range(bits):
        v = jnp.concatenate([v, exchange(v, "rep", 2 << bit)], axis=0)
    other_v = exchange(v, "rep", 1)
    other_f = exchange(own_f, "rep", 1)
    new_errors, mat_momentum_out, mat_weights_out = final(
        place, grads, errors, v, other_v, own_f, other_f, mat_momentum, mat_weights
    )

    vec_own = packed[:, rows:].reshape(1, cols) / count
    vec_other = exchange(vec_own, "rep", 1)
    vec_avg = jnp.where(core == 0, jnp.concatenate([vec_own, vec_other]), jnp.concatenate([vec_other, vec_own]))
    vec_match = match[:, head_items:]
    has_vec = jnp.any(vec_match, axis=1)[:, None]
    picked = sum(jnp.where(vec_match[:, i : i + 1], vec_avg[i : i + 1], 0.0) for i in range(items - head_items))
    vec_moment = 0.9 * vec_momentum + picked
    vec_momentum_out = jnp.where(has_vec, vec_moment, vec_momentum)
    vec_weights_out = jnp.where(has_vec, vec_weights - 0.5 * vec_moment, vec_weights)
    return (new_errors, mat_momentum_out, mat_weights_out, vec_momentum_out, vec_weights_out)


def solution(mesh):
    both = ("rep", "grp")
    return jax.shard_map(
        local,
        mesh=mesh,
        in_specs=(
            P(both, None, None, None),
            P(both, None, None, None),
            P(),
            P(both, None, None),
            P(),
            P(both, None, None),
            P(both, None, None),
            P(both, None),
            P(both, None),
        ),
        out_specs=(
            P(both, None, None, None),
            P(both, None, None),
            P(both, None, None),
            P(both, None),
            P(both, None),
        ),
        check_vma=False,
    )
```

```python
import functools

import jax
import jax.numpy as jnp
from jax import lax
from jax.experimental import pallas as pl
from jax.experimental.pallas import tpu as pltpu
from jax.sharding import PartitionSpec as P

ROOT_ITERS = 12
LANES = 128
f32 = jnp.float32
NN = ((1,), (0,))
NT = ((1,), (1,))
TN = ((0,), (0,))
ANY = pl.BlockSpec(memory_space=pl.ANY)
VMEM = pl.BlockSpec(memory_space=pltpu.VMEM)
SMEM = pl.BlockSpec(memory_space=pltpu.SMEM)


def dot(a, b, dims=NN):
    return lax.dot_general(
        a, b, (dims, ((), ())), precision=lax.Precision.HIGHEST, preferred_element_type=f32
    )


def split3(a):
    high = a.astype(jnp.bfloat16)
    rest = a - high.astype(f32)
    middle = rest.astype(jnp.bfloat16)
    low = (rest - middle.astype(f32)).astype(jnp.bfloat16)
    return high, middle, low


def lanes(n):
    return -(-n // LANES) * LANES


def in_hbm(a):
    return pltpu.with_memory_space_constraint(a, pltpu.HBM)


def in_vmem(a):
    return pltpu.with_memory_space_constraint(a, pltpu.VMEM)


def call(kernel, name, in_specs, out_specs, out_shape, operands, mib=8, flops=0, nbytes=0, scratch=(), aliases={}):
    return pl.pallas_call(
        kernel,
        in_specs=in_specs,
        out_specs=out_specs,
        out_shape=out_shape,
        scratch_shapes=scratch,
        input_output_aliases=aliases,
        compiler_params=pltpu.CompilerParams(vmem_limit_bytes=mib << 20),
        cost_estimate=pl.CostEstimate(flops=flops, bytes_accessed=nbytes, transcendentals=0),
        name=name,
    )(*operands)


def small_call(kernel, name, shapes, *operands):
    return call(
        kernel,
        name,
        [VMEM] * len(operands),
        [VMEM] * len(shapes),
        [jax.ShapeDtypeStruct(s, f32) for s in shapes],
        operands,
        flops=12_000_000,
        nbytes=4 * sum(o.size for o in operands),
    )


def combine_kernel(place, g_hbm, e_hbm, *refs, own, blocks, streams):
    outs, (g, e, sem) = refs[:streams], refs[streams:]
    width = g.shape[2]
    m = place[0] if own else 1 - place[0]

    def copies(i):
        s, p = divmod(i, blocks)
        start = pl.multiple_of(((place[1] ^ p) * streams + s) * width, width)
        where = pl.ds(start, width)
        return (
            pltpu.make_async_copy(g_hbm.at[0, m, :, where], g.at[i], sem.at[i, 0]),
            pltpu.make_async_copy(e_hbm.at[0, m, :, where], e.at[i], sem.at[i, 1]),
        )

    for i in range(blocks * streams):
        for copy in copies(i):
            copy.start()
    for i in range(blocks * streams):
        for copy in copies(i):
            copy.wait()
        s, p = divmod(i, blocks)
        outs[s][p] = g[i].astype(f32) + e[i]


def combine(place, grads, errors, own, blocks, streams):
    rows, cols = grads.shape[2:]
    chunks = blocks * streams
    width = cols // chunks
    return call(
        functools.partial(combine_kernel, own=own, blocks=blocks, streams=streams),
        "own" if own else "outgoing",
        [SMEM, ANY, ANY],
        [VMEM] * streams,
        [pltpu.VMEM((blocks, rows, width), f32)] * streams,
        (place, grads, errors),
        mib=10,
        flops=rows * cols,
        nbytes=rows * cols * 10,
        scratch=[
            pltpu.VMEM((chunks, rows, width), grads.dtype),
            pltpu.VMEM((chunks, rows, width), f32),
            pltpu.SemaphoreType.DMA((chunks, 2)),
        ],
    )


def factor_kernel(place, w_hbm, vec_hbm, *refs, streams):
    combined = (refs[:streams], refs[streams : 2 * streams])
    outs, (w, vec, sem) = refs[2 * streams : 2 * streams + 2], refs[2 * streams + 2 :]
    blocks, rows, width = combined[0][0].shape
    rank = w.shape[1]
    loads = (
        pltpu.make_async_copy(w_hbm, w, sem.at[0]),
        pltpu.make_async_copy(vec_hbm.at[0], vec, sem.at[1]),
    )
    for load in loads:
        load.start()
    for load in loads:
        load.wait()
    for k in range(2):
        m = place[0] if k == 0 else 1 - place[0]
        terms = jnp.zeros((rows, 3 * rank), f32)
        for s in range(streams):
            for p in range(blocks):
                start = pl.multiple_of(((place[1] ^ p) * streams + s) * width, width)
                w_high, w_middle, w_low = split3(w[m, :, pl.ds(start, width)])
                zero = jnp.zeros_like(w_low)
                high, middle, low = split3(combined[k][s][p])
                for part, factors in (
                    (high, (w_high, w_middle, w_low)),
                    (middle, (w_high, w_middle, zero)),
                    (low, (w_high, zero, zero)),
                ):
                    terms += lax.dot_general(
                        part, jnp.concatenate(factors, axis=0), (NT, ((), ())), preferred_element_type=f32
                    )
        out = outs[k]
        out[...] = jnp.zeros(out.shape, f32)
        out[:, :rows] = (terms[:, :rank] + terms[:, rank : 2 * rank] + terms[:, 2 * rank :]).T
        mine = jnp.where(m == 0, vec[0:1, :], vec[1:2, :])
        for i in range(vec.shape[1] // LANES):
            out[i : i + 1, out.shape[1] - LANES :] = mine[:, i * LANES : (i + 1) * LANES]


def first_factors(place, own_c, other_c, warm_start, vec_grads):
    streams = len(own_c)
    rows = own_c[0].shape[1]
    rank = warm_start.shape[1]
    shape = jax.ShapeDtypeStruct((rank, lanes(rows) + LANES), f32)
    return call(
        functools.partial(factor_kernel, streams=streams),
        "factor",
        [SMEM, ANY, ANY] + [VMEM] * (2 * streams),
        [VMEM] * 2,
        [shape] * 2,
        (place, warm_start, vec_grads, *own_c, *other_c),
        mib=12,
        flops=36 * rank * rows * warm_start.shape[2],
        nbytes=8 * rows * warm_start.shape[2],
        scratch=[
            pltpu.VMEM(warm_start.shape, f32),
            pltpu.VMEM(vec_grads.shape[1:], f32),
            pltpu.SemaphoreType.DMA((2,)),
        ],
    )


def kept_blocks(order, blocks, stage):
    return [p for p in range(blocks) if not any(p >> bit & 1 for bit in order[:stage])]


def fold_kernel(*refs, picks):
    ins, out = refs[:-1], refs[-1]
    for i, pick in enumerate(picks):
        out[i] = sum(ref[at] for ref, at in zip(ins, pick))


def fold(terms, order, blocks, stage):
    goes = [p for p in kept_blocks(order, blocks, stage) if p >> order[stage] & 1]
    picks = [
        (p, p, *(kept_blocks(order, blocks, t + 1).index(p) for t in range(len(terms) - 2))) for p in goes
    ]
    shape = (len(goes),) + terms[0].shape[1:]
    return call(
        functools.partial(fold_kernel, picks=picks),
        f"fold{stage}",
        [VMEM] * len(terms),
        VMEM,
        pltpu.VMEM(shape, f32),
        terms,
        nbytes=4 * len(terms) * shape[0] * shape[1] * shape[2],
    )


def project_kernel(*refs, streams, per, count):
    x_ref, parts, (s_ref, v_ref) = refs[0], refs[1 : 1 + per * streams], refs[1 + per * streams :]
    rows = s_ref.shape[0]
    width = s_ref.shape[1] // streams
    factor = x_ref[:, :rows] / count
    for s in range(streams):
        block = sum(part[0] for part in parts[s * per : (s + 1) * per])
        where = slice(s * width, (s + 1) * width)
        s_ref[:, where] = block
        v_ref[:, where] = dot(factor, block) / count


def lift_kernel(v_ref, s_ref, u_ref, *, count):
    u_ref[...] = dot(v_ref[...], s_ref[...], NT) / count


def lower_kernel(u_ref, s_ref, v_ref, *, count):
    v_ref[...] = dot(u_ref[...], s_ref[...]) / count


def identity(rank):
    return (
        lax.broadcasted_iota(jnp.int32, (rank, rank), 0)
        == lax.broadcasted_iota(jnp.int32, (rank, rank), 1)
    ).astype(f32)


def sweeps(left, right, first, last):
    eye = identity(left.shape[0])
    for sweep in range(first, last):
        middle = 1.5 * eye - 0.5 * (left if sweep == 0 else dot(right, left))
        right = middle if sweep == 0 else dot(middle, right)
        if sweep + 1 < ROOT_ITERS:
            left = dot(left, middle)
    return left, right


def root_begin(gram, state):
    spread = jnp.sqrt(jnp.sum(gram * gram, keepdims=True))
    left, right = sweeps(gram / spread, None, 0, ROOT_ITERS // 2)
    state[0], state[1] = left, right
    state[2] = jnp.broadcast_to(spread, gram.shape)


def root_end(state):
    _, right = sweeps(state[0], state[1], ROOT_ITERS // 2, ROOT_ITERS)
    return right / jnp.sqrt(state[2])


def first_begin_kernel(x_ref, state, *, rows, count):
    factor = x_ref[:, :rows] / count
    root_begin(dot(factor, factor, NT), state)


def first_end_kernel(state, a_ref):
    a_ref[...] = root_end(state)


def second_begin_kernel(a_ref, u_ref, state):
    a, u = a_ref[...], u_ref[...]
    root_begin(dot(a, dot(dot(u, u, NT), a), TN), state)


def second_end_kernel(state, a_ref, u_ref, f_ref):
    u = u_ref[...]
    rank, rows = u.shape
    both = dot(a_ref[...], root_end(state))
    f_ref[...] = jnp.zeros(f_ref.shape, f32)
    f_ref[:, :rows] = dot(both, u, TN)
    f_ref[:, rows : rows + rank] = both


def gains_kernel(place, chosen, own_ref, other_ref, mv_ref, wv_ref, mo_ref, wo_ref, vec, *, count, first):
    for i in range(mv_ref.shape[1] // LANES):
        at = slice(i * LANES, (i + 1) * LANES)
        for k, ref in enumerate((own_ref, other_ref)):
            vec[k : k + 1, at] = ref[i : i + 1, ref.shape[1] - LANES :] / count
    for slot in range(mv_ref.shape[0]):
        item = chosen[slot]
        row = jnp.where(item - first == place[0], vec[0:1, :], vec[1:2, :])
        old, weight = mv_ref[slot : slot + 1, :], wv_ref[slot : slot + 1, :]
        new = 0.9 * old + row
        mo_ref[slot : slot + 1, :] = jnp.where(item >= first, new, old)
        wo_ref[slot : slot + 1, :] = jnp.where(item >= first, weight - 0.5 * new, weight)


def gains(place, chosen, own, other, vec_momentum, vec_weights, count, first):
    return call(
        functools.partial(gains_kernel, count=count, first=first),
        "gains",
        [SMEM, SMEM] + [VMEM] * 4,
        [VMEM] * 2,
        [jax.ShapeDtypeStruct(vec_momentum.shape, f32)] * 2,
        (place, chosen, own, other, vec_momentum, vec_weights),
        flops=10 * vec_momentum.size,
        nbytes=16 * vec_momentum.size,
        scratch=[pltpu.VMEM((2, vec_momentum.shape[1]), f32)],
    )


def finish_kernel(place, chosen, v0_ref, v1_ref, f0_ref, f1_ref, *refs, positions, streams, head, later):
    combined = (refs[:streams], refs[streams : 2 * streams])
    mm_hbm, mw_hbm = refs[2 * streams : 2 * streams + 2]
    refs = refs[2 * streams + 2 + later :]
    n_hbm, mo_hbm, wo_hbm, errors, approx, moment, weight, sem, bank_sem = refs
    rank, width = v0_ref.shape[1:]
    rows = errors.shape[2]
    narrow = width // streams

    def columns(p):
        return pl.ds(pl.multiple_of((place[1] ^ p) * width, width), width)

    loads = []
    for k, p in enumerate(positions):
        loads.append(
            (
                pltpu.make_async_copy(mm_hbm.at[:, :, columns(p)], moment.at[k], bank_sem.at[k, 0]),
                pltpu.make_async_copy(mw_hbm.at[:, :, columns(p)], weight.at[k], bank_sem.at[k, 1]),
            )
        )
        for load in loads[-1]:
            load.start()
    left, both = [], []
    for f_ref in (f0_ref, f1_ref):
        high, middle, low = split3(f_ref[:, :rows].T)
        left.append(jnp.concatenate([high, high, middle, high, low, middle], axis=1))
        both.append(f_ref[:, rows : rows + rank])
    stores = []
    for k, p in enumerate(positions):
        for i, v_ref in enumerate((v0_ref, v1_ref)):
            m = place[0] if i == 0 else 1 - place[0]
            high, middle, low = split3(dot(both[i], v_ref[k], TN))
            right = jnp.concatenate([high, middle, high, low, high, middle], axis=0)
            product = jnp.dot(left[i], right, preferred_element_type=f32)
            approx[k, pl.ds(pl.multiple_of(m * rows, rows), rows), :] = product
            for s in range(streams):
                at = slice(s * narrow, (s + 1) * narrow)
                errors[k, i, :, at] = combined[i][s][p] - product[:, at]
            stores.append(
                pltpu.make_async_copy(errors.at[k, i], n_hbm.at[0, m, :, columns(p)], sem.at[k, i])
            )
            stores[-1].start()
        for load in loads[k]:
            load.wait()
        for slot in range(moment.shape[1]):
            item = chosen[slot]

            @pl.when((item >= 0) & (item < approx.shape[1] // head))
            def _():
                block = approx[k, pl.ds(pl.multiple_of(item * head, head), head), :]
                new = 0.9 * moment[k, slot] + block
                moment[k, slot] = new
                weight[k, slot] = weight[k, slot] - 0.5 * new

        for i, (ref, hbm) in enumerate(((moment, mo_hbm), (weight, wo_hbm))):
            stores.append(
                pltpu.make_async_copy(ref.at[k], hbm.at[:, :, columns(p)], bank_sem.at[len(positions) + k, i])
            )
            stores[-1].start()
    for store in stores:
        store.wait()


def finish(positions, outs, place, chosen, own_v, other_v, own_f, other_f, own_c, other_c, shapes, mat_momentum, mat_weights):
    n, rank, width = own_v.shape
    streams = len(own_c)
    matrices, rows, cols = shapes[0][1:]
    slots, head = mat_momentum.shape[:2]
    later = len(outs)
    inputs = 6 + 2 * streams + 2
    return call(
        functools.partial(finish_kernel, positions=positions, streams=streams, head=head, later=later),
        f"finish{positions[0]}",
        [SMEM, SMEM] + [VMEM] * (4 + 2 * streams) + [ANY] * (2 + later),
        [ANY] * 3,
        [pltpu.HBM(s, f32) for s in shapes],
        (place, chosen, own_v, other_v, own_f, other_f, *own_c, *other_c, mat_momentum, mat_weights, *outs),
        mib=4 + 8 * n,
        flops=2 * n * matrices * rows * width * 6 * rank,
        nbytes=4 * n * width * (matrices * rows + 4 * slots * head),
        scratch=[
            pltpu.VMEM((n, matrices, rows, width), f32),
            pltpu.VMEM((n, matrices * rows, width), f32),
            pltpu.VMEM((n, slots, head, width), f32),
            pltpu.VMEM((n, slots, head, width), f32),
            pltpu.SemaphoreType.DMA((n, matrices)),
            pltpu.SemaphoreType.DMA((2 * n, 2)),
        ],
        aliases={inputs + i: i for i in range(later)},
    )


def exchange(a, axis, mask):
    return lax.ppermute(a, axis, [(i, i ^ mask) for i in range(lax.axis_size(axis))])


def hop(a, axis, mask, work=None, *operands):
    if work is None:
        return a + exchange(a, axis, mask)
    a, *operands = lax.optimization_barrier((a, *operands))
    arrived = exchange(a, axis, mask)
    done = work(*operands)
    arrived, *done = lax.optimization_barrier((arrived, *done))
    return a + arrived, *done


def local(grads, errors, warm_start, vec_grads, owners, mat_momentum, mat_weights, vec_momentum, vec_weights):
    reps, groups = lax.axis_size("rep"), lax.axis_size("grp")
    count = float(reps * groups)
    blocks = reps // 2
    bits = blocks.bit_length() - 1
    z_masks = [1 << i for i in range(groups.bit_length() - 1)]
    matrices, rows, cols = grads.shape[1:]
    rank = warm_start.shape[1]
    width = cols // blocks
    streams = 2 if width % 256 == 0 else 1
    rep = lax.axis_index("rep")
    core, spot = rep % 2, rep // 2
    device = rep * groups + lax.axis_index("grp")
    place = jnp.stack([core, spot]).astype(jnp.int32)

    items = owners.shape[0]
    slots, head = mat_momentum.shape[:2]
    earlier = jnp.arange(items)[None, :] < jnp.arange(items)[:, None]
    same = owners[None, :] == owners[:, None]
    slot = jnp.sum((earlier & same).astype(jnp.int32), axis=1)
    match = (owners[None, :] == device) & (slot[None, :] == jnp.arange(slots)[:, None])
    head_items = matrices * (rows // head)
    chosen = jnp.max(jnp.where(match, jnp.arange(items)[None, :], -1), axis=1).astype(jnp.int32)

    grads, errors, warm_start, vec_grads = map(in_hbm, (grads, errors, warm_start, vec_grads))
    mat_momentum, mat_weights = map(in_hbm, (mat_momentum, mat_weights))

    other_c = combine(place, grads, errors, False, blocks, streams)
    arrived_c = [in_vmem(exchange(a, "rep", 1)) for a in other_c]
    own_c = combine(place, grads, errors, True, blocks, streams)

    orders = [list(range(bits)), list(range(bits))[::-1]][:streams]
    parts = [[own_c[s], arrived_c[s]] for s in range(streams)]
    goes = [fold(parts[s], orders[s], blocks, 0) for s in range(streams)]
    firsts = [exchange(goes[s], "rep", 2 << orders[s][0]) for s in range(streams)]

    tied = lax.optimization_barrier((place, *goes))
    own_p, other_p = first_factors(tied[0], own_c, other_c, warm_start, vec_grads)
    packed = own_p + exchange(other_p, "rep", 1)
    for mask in z_masks:
        packed = hop(packed, "grp", mask)
    packed = hop(packed, "rep", 2)
    *firsts, packed = lax.optimization_barrier((*firsts, packed))
    for bit in range(1, bits):
        packed = hop(packed, "rep", 2 << bit)
    for stage in range(bits):
        for s in range(streams):
            if stage == 0:
                arrived = firsts[s]
            else:
                arrived = exchange(fold(parts[s], orders[s], blocks, stage), "rep", 2 << orders[s][stage])
            parts[s].append(in_vmem(arrived))

    kept_sum, v = small_call(
        functools.partial(project_kernel, streams=streams, per=len(parts[0]), count=count),
        "project", [(rows, width), (rank, width)], packed, *sum(parts, []),
    )
    square = (rank, rank)
    state = (3, rank, rank)
    v, first_state = hop(
        v, "grp", z_masks[0],
        lambda x: small_call(
            functools.partial(first_begin_kernel, rows=rows, count=count), "root1a", [state], x
        ), packed,
    )
    v, first_root = hop(
        v, "grp", z_masks[1], lambda x: small_call(first_end_kernel, "root1b", [square], x), first_state
    )
    for mask in z_masks[2:]:
        v = hop(v, "grp", mask)
    (u,) = small_call(functools.partial(lift_kernel, count=count), "lift", [(rank, rows)], v, kept_sum)
    for mask in z_masks[:-1]:
        u = hop(u, "grp", mask)
    u, vec_momentum_out, vec_weights_out = hop(
        u, "grp", z_masks[-1],
        lambda x, y: gains(place, chosen, x, y, vec_momentum, vec_weights, count, head_items),
        packed, exchange(packed, "rep", 1),
    )
    for bit in range(bits):
        u = hop(u, "rep", 2 << bit)
    (v,) = small_call(functools.partial(lower_kernel, count=count), "lower", [(rank, width)], u, kept_sum)
    v, second_state = hop(
        v, "grp", z_masks[0], lambda *x: small_call(second_begin_kernel, "root2a", [state], *x), first_root, u
    )
    v, own_f = hop(
        v, "grp", z_masks[1],
        lambda *x: small_call(second_end_kernel, "root2b", [(rank, lanes(rows + rank))], *x),
        second_state, first_root, u,
    )
    for mask in z_masks[2:]:
        v = hop(v, "grp", mask)
    other_f = exchange(own_f, "rep", 1)

    shapes = [errors.shape, mat_momentum.shape, mat_weights.shape]
    outs = ()
    v = v[None]
    fresh, positions = v, [0]
    for bit in range(bits + 1):
        other_v = exchange(fresh, "rep", 1)
        if bit < bits:
            arrived = exchange(v, "rep", 2 << bit)
        outs = finish(
            positions, outs, place, chosen, fresh, other_v, own_f, other_f, own_c, other_c, shapes,
            mat_momentum, mat_weights,
        )
        if bit < bits:
            arrived, *outs = lax.optimization_barrier((arrived, *outs))
            v = jnp.concatenate([v, arrived], axis=0)
            fresh, positions = arrived, list(range(1 << bit, 2 << bit))
    new_errors, mat_momentum_out, mat_weights_out = outs
    return (new_errors, mat_momentum_out, mat_weights_out, vec_momentum_out, vec_weights_out)


def solution(mesh):
    both = ("rep", "grp")
    return jax.shard_map(
        local,
        mesh=mesh,
        in_specs=(
            P(both, None, None, None),
            P(both, None, None, None),
            P(),
            P(both, None, None),
            P(),
            P(both, None, None),
            P(both, None, None),
            P(both, None),
            P(both, None),
        ),
        out_specs=(
            P(both, None, None, None),
            P(both, None, None),
            P(both, None, None),
            P(both, None),
            P(both, None),
        ),
        check_vma=False,
    )
```

```python
import functools

import jax
import jax.numpy as jnp
from jax import lax
from jax.experimental import pallas as pl
from jax.experimental.pallas import tpu as pltpu
from jax.sharding import PartitionSpec as P

ROOT_ITERS = 12
LANES = 128
f32 = jnp.float32
NN = ((1,), (0,))
NT = ((1,), (1,))
TN = ((0,), (0,))
ANY = pl.BlockSpec(memory_space=pl.ANY)
VMEM = pl.BlockSpec(memory_space=pltpu.VMEM)
SMEM = pl.BlockSpec(memory_space=pltpu.SMEM)


def dot(a, b, dims=NN):
    return lax.dot_general(
        a, b, (dims, ((), ())), precision=lax.Precision.HIGHEST, preferred_element_type=f32
    )


def split3(a):
    high = a.astype(jnp.bfloat16)
    rest = a - high.astype(f32)
    middle = rest.astype(jnp.bfloat16)
    low = (rest - middle.astype(f32)).astype(jnp.bfloat16)
    return high, middle, low


def lanes(n):
    return -(-n // LANES) * LANES


def in_hbm(a):
    return pltpu.with_memory_space_constraint(a, pltpu.HBM)


def in_vmem(a):
    return pltpu.with_memory_space_constraint(a, pltpu.VMEM)


def call(kernel, name, in_specs, out_specs, out_shape, operands, mib=8, flops=0, nbytes=0, scratch=(), aliases={}):
    return pl.pallas_call(
        kernel,
        in_specs=in_specs,
        out_specs=out_specs,
        out_shape=out_shape,
        scratch_shapes=scratch,
        input_output_aliases=aliases,
        compiler_params=pltpu.CompilerParams(vmem_limit_bytes=mib << 20),
        cost_estimate=pl.CostEstimate(flops=flops, bytes_accessed=nbytes, transcendentals=0),
        name=name,
    )(*operands)


def small_call(kernel, name, shapes, *operands):
    return call(
        kernel,
        name,
        [VMEM] * len(operands),
        [VMEM] * len(shapes),
        [jax.ShapeDtypeStruct(s, f32) for s in shapes],
        operands,
        flops=12_000_000,
        nbytes=4 * sum(o.size for o in operands),
    )


def block_columns(place, own, p, blocks, width):
    bits = blocks.bit_length() - 1
    mirrored = sum((p >> i & 1) << (bits - 1 - i) for i in range(bits))
    core = place[0] if own else 1 - place[0]
    block = place[1] ^ jnp.where(core == 0, p, mirrored)
    return pl.ds(pl.multiple_of(block * width, width), width)


def write_factor(out, place, own, w_ref, vec_ref, halves):
    half, rows, width = halves[0].shape
    rank = w_ref.shape[1]
    m = place[0] if own else 1 - place[0]
    terms = jnp.zeros((rows, 3 * rank), f32)
    for p in range(2 * half):
        w_high, w_middle, w_low = split3(w_ref[m, :, block_columns(place, own, p, 2 * half, width)])
        high, middle, _ = split3(halves[p % 2][p // 2])
        for part, pieces in (
            (high, (w_high, w_middle, w_low)),
            (middle, (w_high, w_middle, jnp.zeros_like(w_low))),
        ):
            terms += lax.dot_general(
                part, jnp.concatenate(pieces, axis=0), (NT, ((), ())), preferred_element_type=f32
            )
    out[...] = jnp.zeros(out.shape, f32)
    out[:, :rows] = (terms[:, :rank] + terms[:, rank : 2 * rank] + terms[:, 2 * rank :]).T
    mine = jnp.where(m == 0, vec_ref[0, 0:1, :], vec_ref[0, 1:2, :])
    for i in range(vec_ref.shape[2] // LANES):
        out[i : i + 1, out.shape[1] - LANES :] = mine[:, i * LANES : (i + 1) * LANES]


def factor_shape(rows, warm_start):
    return jax.ShapeDtypeStruct((warm_start.shape[1], lanes(rows) + LANES), f32)


def factor_kernel(place, w_ref, vec_ref, even, odd, out):
    write_factor(out, place, True, w_ref, vec_ref, (even, odd))


def own_factor(place, halves, warm_start, vec_grads):
    rows = halves[0].shape[1]
    return call(
        factor_kernel,
        "factor",
        [SMEM] + [VMEM] * 4,
        VMEM,
        factor_shape(rows, warm_start),
        (place, warm_start, vec_grads, *halves),
        flops=12 * rows * warm_start.size,
        nbytes=8 * rows * warm_start.shape[2],
    )


def combine_kernel(place, g_hbm, e_hbm, *refs, own):
    if own:
        w_ref, vec_ref, other_even, other_odd, *refs = refs
        even, odd, factor, g, e, sem = refs
    else:
        even, odd, g, e, sem = refs
    blocks, rows, width = g.shape
    m = place[0] if own else 1 - place[0]
    order = [*range(1, blocks, 2), *range(0, blocks, 2)]
    loads = {}
    for p in order:
        where = block_columns(place, own, p, blocks, width)
        loads[p] = (
            pltpu.make_async_copy(g_hbm.at[0, m, :, where], g.at[p], sem.at[p, 0]),
            pltpu.make_async_copy(e_hbm.at[0, m, :, where], e.at[p], sem.at[p, 1]),
        )
        for load in loads[p]:
            load.start()
    if own:
        write_factor(factor, place, False, w_ref, vec_ref, (other_even, other_odd))
    for p in order:
        for load in loads[p]:
            load.wait()
        (even, odd)[p % 2][p // 2] = g[p].astype(f32) + e[p]


def combine(place, grads, errors, blocks, factor_of=()):
    rows, cols = grads.shape[2:]
    own = bool(factor_of)
    shape = (blocks, rows, cols // blocks)
    half = pltpu.VMEM((blocks // 2,) + shape[1:], f32)
    return call(
        functools.partial(combine_kernel, own=own),
        "own" if own else "other",
        [SMEM, ANY, ANY] + [VMEM] * len(factor_of),
        [VMEM] * (3 if own else 2),
        [half, half] + ([factor_shape(rows, factor_of[0])] if own else []),
        (place, grads, errors, *factor_of),
        mib=12,
        flops=rows * cols * (200 if own else 1),
        nbytes=rows * cols * 10,
        scratch=[pltpu.VMEM(shape, grads.dtype), pltpu.VMEM(shape, f32), pltpu.SemaphoreType.DMA((blocks, 2))],
    )


def fold_kernel(*refs, picks):
    for i, pick in enumerate(picks):
        refs[-1][i] = sum(refs[k][at] for k, at in pick)


def fold(terms, after=()):
    arrays, picks = [], []
    for pairs in terms:
        pick = []
        for a, at in pairs:
            if not any(a is b for b in arrays):
                arrays.append(a)
            pick.append((next(k for k, b in enumerate(arrays) if a is b), at))
        picks.append(pick)
    shape = (len(terms),) + arrays[0].shape[1:]
    return call(
        functools.partial(fold_kernel, picks=picks),
        "fold",
        [VMEM] * len(arrays) + [ANY] * len(after),
        VMEM,
        pltpu.VMEM(shape, f32),
        (*arrays, *after),
        nbytes=4 * len(picks[0]) * shape[0] * shape[1] * shape[2],
    )


def project_kernel(x_ref, *refs, places, count):
    parts, (s_ref, v_ref) = refs[:-2], refs[-2:]
    block = sum(part[at] for part, at in zip(parts, places))
    s_ref[...] = block
    v_ref[...] = dot(x_ref[:, : block.shape[0]] / count, block) / count


def lift_kernel(v_ref, s_ref, u_ref, *, count):
    u_ref[...] = dot(v_ref[...], s_ref[...], NT) / count


def lower_kernel(u_ref, s_ref, v_ref, *, count):
    v_ref[...] = dot(u_ref[...], s_ref[...]) / count


def identity(rank):
    return (
        lax.broadcasted_iota(jnp.int32, (rank, rank), 0)
        == lax.broadcasted_iota(jnp.int32, (rank, rank), 1)
    ).astype(f32)


def sweeps(left, right, first, last):
    eye = identity(left.shape[0])
    for sweep in range(first, last):
        middle = 1.5 * eye - 0.5 * (left if sweep == 0 else dot(right, left))
        right = middle if sweep == 0 else dot(middle, right)
        if sweep + 1 < ROOT_ITERS:
            left = dot(left, middle)
    return left, right


def root_begin(gram, state):
    spread = jnp.sqrt(jnp.sum(gram * gram, keepdims=True))
    left, right = sweeps(gram / spread, None, 0, ROOT_ITERS // 2)
    state[0], state[1] = left, right
    state[2] = jnp.broadcast_to(spread, gram.shape)


def root_end(state):
    _, right = sweeps(state[0], state[1], ROOT_ITERS // 2, ROOT_ITERS)
    return right / jnp.sqrt(state[2])


def first_begin_kernel(x_ref, state, *, rows, count):
    factor = x_ref[:, :rows] / count
    root_begin(dot(factor, factor, NT), state)


def first_end_kernel(state, a_ref):
    a_ref[...] = root_end(state)


def second_begin_kernel(a_ref, u_ref, state):
    a, u = a_ref[...], u_ref[...]
    root_begin(dot(a, dot(dot(u, u, NT), a), TN), state)


def second_end_kernel(state, a_ref, u_ref, f_ref):
    u = u_ref[...]
    rank, rows = u.shape
    both = dot(a_ref[...], root_end(state))
    f_ref[...] = jnp.zeros(f_ref.shape, f32)
    f_ref[:, :rows] = dot(both, u, TN)
    f_ref[:, rows : rows + rank] = both


def gains_kernel(place, chosen, own_ref, other_ref, mv_ref, wv_ref, mo_ref, wo_ref, vec, *, count, first):
    for i in range(mv_ref.shape[1] // LANES):
        at = slice(i * LANES, (i + 1) * LANES)
        for k, ref in enumerate((own_ref, other_ref)):
            vec[k : k + 1, at] = ref[i : i + 1, ref.shape[1] - LANES :] / count
    for slot in range(mv_ref.shape[0]):
        item = chosen[slot]
        row = jnp.where(item - first == place[0], vec[0:1, :], vec[1:2, :])
        old, weight = mv_ref[slot : slot + 1, :], wv_ref[slot : slot + 1, :]
        new = 0.9 * old + row
        mo_ref[slot : slot + 1, :] = jnp.where(item >= first, new, old)
        wo_ref[slot : slot + 1, :] = jnp.where(item >= first, weight - 0.5 * new, weight)


def gains(place, chosen, own, other, vec_momentum, vec_weights, count, first):
    return call(
        functools.partial(gains_kernel, count=count, first=first),
        "gains",
        [SMEM, SMEM] + [VMEM] * 4,
        [VMEM] * 2,
        [jax.ShapeDtypeStruct(vec_momentum.shape, f32)] * 2,
        (place, chosen, own, other, vec_momentum, vec_weights),
        flops=10 * vec_momentum.size,
        nbytes=16 * vec_momentum.size,
        scratch=[pltpu.VMEM((2, vec_momentum.shape[1]), f32)],
    )


def banks_kernel(mm_hbm, mw_hbm, mm, mw, sem):
    loads = (pltpu.make_async_copy(mm_hbm, mm, sem.at[0]), pltpu.make_async_copy(mw_hbm, mw, sem.at[1]))
    for load in loads:
        load.start()
    for load in loads:
        load.wait()


def banks(mat_momentum, mat_weights):
    return call(
        banks_kernel,
        "banks",
        [ANY, ANY],
        [VMEM] * 2,
        [pltpu.VMEM(mat_momentum.shape, f32)] * 2,
        (mat_momentum, mat_weights),
        nbytes=8 * mat_momentum.size,
        scratch=[pltpu.SemaphoreType.DMA((2,))],
    )


def finish_kernel(
    place, chosen, v0_ref, v1_ref, f0_ref, f1_ref, c0_even, c0_odd, c1_even, c1_odd, mm, mw, *refs, positions, head, later
):
    if later:
        left, refs = refs[0], refs[1 + 3 :]
        n_hbm, mo_hbm, wo_hbm, errors, approx, moment, weight, sem, bank_sem = refs
    else:
        n_hbm, mo_hbm, wo_hbm, left, errors, approx, moment, weight, sem, bank_sem = refs
    rank, width = v0_ref.shape[1:]
    blocks, rows = 2 * c0_even.shape[0], c0_even.shape[1]
    per = rows // head
    stores, bank_stores = [], []
    for k, p in enumerate(positions):
        for i, (v_ref, f_ref, *c_refs) in enumerate(
            ((v0_ref, f0_ref, c0_even, c0_odd), (v1_ref, f1_ref, c1_even, c1_odd))
        ):
            if k == 0 and not later:
                high, middle, low = split3(f_ref[:, :rows].T)
                left[i] = jnp.concatenate([high, high, middle, high, low, middle], axis=1)
            m = place[0] if i == 0 else 1 - place[0]
            columns = block_columns(place, i == 0, p, blocks, width)
            high, middle, low = split3(dot(f_ref[:, rows : rows + rank], v_ref[k], TN))
            right = jnp.concatenate([high, middle, high, low, high, middle], axis=0)
            product = jnp.dot(left[i], right, preferred_element_type=f32)
            approx[k, i] = product
            errors[k, i] = c_refs[p % 2][p // 2] - product
            stores.append(pltpu.make_async_copy(errors.at[k, i], n_hbm.at[0, m, :, columns], sem.at[k, i]))
            stores[-1].start()
            for slot in range(mm.shape[0]):
                item = chosen[slot]
                taken = (item >= m * per) & (item < (m + 1) * per)
                idle = (item < 0) | (item >= 2 * per)
                copies = (
                    pltpu.make_async_copy(
                        moment.at[k, i, slot], mo_hbm.at[slot, :, columns], bank_sem.at[k, i, slot, 0]
                    ),
                    pltpu.make_async_copy(
                        weight.at[k, i, slot], wo_hbm.at[slot, :, columns], bank_sem.at[k, i, slot, 1]
                    ),
                )

                @pl.when(taken)
                def _():
                    at = pl.ds(pl.multiple_of((item - m * per) * head, head), head)
                    new = 0.9 * mm[slot, :, columns] + approx[k, i, at, :]
                    moment[k, i, slot] = new
                    weight[k, i, slot] = mw[slot, :, columns] - 0.5 * new

                writes = taken
                if i == 0:
                    writes = taken | idle

                    @pl.when(idle)
                    def _():
                        moment[k, i, slot] = mm[slot, :, columns]
                        weight[k, i, slot] = mw[slot, :, columns]

                @pl.when(writes)
                def _():
                    for copy in copies:
                        copy.start()

                bank_stores.append((writes, copies))
    for store in stores:
        store.wait()
    for writes, copies in bank_stores:

        @pl.when(writes)
        def _():
            for copy in copies:
                copy.wait()


def finish(positions, left, outs, place, chosen, own_v, other_v, own_f, other_f, own_c, other_c, shapes, mm, mw):
    n, rank, width = own_v.shape
    matrices, rows, cols = shapes[0][1:]
    slots, head = mm.shape[:2]
    later = len(outs) > 0
    inputs = 12 + len(left)
    first = [] if later else [pltpu.VMEM((2, rows, 6 * rank), jnp.bfloat16)]
    return call(
        functools.partial(finish_kernel, positions=positions, head=head, later=later),
        f"finish{positions[0]}",
        [SMEM, SMEM] + [VMEM] * (10 + len(left)) + [ANY] * len(outs),
        [ANY] * 3 + [VMEM] * len(first),
        [pltpu.HBM(s, f32) for s in shapes] + first,
        (place, chosen, own_v, other_v, own_f, other_f, *own_c, *other_c, mm, mw, *left, *outs),
        mib=4 + 8 * n,
        flops=2 * n * matrices * rows * width * 6 * rank,
        nbytes=4 * n * width * (matrices * rows + 4 * slots * head),
        scratch=[
            pltpu.VMEM((n, 2, rows, width), f32),
            pltpu.VMEM((n, 2, rows, width), f32),
            pltpu.VMEM((n, 2, slots, head, width), f32),
            pltpu.VMEM((n, 2, slots, head, width), f32),
            pltpu.SemaphoreType.DMA((n, 2)),
            pltpu.SemaphoreType.DMA((n, 2, slots, 2)),
        ],
        aliases={inputs + i: i for i in range(len(outs))},
    )


def partner(kind, step):
    planes = (lax.axis_size("rep") // 2).bit_length() - 1
    depths = lax.axis_size("grp").bit_length() - 1

    def of(rep, grp):
        if kind == "core":
            return rep ^ 1, grp
        if kind == "plane":
            return rep ^ (2 << (step if rep % 2 == 0 else planes - 1 - step)), grp
        return rep, grp ^ (1 << (step if rep % 2 == 0 else depths - 1 - step))

    return of


def exchange(a, kind, step=0):
    groups = lax.axis_size("grp")
    of = partner(kind, step)
    pairs = []
    for rep in range(lax.axis_size("rep")):
        for grp in range(groups):
            to_rep, to_grp = of(rep, grp)
            pairs.append((rep * groups + grp, to_rep * groups + to_grp))
    return lax.ppermute(a, ("rep", "grp"), pairs)


def hop(a, kind, step, work=None, *operands):
    if work is None:
        return a + exchange(a, kind, step)
    a, *operands = lax.optimization_barrier((a, *operands))
    arrived = exchange(a, kind, step)
    done = work(*operands)
    arrived, *done = lax.optimization_barrier((arrived, *done))
    return a + arrived, *done


def local(grads, errors, warm_start, vec_grads, owners, mat_momentum, mat_weights, vec_momentum, vec_weights):
    reps, groups = lax.axis_size("rep"), lax.axis_size("grp")
    count = float(reps * groups)
    blocks = reps // 2
    bits = blocks.bit_length() - 1
    depths = groups.bit_length() - 1
    matrices, rows, cols = grads.shape[1:]
    rank = warm_start.shape[1]
    width = cols // blocks
    rep = lax.axis_index("rep")
    core, spot = rep % 2, rep // 2
    device = rep * groups + lax.axis_index("grp")
    place = jnp.stack([core, spot]).astype(jnp.int32)

    items = owners.shape[0]
    slots, head = mat_momentum.shape[:2]
    earlier = jnp.arange(items)[None, :] < jnp.arange(items)[:, None]
    same = owners[None, :] == owners[:, None]
    slot = jnp.sum((earlier & same).astype(jnp.int32), axis=1)
    match = (owners[None, :] == device) & (slot[None, :] == jnp.arange(slots)[:, None])
    head_items = matrices * (rows // head)
    chosen = jnp.max(jnp.where(match, jnp.arange(items)[None, :], -1), axis=1).astype(jnp.int32)

    grads, errors = in_hbm(grads), in_hbm(errors)
    mat_momentum, mat_weights = map(in_hbm, (mat_momentum, mat_weights))

    other_c = combine(place, grads, errors, blocks)
    arrived_odd = in_vmem(exchange(other_c[1], "core"))
    arrived_even = in_vmem(exchange(other_c[0], "core"))
    *own_c, other_p = combine(place, grads, errors, blocks, (warm_start, vec_grads, *other_c))

    terms = [[(own_c[p % 2], p // 2), ((arrived_even, arrived_odd)[p % 2], p // 2)] for p in range(blocks)]

    def send(goes, stage, after=()):
        return goes, stage, exchange(fold([terms[p] for p in goes], after), "plane", stage)

    def land(goes, stage, arrived):
        arrived = in_vmem(arrived)
        for i, p in enumerate(goes):
            terms[p ^ (1 << stage)].append((arrived, i))

    odd = [p for p in range(blocks) if p & 1]
    go = fold([terms[p] for p in odd if p & 2])
    ahead = [p for p in odd if p & 2], 0, exchange(go, "plane", 0)

    rest = [p for p in odd if not p & 2]
    go_rest = fold([terms[p] for p in rest])
    pending = [(rest, 0, exchange(go_rest, "plane", 0))]

    later, *_ = lax.optimization_barrier((place, go, go_rest))
    own_p = own_factor(later, own_c, warm_start, vec_grads)
    packed = own_p + exchange(other_p, "core")
    packed = hop(packed, "plane", bits - 1)
    land(*ahead)
    for stage in range(1, bits):
        goes = [p for p in range(blocks) if p >> stage & 1 and not p & ((1 << stage) - 1)]
        if stage > 1:
            while pending:
                land(*pending.pop(0))
        pending.append(send(goes, stage, (packed,)))
    for step in range(depths):
        packed = hop(packed, "z", step)
    for step in range(bits - 2, -1, -1):
        packed = hop(packed, "plane", step)
    while pending:
        land(*pending.pop(0))

    kept_sum, v = small_call(
        functools.partial(project_kernel, places=[at for _, at in terms[0]], count=count),
        "project", [(rows, width), (rank, width)], packed, *[a for a, _ in terms[0]],
    )
    square = (rank, rank)
    state = (3, rank, rank)
    v, first_state = hop(
        v, "z", 0,
        lambda x: small_call(
            functools.partial(first_begin_kernel, rows=rows, count=count), "root1a", [state], x
        ), packed,
    )
    v, first_root = hop(v, "z", 1, lambda x: small_call(first_end_kernel, "root1b", [square], x), first_state)
    for step in range(2, depths):
        v = hop(v, "z", step)
    (u,) = small_call(functools.partial(lift_kernel, count=count), "lift", [(rank, rows)], v, kept_sum)
    for step in range(depths - 1):
        u = hop(u, "z", step)
    u, vec_momentum_out, vec_weights_out = hop(
        u, "z", depths - 1,
        lambda x, y: gains(place, chosen, x, y, vec_momentum, vec_weights, count, head_items),
        packed, exchange(packed, "core"),
    )
    u, mm, mw = hop(u, "plane", 0, banks, mat_momentum, mat_weights)
    for step in range(1, bits):
        u = hop(u, "plane", step)
    (v,) = small_call(functools.partial(lower_kernel, count=count), "lower", [(rank, width)], u, kept_sum)
    v, second_state = hop(
        v, "z", 0, lambda *x: small_call(second_begin_kernel, "root2a", [state], *x), first_root, u
    )
    early = []

    def second_end(*x):
        early.extend(small_call(second_end_kernel, "root2b", [(rank, lanes(rows + rank))], *x))
        return early

    v, own_f = hop(v, "z", 1, second_end, second_state, first_root, u)
    other_f = exchange(early[0], "core")
    for step in range(2, depths):
        v = hop(v, "z", step)

    shapes = [errors.shape, mat_momentum.shape, mat_weights.shape]
    outs, left = (), ()
    v = v[None]
    fresh, positions = v, [0]
    for step in range(bits + 1):
        other_v = exchange(fresh, "core")
        if step < bits:
            arrived = exchange(v, "plane", step)
        outs = finish(
            positions, left, outs, place, chosen, fresh, other_v, own_f, other_f, own_c, other_c, shapes, mm, mw
        )
        if not left:
            *outs, left = outs
            left = (left,)
        if step < bits:
            arrived, *outs = lax.optimization_barrier((arrived, *outs))
            v = jnp.concatenate([v, arrived], axis=0)
            fresh, positions = arrived, list(range(1 << step, 2 << step))
    new_errors, mat_momentum_out, mat_weights_out = outs
    return (new_errors, mat_momentum_out, mat_weights_out, vec_momentum_out, vec_weights_out)


def solution(mesh):
    both = ("rep", "grp")
    return jax.shard_map(
        local,
        mesh=mesh,
        in_specs=(
            P(both, None, None, None),
            P(both, None, None, None),
            P(),
            P(both, None, None),
            P(),
            P(both, None, None),
            P(both, None, None),
            P(both, None),
            P(both, None),
        ),
        out_specs=(
            P(both, None, None, None),
            P(both, None, None),
            P(both, None, None),
            P(both, None),
            P(both, None),
        ),
        check_vma=False,
    )
```

```python
import functools

import jax
import jax.numpy as jnp
from jax import lax
from jax.experimental import pallas as pl
from jax.experimental.pallas import tpu as pltpu
from jax.sharding import PartitionSpec as P

ROOT_ITERS = 12
LANES = 128
f32 = jnp.float32
NN = ((1,), (0,))
NT = ((1,), (1,))
TN = ((0,), (0,))
ANY = pl.BlockSpec(memory_space=pl.ANY)
VMEM = pl.BlockSpec(memory_space=pltpu.VMEM)
SMEM = pl.BlockSpec(memory_space=pltpu.SMEM)


def dot(a, b, dims=NN):
    return lax.dot_general(
        a, b, (dims, ((), ())), precision=lax.Precision.HIGHEST, preferred_element_type=f32
    )


def split3(a):
    high = a.astype(jnp.bfloat16)
    rest = a - high.astype(f32)
    middle = rest.astype(jnp.bfloat16)
    low = (rest - middle.astype(f32)).astype(jnp.bfloat16)
    return high, middle, low


def lanes(n):
    return -(-n // LANES) * LANES


def in_hbm(a):
    return pltpu.with_memory_space_constraint(a, pltpu.HBM)


def in_vmem(a):
    return pltpu.with_memory_space_constraint(a, pltpu.VMEM)


def call(kernel, name, in_specs, out_specs, out_shape, operands, mib=4, flops=0, nbytes=0, scratch=(), aliases={}):
    return pl.pallas_call(
        kernel,
        in_specs=in_specs,
        out_specs=out_specs,
        out_shape=out_shape,
        scratch_shapes=scratch,
        input_output_aliases=aliases,
        compiler_params=pltpu.CompilerParams(vmem_limit_bytes=mib << 20),
        cost_estimate=pl.CostEstimate(flops=flops, bytes_accessed=nbytes, transcendentals=0),
        name=name,
    )(*operands)


def small_call(kernel, name, shapes, *operands):
    return call(
        kernel,
        name,
        [VMEM] * len(operands),
        [VMEM] * len(shapes),
        [jax.ShapeDtypeStruct(s, f32) for s in shapes],
        operands,
        flops=12_000_000,
        nbytes=4 * sum(o.size for o in operands),
    )


def block_columns(place, own, p, blocks, width):
    bits = blocks.bit_length() - 1
    core = place[0] if own else 1 - place[0]
    block = place[1] ^ jnp.where(core == 0, p, mirror(p, bits))
    return pl.ds(pl.multiple_of(block * width, width), width)


def write_factor(out, place, own, w_ref, vec_ref, halves):
    half, rows, width = halves[0].shape
    rank = w_ref.shape[1]
    m = place[0] if own else 1 - place[0]
    terms = jnp.zeros((rows, 3 * rank), f32)
    for p in range(2 * half):
        w_high, w_middle, w_low = split3(w_ref[m, :, block_columns(place, own, p, 2 * half, width)])
        high, middle, _ = split3(halves[p % 2][p // 2])
        for part, pieces in (
            (high, (w_high, w_middle, w_low)),
            (middle, (w_high, w_middle, jnp.zeros_like(w_low))),
        ):
            terms += lax.dot_general(
                part, jnp.concatenate(pieces, axis=0), (NT, ((), ())), preferred_element_type=f32
            )
    out[...] = jnp.zeros(out.shape, f32)
    out[:, :rows] = (terms[:, :rank] + terms[:, rank : 2 * rank] + terms[:, 2 * rank :]).T
    mine = jnp.where(m == 0, vec_ref[0, 0:1, :], vec_ref[0, 1:2, :])
    for i in range(vec_ref.shape[2] // LANES):
        out[i : i + 1, out.shape[1] - LANES :] = mine[:, i * LANES : (i + 1) * LANES]


def factor_shape(rows, warm_start):
    return jax.ShapeDtypeStruct((warm_start.shape[1], lanes(rows) + LANES), f32)


def factor_kernel(place, w_ref, vec_ref, even, odd, out):
    write_factor(out, place, True, w_ref, vec_ref, (even, odd))


def own_factor(place, halves, warm_start, vec_grads):
    rows = halves[0].shape[1]
    return call(
        factor_kernel,
        "factor",
        [SMEM] + [VMEM] * 4,
        VMEM,
        factor_shape(rows, warm_start),
        (place, warm_start, vec_grads, *halves),
        flops=12 * rows * warm_start.size,
        nbytes=8 * rows * warm_start.shape[2],
    )


def combine_kernel(place, g_hbm, e_hbm, *refs, own):
    if own:
        w_ref, vec_ref, other_even, other_odd, *refs = refs
        even, odd, factor, g, e, sem = refs
    else:
        even, odd, g, e, sem = refs
    blocks, rows, width = g.shape
    m = place[0] if own else 1 - place[0]
    order = [*range(1, blocks, 2), *range(0, blocks, 2)]
    loads = {}
    for p in order:
        where = block_columns(place, own, p, blocks, width)
        loads[p] = (
            pltpu.make_async_copy(g_hbm.at[0, m, :, where], g.at[p], sem.at[p, 0]),
            pltpu.make_async_copy(e_hbm.at[0, m, :, where], e.at[p], sem.at[p, 1]),
        )
        for load in loads[p]:
            load.start()
    if own:
        write_factor(factor, place, False, w_ref, vec_ref, (other_even, other_odd))
    for p in order:
        for load in loads[p]:
            load.wait()
        (even, odd)[p % 2][p // 2] = g[p].astype(f32) + e[p]


def combine(place, grads, errors, blocks, factor_of=()):
    rows, cols = grads.shape[2:]
    own = bool(factor_of)
    shape = (blocks, rows, cols // blocks)
    half = pltpu.VMEM((blocks // 2,) + shape[1:], f32)
    return call(
        functools.partial(combine_kernel, own=own),
        "own" if own else "other",
        [SMEM, ANY, ANY] + [VMEM] * len(factor_of),
        [VMEM] * (3 if own else 2),
        [half, half] + ([factor_shape(rows, factor_of[0])] if own else []),
        (place, grads, errors, *factor_of),
        mib=8,
        flops=rows * cols * (200 if own else 1),
        nbytes=rows * cols * 10,
        scratch=[pltpu.VMEM(shape, grads.dtype), pltpu.VMEM(shape, f32), pltpu.SemaphoreType.DMA((blocks, 2))],
    )


def fold_kernel(*refs, picks):
    for i, pick in enumerate(picks):
        refs[-1][i] = sum(refs[k][at] for k, at in pick)


def fold(terms, after=()):
    arrays, picks = [], []
    for pairs in terms:
        pick = []
        for a, at in pairs:
            if not any(a is b for b in arrays):
                arrays.append(a)
            pick.append((next(k for k, b in enumerate(arrays) if a is b), at))
        picks.append(pick)
    shape = (len(terms),) + arrays[0].shape[1:]
    return call(
        functools.partial(fold_kernel, picks=picks),
        "fold",
        [VMEM] * len(arrays) + [ANY] * len(after),
        VMEM,
        pltpu.VMEM(shape, f32),
        (*arrays, *after),
        nbytes=4 * len(picks[0]) * shape[0] * shape[1] * shape[2],
    )


def project_kernel(x_ref, *refs, places, count):
    parts, (s_ref, v_ref) = refs[:-2], refs[-2:]
    block = sum(part[at] for part, at in zip(parts, places))
    s_ref[...] = block
    v_ref[...] = dot(x_ref[:, : block.shape[0]] / count, block) / count


def lift_kernel(v_ref, s_ref, u_ref, *, count):
    u_ref[...] = dot(v_ref[...], s_ref[...], NT) / count


def lower_kernel(u_ref, s_ref, v_ref, *, count):
    v_ref[...] = dot(u_ref[...], s_ref[...]) / count


def identity(rank):
    return (
        lax.broadcasted_iota(jnp.int32, (rank, rank), 0)
        == lax.broadcasted_iota(jnp.int32, (rank, rank), 1)
    ).astype(f32)


def sweeps(left, right, first, last):
    eye = identity(left.shape[0])
    for sweep in range(first, last):
        middle = 1.5 * eye - 0.5 * (left if sweep == 0 else dot(right, left))
        right = middle if sweep == 0 else dot(middle, right)
        if sweep + 1 < ROOT_ITERS:
            left = dot(left, middle)
    return left, right


def root_begin(gram, state):
    spread = jnp.sqrt(jnp.sum(gram * gram, keepdims=True))
    left, right = sweeps(gram / spread, None, 0, ROOT_ITERS // 2)
    state[0], state[1] = left, right
    state[2] = jnp.broadcast_to(spread, gram.shape)


def root_end(state):
    _, right = sweeps(state[0], state[1], ROOT_ITERS // 2, ROOT_ITERS)
    return right / jnp.sqrt(state[2])


def first_begin_kernel(x_ref, state, *, rows, count):
    factor = x_ref[:, :rows] / count
    root_begin(dot(factor, factor, NT), state)


def first_end_kernel(state, a_ref):
    a_ref[...] = root_end(state)


def second_begin_kernel(a_ref, u_ref, state):
    a, u = a_ref[...], u_ref[...]
    root_begin(dot(a, dot(dot(u, u, NT), a), TN), state)


def second_end_kernel(state, a_ref, u_ref, f_ref):
    u = u_ref[...]
    rank, rows = u.shape
    both = dot(a_ref[...], root_end(state))
    f_ref[...] = jnp.zeros(f_ref.shape, f32)
    f_ref[:, :rows] = dot(both, u, TN)
    f_ref[:, rows : rows + rank] = both


def taken_items(place, owners, slots):
    items, before = [jnp.int32(-1)] * slots, jnp.int32(0)
    for item in range(owners.shape[0]):
        mine = owners[item] == place[2]
        items = [jnp.where(mine & (before == slot), item, old) for slot, old in enumerate(items)]
        before = before + jnp.where(mine, 1, 0)
    return items


def gains_kernel(place, owners, own_ref, other_ref, mv_ref, wv_ref, mo_ref, wo_ref, vec, *, count, first):
    for i in range(mv_ref.shape[1] // LANES):
        at = slice(i * LANES, (i + 1) * LANES)
        for k, ref in enumerate((own_ref, other_ref)):
            vec[k : k + 1, at] = ref[i : i + 1, ref.shape[1] - LANES :] / count
    for slot, item in enumerate(taken_items(place, owners, mv_ref.shape[0])):
        row = jnp.where(item - first == place[0], vec[0:1, :], vec[1:2, :])
        old, weight = mv_ref[slot : slot + 1, :], wv_ref[slot : slot + 1, :]
        new = 0.9 * old + row
        mo_ref[slot : slot + 1, :] = jnp.where(item >= first, new, old)
        wo_ref[slot : slot + 1, :] = jnp.where(item >= first, weight - 0.5 * new, weight)


def gains(place, owners, own, other, vec_momentum, vec_weights, count, first):
    return call(
        functools.partial(gains_kernel, count=count, first=first),
        "gains",
        [SMEM, SMEM] + [VMEM] * 4,
        [VMEM] * 2,
        [jax.ShapeDtypeStruct(vec_momentum.shape, f32)] * 2,
        (place, owners, own, other, vec_momentum, vec_weights),
        flops=10 * vec_momentum.size,
        nbytes=16 * vec_momentum.size,
        scratch=[pltpu.VMEM((2, vec_momentum.shape[1]), f32)],
    )


def banks_kernel(mm_hbm, mw_hbm, mm, mw, sem):
    loads = (pltpu.make_async_copy(mm_hbm, mm, sem.at[0]), pltpu.make_async_copy(mw_hbm, mw, sem.at[1]))
    for load in loads:
        load.start()
    for load in loads:
        load.wait()


def banks(mat_momentum, mat_weights):
    return call(
        banks_kernel,
        "banks",
        [ANY, ANY],
        [VMEM] * 2,
        [pltpu.VMEM(mat_momentum.shape, f32)] * 2,
        (mat_momentum, mat_weights),
        nbytes=8 * mat_momentum.size,
        scratch=[pltpu.SemaphoreType.DMA((2,))],
    )


def finish_kernel(
    place, owners, v0_ref, v1_ref, f0_ref, f1_ref, c0_even, c0_odd, c1_even, c1_odd, mm, mw, *refs, positions, head, later
):
    if later:
        left, refs = refs[0], refs[1 + 3 :]
        n_hbm, mo_hbm, wo_hbm, errors, approx, moment, weight, sem, bank_sem = refs
    else:
        n_hbm, mo_hbm, wo_hbm, left, errors, approx, moment, weight, sem, bank_sem = refs
    rank, width = v0_ref.shape[1:]
    blocks, rows = 2 * c0_even.shape[0], c0_even.shape[1]
    per = rows // head
    if not later:
        for i, f_ref in enumerate((f0_ref, f1_ref)):
            high, middle, low = split3(f_ref[:, :rows].T)
            left[i] = jnp.concatenate([high, high, middle, high, low, middle], axis=1)
    units = [(k, p, i) for k, p in enumerate(positions) for i in range(2)]
    rights = []
    for k, p, i in units:
        f_ref, v_ref = ((f0_ref, v0_ref), (f1_ref, v1_ref))[i]
        high, middle, low = split3(dot(f_ref[:, rows : rows + rank], v_ref[k], TN))
        rights.append(jnp.concatenate([high, middle, high, low, high, middle], axis=0))
    stores = []
    for (k, p, i), right in zip(units, rights):
        m = place[0] if i == 0 else 1 - place[0]
        product = jnp.dot(left[i], right, preferred_element_type=f32)
        approx[k, i] = product
        errors[k, i] = ((c0_even, c0_odd), (c1_even, c1_odd))[i][p % 2][p // 2] - product
        columns = block_columns(place, i == 0, p, blocks, width)
        stores.append(pltpu.make_async_copy(errors.at[k, i], n_hbm.at[0, m, :, columns], sem.at[k, i]))
        stores[-1].start()
    bank_stores = []
    items = taken_items(place, owners, mm.shape[0])
    for k, p, i in units:
        m = place[0] if i == 0 else 1 - place[0]
        columns = block_columns(place, i == 0, p, blocks, width)
        for slot, item in enumerate(items):
            taken = (item >= m * per) & (item < (m + 1) * per)
            idle = (item < 0) | (item >= 2 * per)
            copies = (
                pltpu.make_async_copy(
                    moment.at[k, i, slot], mo_hbm.at[slot, :, columns], bank_sem.at[k, i, slot, 0]
                ),
                pltpu.make_async_copy(
                    weight.at[k, i, slot], wo_hbm.at[slot, :, columns], bank_sem.at[k, i, slot, 1]
                ),
            )

            @pl.when(taken)
            def _():
                at = pl.ds(pl.multiple_of((item - m * per) * head, head), head)
                new = 0.9 * mm[slot, :, columns] + approx[k, i, at, :]
                moment[k, i, slot] = new
                weight[k, i, slot] = mw[slot, :, columns] - 0.5 * new
                for copy in copies:
                    copy.start()

            writes = taken
            if i == 0:
                writes = taken | idle

                @pl.when(idle)
                def _():
                    moment[k, i, slot] = mm[slot, :, columns]
                    weight[k, i, slot] = mw[slot, :, columns]
                    for copy in copies:
                        copy.start()

            bank_stores.append((writes, copies))
    for store in stores:
        store.wait()
    for writes, copies in bank_stores:

        @pl.when(writes)
        def _():
            for copy in copies:
                copy.wait()


def finish(positions, left, outs, place, owners, own_v, other_v, own_f, other_f, own_c, other_c, shapes, mm, mw):
    n, rank, width = own_v.shape
    matrices, rows, cols = shapes[0][1:]
    slots, head = mm.shape[:2]
    later = len(outs) > 0
    inputs = 12 + len(left)
    first = [] if later else [pltpu.VMEM((2, rows, 6 * rank), jnp.bfloat16)]
    return call(
        functools.partial(finish_kernel, positions=positions, head=head, later=later),
        f"finish{positions[0]}",
        [SMEM, SMEM] + [VMEM] * (10 + len(left)) + [ANY] * len(outs),
        [ANY] * 3 + [VMEM] * len(first),
        [pltpu.HBM(s, f32) for s in shapes] + first,
        (place, owners, own_v, other_v, own_f, other_f, *own_c, *other_c, mm, mw, *left, *outs),
        mib=4 + 5 * n,
        flops=2 * n * matrices * rows * width * 6 * rank,
        nbytes=4 * n * width * (matrices * rows + 4 * slots * head),
        scratch=[
            pltpu.VMEM((n, 2, rows, width), f32),
            pltpu.VMEM((n, 2, rows, width), f32),
            pltpu.VMEM((n, 2, slots, head, width), f32),
            pltpu.VMEM((n, 2, slots, head, width), f32),
            pltpu.SemaphoreType.DMA((n, 2)),
            pltpu.SemaphoreType.DMA((n, 2, slots, 2)),
        ],
        aliases={inputs + i: i for i in range(len(outs))},
    )


def mirror(p, bits):
    return sum((p >> i & 1) << (bits - 1 - i) for i in range(bits))


def partner(kind, step):
    planes = (lax.axis_size("rep") // 2).bit_length() - 1
    depths = lax.axis_size("grp").bit_length() - 1

    def of(rep, grp):
        if kind == "core":
            return rep ^ 1, grp
        if kind == "plane":
            return rep ^ (2 << (step if rep % 2 == 0 else planes - 1 - step)), grp
        if kind == "depth":
            return rep, grp ^ step
        if kind == "place":
            return rep ^ 2 * (step if rep % 2 == 0 else mirror(step, planes)), grp
        return rep, grp ^ (1 << (step if rep % 2 == 0 else depths - 1 - step))

    return of


def exchange(a, kind, step=0):
    groups = lax.axis_size("grp")
    of = partner(kind, step)
    pairs = []
    for rep in range(lax.axis_size("rep")):
        for grp in range(groups):
            to_rep, to_grp = of(rep, grp)
            pairs.append((rep * groups + grp, to_rep * groups + to_grp))
    return lax.ppermute(a, ("rep", "grp"), pairs)


def hop(a, kind, step, work=None, *operands):
    if work is None:
        return a + exchange(a, kind, step)
    a, *operands = lax.optimization_barrier((a, *operands))
    steps = step if isinstance(step, list) else [step]
    arrived = [exchange(a, kind, each) for each in steps]
    done = work(*operands)
    arrived, done = lax.optimization_barrier((arrived, list(done)))
    return sum(arrived, a), *done


def local(grads, errors, warm_start, vec_grads, owners, mat_momentum, mat_weights, vec_momentum, vec_weights):
    reps, groups = lax.axis_size("rep"), lax.axis_size("grp")
    count = float(reps * groups)
    blocks = reps // 2
    bits = blocks.bit_length() - 1
    depths = groups.bit_length() - 1
    matrices, rows, cols = grads.shape[1:]
    rank = warm_start.shape[1]
    width = cols // blocks
    rep = lax.axis_index("rep")
    core, spot = rep % 2, rep // 2
    place = jnp.stack([core, spot, rep * groups + lax.axis_index("grp")]).astype(jnp.int32)
    head_items = matrices * (rows // mat_momentum.shape[1])

    grads, errors = in_hbm(grads), in_hbm(errors)
    mat_momentum, mat_weights = map(in_hbm, (mat_momentum, mat_weights))

    other_c = combine(place, grads, errors, blocks)
    arrived_odd = in_vmem(exchange(other_c[1], "core"))
    arrived_even = in_vmem(exchange(other_c[0], "core"))
    *own_c, other_p = combine(place, grads, errors, blocks, (warm_start, vec_grads, *other_c))

    terms = [[(own_c[p % 2], p // 2), ((arrived_even, arrived_odd)[p % 2], p // 2)] for p in range(blocks)]

    def send(goes, stage, after=()):
        return goes, stage, exchange(fold([terms[p] for p in goes], after), "plane", stage)

    def land(goes, stage, arrived):
        arrived = in_vmem(arrived)
        for i, p in enumerate(goes):
            terms[p ^ (1 << stage)].append((arrived, i))

    odd = [p for p in range(blocks) if p & 1]
    go = fold([terms[p] for p in odd if p & 2])
    ahead = [p for p in odd if p & 2], 0, exchange(go, "plane", 0)

    rest = [p for p in odd if not p & 2]
    go_rest = fold([terms[p] for p in rest])
    pending = [(rest, 0, exchange(go_rest, "plane", 0))]

    later, *_ = lax.optimization_barrier((place, go, go_rest))
    own_p = own_factor(later, own_c, warm_start, vec_grads)
    packed = own_p + exchange(other_p, "core")
    packed = hop(packed, "plane", bits - 1)
    packed = hop(packed, "z", 0)
    land(*ahead)
    for stage in range(1, bits):
        goes = [p for p in range(blocks) if p >> stage & 1 and not p & ((1 << stage) - 1)]
        if stage > 1:
            while pending:
                land(*pending.pop(0))
        pending.append(send(goes, stage, (packed,)))
    for step in range(1, depths):
        packed = hop(packed, "z", step)
    arrived, packed = lax.optimization_barrier((pending[0][2], packed))
    pending[0] = (*pending[0][:2], arrived)
    for step in range(bits - 2, -1, -1):
        packed = hop(packed, "plane", step)
    while pending:
        land(*pending.pop(0))

    kept_sum, v = small_call(
        functools.partial(project_kernel, places=[at for _, at in terms[0]], count=count),
        "project", [(rows, width), (rank, width)], packed, *[a for a, _ in terms[0]],
    )
    square = (rank, rank)
    state = (3, rank, rank)
    def first(x):
        (begun,) = small_call(functools.partial(first_begin_kernel, rows=rows, count=count), "root1a", [state], x)
        return small_call(first_end_kernel, "root1b", [square], begun)

    depth = list(range(1, groups))
    v, first_root = hop(v, "depth", depth, first, packed)
    (u,) = small_call(functools.partial(lift_kernel, count=count), "lift", [(rank, rows)], v, kept_sum)
    u, vec_momentum_out, vec_weights_out = hop(
        u, "depth", depth,
        lambda x, y: gains(place, owners, x, y, vec_momentum, vec_weights, count, head_items),
        packed, exchange(packed, "core"),
    )
    u, mm, mw = hop(u, "place", list(range(1, blocks)), banks, mat_momentum, mat_weights)
    (v,) = small_call(functools.partial(lower_kernel, count=count), "lower", [(rank, width)], u, kept_sum)
    def second(a, u):
        (begun,) = small_call(second_begin_kernel, "root2a", [state], a, u)
        return small_call(second_end_kernel, "root2b", [(rank, lanes(rows + rank))], begun, a, u)

    v, own_f = hop(v, "depth", depth, second, first_root, u)
    other_f = exchange(own_f, "core")
    shapes = [errors.shape, mat_momentum.shape, mat_weights.shape]
    v = v[None]
    other_v = exchange(v, "core")
    arrived = [exchange(v, "place", p) for p in range(1, blocks)]
    *outs, left = finish(
        [0], (), (), place, owners, v, other_v, own_f, other_f, own_c, other_c, shapes, mm, mw
    )
    *arrived, left = lax.optimization_barrier((*arrived, left))
    v = jnp.concatenate(arrived, axis=0)
    outs = finish(
        list(range(1, blocks)), (left,), outs, place, owners, v, exchange(v, "core"), own_f, other_f, own_c, other_c,
        shapes, mm, mw,
    )
    new_errors, mat_momentum_out, mat_weights_out = outs
    return (new_errors, mat_momentum_out, mat_weights_out, vec_momentum_out, vec_weights_out)


def solution(mesh):
    both = ("rep", "grp")
    return jax.shard_map(
        local,
        mesh=mesh,
        in_specs=(
            P(both, None, None, None),
            P(both, None, None, None),
            P(),
            P(both, None, None),
            P(),
            P(both, None, None),
            P(both, None, None),
            P(both, None),
            P(both, None),
        ),
        out_specs=(
            P(both, None, None, None),
            P(both, None, None),
            P(both, None, None),
            P(both, None),
            P(both, None),
        ),
        check_vma=False,
    )
```

```python
import functools

import jax
import jax.numpy as jnp
from jax import lax
from jax.experimental import pallas as pl
from jax.experimental.pallas import tpu as pltpu
from jax.sharding import PartitionSpec as P

ROOT_ITERS = 12
LANES = 128
f32 = jnp.float32
NN = ((1,), (0,))
NT = ((1,), (1,))
TN = ((0,), (0,))
ANY = pl.BlockSpec(memory_space=pl.ANY)
VMEM = pl.BlockSpec(memory_space=pltpu.VMEM)
SMEM = pl.BlockSpec(memory_space=pltpu.SMEM)


def dot(a, b, dims=NN):
    return lax.dot_general(
        a, b, (dims, ((), ())), precision=lax.Precision.HIGHEST, preferred_element_type=f32
    )


def split3(a):
    high = a.astype(jnp.bfloat16)
    rest = a - high.astype(f32)
    middle = rest.astype(jnp.bfloat16)
    low = (rest - middle.astype(f32)).astype(jnp.bfloat16)
    return high, middle, low


def lanes(n):
    return -(-n // LANES) * LANES


def pack_factor(out, u):
    rank, rows = u.shape
    whole, left = divmod(rows, LANES)
    for i in range(whole):
        out[i * rank : (i + 1) * rank, :] = u[:, i * LANES : (i + 1) * LANES]
    if left:
        short = rank * left // LANES
        for i in range(LANES // left):
            out[whole * rank : whole * rank + short, i * left : (i + 1) * left] = u[
                i * short : (i + 1) * short, whole * LANES :
            ]


def unpack_factor(x, rank, rows):
    whole, left = divmod(rows, LANES)
    parts = [x[i * rank : (i + 1) * rank, :] for i in range(whole)]
    if left:
        short = rank * left // LANES
        tail = x[whole * rank : whole * rank + short, :]
        parts.append(jnp.concatenate([tail[:, i * left : (i + 1) * left] for i in range(LANES // left)], axis=0))
    return jnp.concatenate(parts, axis=1)


def in_hbm(a):
    return pltpu.with_memory_space_constraint(a, pltpu.HBM)


def in_vmem(a):
    return pltpu.with_memory_space_constraint(a, pltpu.VMEM)


def call(kernel, name, in_specs, out_specs, out_shape, operands, mib=4, flops=0, nbytes=0, scratch=(), aliases={}):
    return pl.pallas_call(
        kernel,
        in_specs=in_specs,
        out_specs=out_specs,
        out_shape=out_shape,
        scratch_shapes=scratch,
        input_output_aliases=aliases,
        compiler_params=pltpu.CompilerParams(vmem_limit_bytes=mib << 20),
        cost_estimate=pl.CostEstimate(flops=flops, bytes_accessed=nbytes, transcendentals=0),
        name=name,
    )(*operands)


def small_call(kernel, name, shapes, *operands):
    return call(
        kernel,
        name,
        [VMEM] * len(operands),
        [VMEM] * len(shapes),
        [jax.ShapeDtypeStruct(s, f32) for s in shapes],
        operands,
        flops=12_000_000,
        nbytes=4 * sum(o.size for o in operands),
    )


def block_columns(place, own, p, blocks, width):
    bits = blocks.bit_length() - 1
    core = place[0] if own else 1 - place[0]
    block = place[1] ^ jnp.where(core == 0, p, mirror(p, bits))
    return pl.ds(pl.multiple_of(block * width, width), width)


def write_factor(out, place, own, w_ref, vec_ref, halves):
    half, rows, width = halves[0].shape
    rank = w_ref.shape[1]
    m = place[0] if own else 1 - place[0]
    terms = jnp.zeros((rows, 3 * rank), f32)
    for p in range(2 * half):
        w_high, w_middle, w_low = split3(w_ref[m, :, block_columns(place, own, p, 2 * half, width)])
        high, middle, _ = split3(halves[p % 2][p // 2])
        for part, pieces in (
            (high, (w_high, w_middle, w_low)),
            (middle, (w_high, w_middle, jnp.zeros_like(w_low))),
        ):
            terms += lax.dot_general(
                part, jnp.concatenate(pieces, axis=0), (NT, ((), ())), preferred_element_type=f32
            )
    pack_factor(out, (terms[:, :rank] + terms[:, rank : 2 * rank] + terms[:, 2 * rank :]).T)
    base = rank * rows // LANES
    mine = jnp.where(m == 0, vec_ref[0, 0:1, :], vec_ref[0, 1:2, :])
    for i in range(vec_ref.shape[2] // LANES):
        out[base + i : base + i + 1, :] = mine[:, i * LANES : (i + 1) * LANES]


def factor_shape(rows, warm_start):
    _, rank, cols = warm_start.shape
    return jax.ShapeDtypeStruct(((rank * rows + cols) // LANES, LANES), f32)


def factor_kernel(place, w_ref, vec_ref, even, odd, out):
    write_factor(out, place, True, w_ref, vec_ref, (even, odd))


def own_factor(place, halves, warm_start, vec_grads):
    rows = halves[0].shape[1]
    return call(
        factor_kernel,
        "factor",
        [SMEM] + [VMEM] * 4,
        VMEM,
        factor_shape(rows, warm_start),
        (place, warm_start, vec_grads, *halves),
        flops=12 * rows * warm_start.size,
        nbytes=8 * rows * warm_start.shape[2],
    )


def combine_kernel(place, g_hbm, e_hbm, *refs, own):
    if own:
        w_ref, vec_ref, other_even, other_odd, *refs = refs
        even, odd, factor, g, e, sem = refs
    else:
        even, odd, g, e, sem = refs
    blocks, rows, width = g.shape
    m = place[0] if own else 1 - place[0]
    order = [*range(1, blocks, 2), *range(0, blocks, 2)]
    loads = {}
    for p in order:
        where = block_columns(place, own, p, blocks, width)
        loads[p] = (
            pltpu.make_async_copy(g_hbm.at[0, m, :, where], g.at[p], sem.at[p, 0]),
            pltpu.make_async_copy(e_hbm.at[0, m, :, where], e.at[p], sem.at[p, 1]),
        )
        for load in loads[p]:
            load.start()
    if own:
        write_factor(factor, place, False, w_ref, vec_ref, (other_even, other_odd))
    for p in order:
        for load in loads[p]:
            load.wait()
        (even, odd)[p % 2][p // 2] = g[p].astype(f32) + e[p]


def combine(place, grads, errors, blocks, factor_of=()):
    rows, cols = grads.shape[2:]
    own = bool(factor_of)
    shape = (blocks, rows, cols // blocks)
    half = pltpu.VMEM((blocks // 2,) + shape[1:], f32)
    return call(
        functools.partial(combine_kernel, own=own),
        "own" if own else "other",
        [SMEM, ANY, ANY] + [VMEM] * len(factor_of),
        [VMEM] * (3 if own else 2),
        [half, half] + ([factor_shape(rows, factor_of[0])] if own else []),
        (place, grads, errors, *factor_of),
        mib=8,
        flops=rows * cols * (200 if own else 1),
        nbytes=rows * cols * 10,
        scratch=[pltpu.VMEM(shape, grads.dtype), pltpu.VMEM(shape, f32), pltpu.SemaphoreType.DMA((blocks, 2))],
    )


def fold_kernel(*refs, picks):
    for i, pick in enumerate(picks):
        refs[-1][i] = sum(refs[k][at] for k, at in pick)


def fold(terms, after=()):
    arrays, picks = [], []
    for pairs in terms:
        pick = []
        for a, at in pairs:
            if not any(a is b for b in arrays):
                arrays.append(a)
            pick.append((next(k for k, b in enumerate(arrays) if a is b), at))
        picks.append(pick)
    shape = (len(terms),) + arrays[0].shape[1:]
    return call(
        functools.partial(fold_kernel, picks=picks),
        "fold",
        [VMEM] * len(arrays) + [ANY] * len(after),
        VMEM,
        pltpu.VMEM(shape, f32),
        (*arrays, *after),
        nbytes=4 * len(picks[0]) * shape[0] * shape[1] * shape[2],
    )


def project_kernel(x_ref, *refs, places, count):
    parts, (s_ref, v_ref) = refs[:-2], refs[-2:]
    block = sum(part[at] for part, at in zip(parts, places))
    s_ref[...] = block
    v_ref[...] = dot(unpack_factor(x_ref[...], v_ref.shape[0], block.shape[0]) / count, block) / count


def lift_kernel(v_ref, s_ref, u_ref, *, count):
    pack_factor(u_ref, dot(v_ref[...], s_ref[...], NT) / count)


def lower_kernel(u_ref, s_ref, v_ref, *, count):
    v_ref[...] = dot(unpack_factor(u_ref[...], v_ref.shape[0], s_ref.shape[0]), s_ref[...]) / count


def identity(rank):
    return (
        lax.broadcasted_iota(jnp.int32, (rank, rank), 0)
        == lax.broadcasted_iota(jnp.int32, (rank, rank), 1)
    ).astype(f32)


def sweeps(left, right, first, last):
    eye = identity(left.shape[0])
    for sweep in range(first, last):
        middle = 1.5 * eye - 0.5 * (left if sweep == 0 else dot(right, left))
        right = middle if sweep == 0 else dot(middle, right)
        if sweep + 1 < ROOT_ITERS:
            left = dot(left, middle)
    return left, right


def root_begin(gram, state):
    spread = jnp.sqrt(jnp.sum(gram * gram, keepdims=True))
    left, right = sweeps(gram / spread, None, 0, ROOT_ITERS // 2)
    state[0], state[1] = left, right
    state[2] = jnp.broadcast_to(spread, gram.shape)


def root_end(state):
    _, right = sweeps(state[0], state[1], ROOT_ITERS // 2, ROOT_ITERS)
    return right / jnp.sqrt(state[2])


def first_begin_kernel(x_ref, state, *, rows, count):
    factor = unpack_factor(x_ref[...], state.shape[1], rows) / count
    root_begin(dot(factor, factor, NT), state)


def first_end_kernel(state, a_ref):
    a_ref[...] = root_end(state)


def second_begin_kernel(a_ref, u_ref, state, *, rows):
    a = a_ref[...]
    u = unpack_factor(u_ref[...], a.shape[0], rows)
    root_begin(dot(a, dot(dot(u, u, NT), a), TN), state)


def second_end_kernel(state, a_ref, u_ref, f_ref, *, rows):
    rank = a_ref.shape[0]
    u = unpack_factor(u_ref[...], rank, rows)
    both = dot(a_ref[...], root_end(state))
    f_ref[...] = jnp.zeros(f_ref.shape, f32)
    f_ref[:, :rows] = dot(both, u, TN)
    f_ref[:, rows : rows + rank] = both


def taken_items(place, owners, slots):
    items, before = [jnp.int32(-1)] * slots, jnp.int32(0)
    for item in range(owners.shape[0]):
        mine = owners[item] == place[2]
        items = [jnp.where(mine & (before == slot), item, old) for slot, old in enumerate(items)]
        before = before + jnp.where(mine, 1, 0)
    return items


def gains_kernel(place, owners, own_ref, other_ref, mv_ref, wv_ref, mo_ref, wo_ref, vec, *, count, first):
    for i in range(mv_ref.shape[1] // LANES):
        at = slice(i * LANES, (i + 1) * LANES)
        for k, ref in enumerate((own_ref, other_ref)):
            row = ref.shape[0] - mv_ref.shape[1] // LANES + i
            vec[k : k + 1, at] = ref[row : row + 1, :] / count
    for slot, item in enumerate(taken_items(place, owners, mv_ref.shape[0])):
        row = jnp.where(item - first == place[0], vec[0:1, :], vec[1:2, :])
        old, weight = mv_ref[slot : slot + 1, :], wv_ref[slot : slot + 1, :]
        new = 0.9 * old + row
        mo_ref[slot : slot + 1, :] = jnp.where(item >= first, new, old)
        wo_ref[slot : slot + 1, :] = jnp.where(item >= first, weight - 0.5 * new, weight)


def gains(place, owners, own, other, vec_momentum, vec_weights, count, first):
    return call(
        functools.partial(gains_kernel, count=count, first=first),
        "gains",
        [SMEM, SMEM] + [VMEM] * 4,
        [VMEM] * 2,
        [jax.ShapeDtypeStruct(vec_momentum.shape, f32)] * 2,
        (place, owners, own, other, vec_momentum, vec_weights),
        flops=10 * vec_momentum.size,
        nbytes=16 * vec_momentum.size,
        scratch=[pltpu.VMEM((2, vec_momentum.shape[1]), f32)],
    )


def banks_kernel(mm_hbm, mw_hbm, mm, mw, sem):
    loads = (pltpu.make_async_copy(mm_hbm, mm, sem.at[0]), pltpu.make_async_copy(mw_hbm, mw, sem.at[1]))
    for load in loads:
        load.start()
    for load in loads:
        load.wait()


def banks(mat_momentum, mat_weights):
    return call(
        banks_kernel,
        "banks",
        [ANY, ANY],
        [VMEM] * 2,
        [pltpu.VMEM(mat_momentum.shape, f32)] * 2,
        (mat_momentum, mat_weights),
        nbytes=8 * mat_momentum.size,
        scratch=[pltpu.SemaphoreType.DMA((2,))],
    )


def finish_kernel(
    place, owners, v0_ref, v1_ref, f0_ref, f1_ref, c0_even, c0_odd, c1_even, c1_odd, mm, mw, *refs, positions, head, later
):
    if later:
        left, refs = refs[0], refs[1 + 3 :]
        n_hbm, mo_hbm, wo_hbm, errors, approx, moment, weight, sem, bank_sem = refs
    else:
        n_hbm, mo_hbm, wo_hbm, left, errors, approx, moment, weight, sem, bank_sem = refs
    rank, width = v0_ref.shape[1:]
    blocks, rows = 2 * c0_even.shape[0], c0_even.shape[1]
    per = rows // head
    if not later:
        for i, f_ref in enumerate((f0_ref, f1_ref)):
            high, middle, low = split3(f_ref[:, :rows].T)
            left[i] = jnp.concatenate([high, high, middle, high, low, middle], axis=1)
    units = [(k, p, i) for k, p in enumerate(positions) for i in range(2)]
    rights = []
    for k, p, i in units:
        f_ref, v_ref = ((f0_ref, v0_ref), (f1_ref, v1_ref))[i]
        high, middle, low = split3(dot(f_ref[:, rows : rows + rank], v_ref[k], TN))
        rights.append(jnp.concatenate([high, middle, high, low, high, middle], axis=0))
    stores = []
    for (k, p, i), right in zip(units, rights):
        m = place[0] if i == 0 else 1 - place[0]
        product = jnp.dot(left[i], right, preferred_element_type=f32)
        approx[k, i] = product
        errors[k, i] = ((c0_even, c0_odd), (c1_even, c1_odd))[i][p % 2][p // 2] - product
        columns = block_columns(place, i == 0, p, blocks, width)
        stores.append(pltpu.make_async_copy(errors.at[k, i], n_hbm.at[0, m, :, columns], sem.at[k, i]))
        stores[-1].start()
    bank_stores = []
    items = taken_items(place, owners, mm.shape[0])
    for k, p, i in units:
        m = place[0] if i == 0 else 1 - place[0]
        columns = block_columns(place, i == 0, p, blocks, width)
        for slot, item in enumerate(items):
            taken = (item >= m * per) & (item < (m + 1) * per)
            idle = (item < 0) | (item >= 2 * per)
            copies = (
                pltpu.make_async_copy(
                    moment.at[k, i, slot], mo_hbm.at[slot, :, columns], bank_sem.at[k, i, slot, 0]
                ),
                pltpu.make_async_copy(
                    weight.at[k, i, slot], wo_hbm.at[slot, :, columns], bank_sem.at[k, i, slot, 1]
                ),
            )

            @pl.when(taken)
            def _():
                at = pl.ds(pl.multiple_of((item - m * per) * head, head), head)
                new = 0.9 * mm[slot, :, columns] + approx[k, i, at, :]
                moment[k, i, slot] = new
                weight[k, i, slot] = mw[slot, :, columns] - 0.5 * new
                for copy in copies:
                    copy.start()

            writes = taken
            if i == 0:
                writes = taken | idle

                @pl.when(idle)
                def _():
                    moment[k, i, slot] = mm[slot, :, columns]
                    weight[k, i, slot] = mw[slot, :, columns]
                    for copy in copies:
                        copy.start()

            bank_stores.append((writes, copies))
    for store in stores:
        store.wait()
    for writes, copies in bank_stores:

        @pl.when(writes)
        def _():
            for copy in copies:
                copy.wait()


def finish(positions, left, outs, place, owners, own_v, other_v, own_f, other_f, own_c, other_c, shapes, mm, mw):
    n, rank, width = own_v.shape
    matrices, rows, cols = shapes[0][1:]
    slots, head = mm.shape[:2]
    later = len(outs) > 0
    inputs = 12 + len(left)
    first = [] if later else [pltpu.VMEM((2, rows, 6 * rank), jnp.bfloat16)]
    return call(
        functools.partial(finish_kernel, positions=positions, head=head, later=later),
        f"finish{positions[0]}",
        [SMEM, SMEM] + [VMEM] * (10 + len(left)) + [ANY] * len(outs),
        [ANY] * 3 + [VMEM] * len(first),
        [pltpu.HBM(s, f32) for s in shapes] + first,
        (place, owners, own_v, other_v, own_f, other_f, *own_c, *other_c, mm, mw, *left, *outs),
        mib=4 + 5 * n,
        flops=2 * n * matrices * rows * width * 6 * rank,
        nbytes=4 * n * width * (matrices * rows + 4 * slots * head),
        scratch=[
            pltpu.VMEM((n, 2, rows, width), f32),
            pltpu.VMEM((n, 2, rows, width), f32),
            pltpu.VMEM((n, 2, slots, head, width), f32),
            pltpu.VMEM((n, 2, slots, head, width), f32),
            pltpu.SemaphoreType.DMA((n, 2)),
            pltpu.SemaphoreType.DMA((n, 2, slots, 2)),
        ],
        aliases={inputs + i: i for i in range(len(outs))},
    )


def mirror(p, bits):
    return sum((p >> i & 1) << (bits - 1 - i) for i in range(bits))


def partner(kind, step):
    planes = (lax.axis_size("rep") // 2).bit_length() - 1
    depths = lax.axis_size("grp").bit_length() - 1

    def of(rep, grp):
        if kind == "core":
            return rep ^ 1, grp
        if kind == "plane":
            return rep ^ (2 << (step if rep % 2 == 0 else planes - 1 - step)), grp
        if kind == "depth":
            return rep, grp ^ step
        if kind == "place":
            return rep ^ 2 * (step if rep % 2 == 0 else mirror(step, planes)), grp
        return rep, grp ^ (1 << (step if rep % 2 == 0 else depths - 1 - step))

    return of


def exchange(a, kind, step=0):
    groups = lax.axis_size("grp")
    of = partner(kind, step)
    pairs = []
    for rep in range(lax.axis_size("rep")):
        for grp in range(groups):
            to_rep, to_grp = of(rep, grp)
            pairs.append((rep * groups + grp, to_rep * groups + to_grp))
    return lax.ppermute(a, ("rep", "grp"), pairs)


def hop(a, kind, step, work=None, *operands):
    if work is None:
        return a + exchange(a, kind, step)
    a, *operands = lax.optimization_barrier((a, *operands))
    steps = step if isinstance(step, list) else [step]
    arrived = [exchange(a, kind, each) for each in steps]
    done = work(*operands)
    arrived, done = lax.optimization_barrier((arrived, list(done)))
    return sum(arrived, a), *done


def local(grads, errors, warm_start, vec_grads, owners, mat_momentum, mat_weights, vec_momentum, vec_weights):
    reps, groups = lax.axis_size("rep"), lax.axis_size("grp")
    count = float(reps * groups)
    blocks = reps // 2
    bits = blocks.bit_length() - 1
    depths = groups.bit_length() - 1
    matrices, rows, cols = grads.shape[1:]
    rank = warm_start.shape[1]
    width = cols // blocks
    rep = lax.axis_index("rep")
    core, spot = rep % 2, rep // 2
    place = jnp.stack([core, spot, rep * groups + lax.axis_index("grp")]).astype(jnp.int32)
    head_items = matrices * (rows // mat_momentum.shape[1])

    grads, errors = in_hbm(grads), in_hbm(errors)
    mat_momentum, mat_weights = map(in_hbm, (mat_momentum, mat_weights))

    other_c = combine(place, grads, errors, blocks)
    arrived_odd = in_vmem(exchange(other_c[1], "core"))
    arrived_even = in_vmem(exchange(other_c[0], "core"))
    *own_c, other_p = combine(place, grads, errors, blocks, (warm_start, vec_grads, *other_c))

    terms = [[(own_c[p % 2], p // 2), ((arrived_even, arrived_odd)[p % 2], p // 2)] for p in range(blocks)]

    def send(goes, stage, after=()):
        return goes, stage, exchange(fold([terms[p] for p in goes], after), "plane", stage)

    def land(goes, stage, arrived):
        arrived = in_vmem(arrived)
        for i, p in enumerate(goes):
            terms[p ^ (1 << stage)].append((arrived, i))

    odd = [p for p in range(blocks) if p & 1]
    go = fold([terms[p] for p in odd if p & 2])
    ahead = [p for p in odd if p & 2], 0, exchange(go, "plane", 0)

    rest = [p for p in odd if not p & 2]
    go_rest = fold([terms[p] for p in rest])
    pending = [(rest, 0, exchange(go_rest, "plane", 0))]

    later, *_ = lax.optimization_barrier((place, go, go_rest))
    own_p = own_factor(later, own_c, warm_start, vec_grads)
    packed = own_p + exchange(other_p, "core")
    packed, mm, mw = hop(packed, "plane", bits - 1, banks, mat_momentum, mat_weights)
    packed = hop(packed, "z", 0)
    land(*ahead)
    for stage in range(1, bits):
        goes = [p for p in range(blocks) if p >> stage & 1 and not p & ((1 << stage) - 1)]
        if stage > 1:
            while pending:
                land(*pending.pop(0))
        pending.append(send(goes, stage, (packed,)))
    for step in range(1, depths):
        packed = hop(packed, "z", step)
    for step in range(bits - 2, 0, -1):
        packed = hop(packed, "plane", step)
    land(*pending.pop(0))
    packed, keep = hop(packed, "plane", 0, lambda *x: [fold([list(zip(x, [at for _, at in terms[0]]))])],
                       *[a for a, _ in terms[0]])
    terms[0] = [(keep, 0)]
    while pending:
        land(*pending.pop(0))

    kept_sum, v = small_call(
        functools.partial(project_kernel, places=[at for _, at in terms[0]], count=count),
        "project", [(rows, width), (rank, width)], packed, *[a for a, _ in terms[0]],
    )
    square = (rank, rank)
    state = (3, rank, rank)
    depth = list(range(1, groups))
    v, first_state = hop(
        v, "depth", depth,
        lambda x: small_call(
            functools.partial(first_begin_kernel, rows=rows, count=count), "root1a", [state], x
        ), packed,
    )
    (u,) = small_call(functools.partial(lift_kernel, count=count), "lift", [(rank * rows // LANES, LANES)], v, kept_sum)
    u, first_root = hop(u, "depth", depth, lambda x: small_call(first_end_kernel, "root1b", [square], x), first_state)
    u, vec_momentum_out, vec_weights_out = hop(
        u, "place", list(range(1, blocks)),
        lambda x, y: gains(place, owners, x, y, vec_momentum, vec_weights, count, head_items),
        packed, exchange(packed, "core"),
    )
    (v,) = small_call(functools.partial(lower_kernel, count=count), "lower", [(rank, width)], u, kept_sum)
    def second(a, u):
        (begun,) = small_call(functools.partial(second_begin_kernel, rows=rows), "root2a", [state], a, u)
        return small_call(
            functools.partial(second_end_kernel, rows=rows), "root2b", [(rank, lanes(rows + rank))], begun, a, u
        )

    v, own_f = hop(v, "depth", depth, second, first_root, u)

    shapes = [errors.shape, mat_momentum.shape, mat_weights.shape]
    swapped = exchange(jnp.concatenate([v, own_f], axis=1), "core")
    other_v, other_f = swapped[None, :, :width], swapped[:, width:]
    v = v[None]
    arrived = [exchange(v, "place", p) for p in range(1, blocks)]
    *outs, left = finish(
        [0], (), (), place, owners, v, other_v, own_f, other_f, own_c, other_c, shapes, mm, mw
    )
    *arrived, left = lax.optimization_barrier((*arrived, left))
    v = jnp.concatenate(arrived, axis=0)
    outs = finish(
        list(range(1, blocks)), (left,), outs, place, owners, v, exchange(v, "core"), own_f, other_f, own_c, other_c,
        shapes, mm, mw,
    )
    new_errors, mat_momentum_out, mat_weights_out = outs
    return (new_errors, mat_momentum_out, mat_weights_out, vec_momentum_out, vec_weights_out)


def solution(mesh):
    both = ("rep", "grp")
    return jax.shard_map(
        local,
        mesh=mesh,
        in_specs=(
            P(both, None, None, None),
            P(both, None, None, None),
            P(),
            P(both, None, None),
            P(),
            P(both, None, None),
            P(both, None, None),
            P(both, None),
            P(both, None),
        ),
        out_specs=(
            P(both, None, None, None),
            P(both, None, None),
            P(both, None, None),
            P(both, None),
            P(both, None),
        ),
        check_vma=False,
    )
```

```python
import functools

import jax
import jax.numpy as jnp
from jax import lax
from jax.experimental import pallas as pl
from jax.experimental.pallas import tpu as pltpu
from jax.sharding import PartitionSpec as P

ROOT_ITERS = 12
LANES = 128
f32 = jnp.float32
NN = ((1,), (0,))
NT = ((1,), (1,))
TN = ((0,), (0,))
ANY = pl.BlockSpec(memory_space=pl.ANY)
VMEM = pl.BlockSpec(memory_space=pltpu.VMEM)
SMEM = pl.BlockSpec(memory_space=pltpu.SMEM)


def dot(a, b, dims=NN):
    return lax.dot_general(
        a, b, (dims, ((), ())), precision=lax.Precision.HIGHEST, preferred_element_type=f32
    )


def split3(a):
    high = a.astype(jnp.bfloat16)
    rest = a - high.astype(f32)
    middle = rest.astype(jnp.bfloat16)
    low = (rest - middle.astype(f32)).astype(jnp.bfloat16)
    return high, middle, low


def lanes(n):
    return -(-n // LANES) * LANES


def pack_factor(out, u):
    rank, rows = u.shape
    whole, left = divmod(rows, LANES)
    for i in range(whole):
        out[i * rank : (i + 1) * rank, :] = u[:, i * LANES : (i + 1) * LANES]
    if left:
        short = rank * left // LANES
        for i in range(LANES // left):
            out[whole * rank : whole * rank + short, i * left : (i + 1) * left] = u[
                i * short : (i + 1) * short, whole * LANES :
            ]


def unpack_factor(x, rank, rows):
    whole, left = divmod(rows, LANES)
    parts = [x[i * rank : (i + 1) * rank, :] for i in range(whole)]
    if left:
        short = rank * left // LANES
        tail = x[whole * rank : whole * rank + short, :]
        parts.append(jnp.concatenate([tail[:, i * left : (i + 1) * left] for i in range(LANES // left)], axis=0))
    return jnp.concatenate(parts, axis=1)


def in_hbm(a):
    return pltpu.with_memory_space_constraint(a, pltpu.HBM)


def in_vmem(a):
    return pltpu.with_memory_space_constraint(a, pltpu.VMEM)


def call(kernel, name, in_specs, out_specs, out_shape, operands, mib=4, flops=1, nbytes=1, scratch=(), aliases={}):
    return pl.pallas_call(
        kernel,
        in_specs=in_specs,
        out_specs=out_specs,
        out_shape=out_shape,
        scratch_shapes=scratch,
        input_output_aliases=aliases,
        compiler_params=pltpu.CompilerParams(vmem_limit_bytes=mib << 20),
        cost_estimate=pl.CostEstimate(flops=flops, bytes_accessed=nbytes, transcendentals=0),
        name=name,
    )(*operands)


def small_call(kernel, name, shapes, *operands):
    return call(
        kernel,
        name,
        [VMEM] * len(operands),
        [VMEM] * len(shapes),
        [jax.ShapeDtypeStruct(s, f32) for s in shapes],
        operands,
        flops=12_000_000,
        nbytes=4 * sum(o.size for o in operands),
    )


def block_columns(place, own, p, blocks, width):
    bits = blocks.bit_length() - 1
    core = place[0] if own else 1 - place[0]
    block = place[1] ^ jnp.where(core == 0, p, mirror(p, bits))
    return pl.ds(pl.multiple_of(block * width, width), width)


def part_of_factor(place, own, w_ref, part, places, blocks):
    _, rows, width = part.shape
    rank = w_ref.shape[1]
    m = place[0] if own else 1 - place[0]
    terms = jnp.zeros((rows, 3 * rank), f32)
    for i, p in enumerate(places):
        w_high, w_middle, w_low = split3(w_ref[m, :, block_columns(place, own, p, blocks, width)])
        high, middle, _ = split3(part[i])
        for piece, pieces in (
            (high, (w_high, w_middle, w_low)),
            (middle, (w_high, w_middle, jnp.zeros_like(w_low))),
        ):
            terms += lax.dot_general(
                piece, jnp.concatenate(pieces, axis=0), (NT, ((), ())), preferred_element_type=f32
            )
    return (terms[:, :rank] + terms[:, rank : 2 * rank] + terms[:, 2 * rank :]).T


def write_factor(out, place, own, factor, vec_ref):
    rank, rows = factor.shape
    pack_factor(out, factor)
    base = rank * rows // LANES
    mine = jnp.where((place[0] if own else 1 - place[0]) == 0, vec_ref[0, 0:1, :], vec_ref[0, 1:2, :])
    for i in range(vec_ref.shape[2] // LANES):
        out[base + i : base + i + 1, :] = mine[:, i * LANES : (i + 1) * LANES]


def factor_shape(rows, warm_start):
    _, rank, cols = warm_start.shape
    return jax.ShapeDtypeStruct(((rank * rows + cols) // LANES, LANES), f32)


def factor_kernel(place, w_ref, vec_ref, part, before, out, *, places, blocks):
    factor = before[...] + part_of_factor(place, True, w_ref, part, places, blocks)
    write_factor(out, place, True, factor, vec_ref)


def own_factor(place, part, places, before, warm_start, vec_grads, blocks):
    return call(
        functools.partial(factor_kernel, places=places, blocks=blocks),
        "factor",
        [SMEM] + [VMEM] * 4,
        VMEM,
        factor_shape(part.shape[1], warm_start),
        (place, warm_start, vec_grads, part, before),
    )


def combine_kernel(place, g_hbm, e_hbm, *refs, own, groups, blocks, sides):
    refs = list(refs)
    if sides:
        w_ref, vec_ref = refs.pop(0), refs.pop(0)
    ins = [[refs.pop(0) for _ in spots] for _, spots, _ in sides]
    outs = [refs.pop(0) for _ in groups]
    factors = [refs.pop(0) for _ in sides]
    g, e, sem = refs
    m = place[0] if own else 1 - place[0]
    loads = []
    for i, p in enumerate(sum(groups, [])):
        where = block_columns(place, own, p, blocks, g.shape[2])
        loads.append(
            (
                pltpu.make_async_copy(g_hbm.at[0, m, :, where], g.at[i], sem.at[i, 0]),
                pltpu.make_async_copy(e_hbm.at[0, m, :, where], e.at[i], sem.at[i, 1]),
            )
        )
        for load in loads[-1]:
            load.start()
    for (whose, spots, whole), parts, factor in zip(sides, ins, factors):
        value = sum(part_of_factor(place, whose, w_ref, part, at, blocks) for part, at in zip(parts, spots))
        if whole:
            write_factor(factor, place, whose, value, vec_ref)
        else:
            factor[...] = value
    i = 0
    for out in outs:
        for at in range(out.shape[0]):
            for load in loads[i]:
                load.wait()
            out[at] = g[i].astype(f32) + e[i]
            i += 1


def combine(place, grads, errors, own, groups, blocks, sides=(), extra=()):
    rows, cols = grads.shape[2:]
    width = cols // blocks
    shape = (sum(map(len, groups)), rows, width)
    shapes = [
        factor_shape(rows, extra[0]) if whole else jax.ShapeDtypeStruct((extra[0].shape[1], rows), f32)
        for _, _, whole in sides
    ]
    return call(
        functools.partial(combine_kernel, own=own, groups=groups, blocks=blocks, sides=sides),
        ("own" if own else "other") + str(len(sides)),
        [SMEM, ANY, ANY] + [VMEM] * len(extra),
        [VMEM] * (len(groups) + len(sides)),
        [pltpu.VMEM((len(group), rows, width), f32) for group in groups] + shapes,
        (place, grads, errors, *extra),
        mib=8,
        scratch=[
            pltpu.VMEM(shape, grads.dtype), pltpu.VMEM(shape, f32), pltpu.SemaphoreType.DMA((shape[0], 2))
        ],
    )


def parted(blocks):
    front = [p for p in range(blocks) if p & 3 == 3]
    return front, [p for p in range(blocks) if p & 3 == 1] + list(range(0, blocks, 2))


def within(p, blocks):
    front, back = parted(blocks)
    return (0, front.index(p)) if p in front else (1, back.index(p))


def fold_kernel(*refs, picks):
    for i, pick in enumerate(picks):
        refs[-1][i] = sum(refs[k][at] for k, at in pick)


def fold(terms, after=()):
    arrays, picks = [], []
    for pairs in terms:
        pick = []
        for a, at in pairs:
            if not any(a is b for b in arrays):
                arrays.append(a)
            pick.append((next(k for k, b in enumerate(arrays) if a is b), at))
        picks.append(pick)
    shape = (len(terms),) + arrays[0].shape[1:]
    return call(
        functools.partial(fold_kernel, picks=picks),
        "fold",
        [VMEM] * len(arrays) + [ANY] * len(after),
        VMEM,
        pltpu.VMEM(shape, f32),
        (*arrays, *after),
        nbytes=4 * len(picks[0]) * shape[0] * shape[1] * shape[2],
    )


def project_kernel(x_ref, *refs, places, count):
    parts, (s_ref, v_ref) = refs[:-2], refs[-2:]
    block = sum(part[at] for part, at in zip(parts, places))
    s_ref[...] = block
    v_ref[...] = dot(unpack_factor(x_ref[...], v_ref.shape[0], block.shape[0]) / count, block) / count


def lift_kernel(v_ref, s_ref, u_ref, *, count):
    pack_factor(u_ref, dot(v_ref[...], s_ref[...], NT) / count)


def lower_kernel(u_ref, s_ref, v_ref, *, count):
    v_ref[...] = dot(unpack_factor(u_ref[...], v_ref.shape[0], s_ref.shape[0]), s_ref[...]) / count


def identity(rank):
    return (
        lax.broadcasted_iota(jnp.int32, (rank, rank), 0)
        == lax.broadcasted_iota(jnp.int32, (rank, rank), 1)
    ).astype(f32)


def sweeps(left, right, first, last):
    eye = identity(left.shape[0])
    for sweep in range(first, last):
        middle = 1.5 * eye - 0.5 * (left if sweep == 0 else dot(right, left))
        right = middle if sweep == 0 else dot(middle, right)
        if sweep + 1 < ROOT_ITERS:
            left = dot(left, middle)
    return left, right


def root_begin(gram, state):
    spread = jnp.sqrt(jnp.sum(gram * gram, keepdims=True))
    left, right = sweeps(gram / spread, None, 0, ROOT_ITERS // 2)
    state[0], state[1] = left, right
    state[2] = jnp.broadcast_to(spread, gram.shape)


def root_end(state):
    _, right = sweeps(state[0], state[1], ROOT_ITERS // 2, ROOT_ITERS)
    return right / jnp.sqrt(state[2])


def first_begin_kernel(x_ref, state, *, rows, count):
    factor = unpack_factor(x_ref[...], state.shape[1], rows) / count
    root_begin(dot(factor, factor, NT), state)


def first_end_kernel(state, a_ref):
    a_ref[...] = root_end(state)


def second_begin_kernel(a_ref, u_ref, state, *, rows):
    a = a_ref[...]
    u = unpack_factor(u_ref[...], a.shape[0], rows)
    root_begin(dot(a, dot(dot(u, u, NT), a), TN), state)


def second_end_kernel(state, a_ref, u_ref, f_ref, *, rows):
    rank = a_ref.shape[0]
    u = unpack_factor(u_ref[...], rank, rows)
    both = dot(a_ref[...], root_end(state))
    f_ref[...] = jnp.zeros(f_ref.shape, f32)
    f_ref[:, :rows] = dot(both, u, TN)
    f_ref[:, rows : rows + rank] = both


def taken_items(place, owners, slots):
    items, before = [jnp.int32(-1)] * slots, jnp.int32(0)
    for item in range(owners.shape[0]):
        mine = owners[item] == place[2]
        items = [jnp.where(mine & (before == slot), item, old) for slot, old in enumerate(items)]
        before = before + jnp.where(mine, 1, 0)
    return items


def gains_kernel(place, owners, own_ref, other_ref, mv_ref, wv_ref, mo_ref, wo_ref, vec, *, count, first):
    for i in range(mv_ref.shape[1] // LANES):
        at = slice(i * LANES, (i + 1) * LANES)
        for k, ref in enumerate((own_ref, other_ref)):
            row = ref.shape[0] - mv_ref.shape[1] // LANES + i
            vec[k : k + 1, at] = ref[row : row + 1, :] / count
    for slot, item in enumerate(taken_items(place, owners, mv_ref.shape[0])):
        row = jnp.where(item - first == place[0], vec[0:1, :], vec[1:2, :])
        old, weight = mv_ref[slot : slot + 1, :], wv_ref[slot : slot + 1, :]
        new = 0.9 * old + row
        mo_ref[slot : slot + 1, :] = jnp.where(item >= first, new, old)
        wo_ref[slot : slot + 1, :] = jnp.where(item >= first, weight - 0.5 * new, weight)


def gains(place, owners, own, other, vec_momentum, vec_weights, count, first):
    return call(
        functools.partial(gains_kernel, count=count, first=first),
        "gains",
        [SMEM, SMEM] + [VMEM] * 4,
        [VMEM] * 2,
        [jax.ShapeDtypeStruct(vec_momentum.shape, f32)] * 2,
        (place, owners, own, other, vec_momentum, vec_weights),
        flops=10 * vec_momentum.size,
        nbytes=16 * vec_momentum.size,
        scratch=[pltpu.VMEM((2, vec_momentum.shape[1]), f32)],
    )


def banks_kernel(mm_hbm, mw_hbm, mm, mw, sem):
    loads = (pltpu.make_async_copy(mm_hbm, mm, sem.at[0]), pltpu.make_async_copy(mw_hbm, mw, sem.at[1]))
    for load in loads:
        load.start()
    for load in loads:
        load.wait()


def banks(mat_momentum, mat_weights):
    return call(
        banks_kernel,
        "banks",
        [ANY, ANY],
        [VMEM] * 2,
        [pltpu.VMEM(mat_momentum.shape, f32)] * 2,
        (mat_momentum, mat_weights),
        nbytes=8 * mat_momentum.size,
        scratch=[pltpu.SemaphoreType.DMA((2,))],
    )


def finish_kernel(
    place, owners, v0_ref, v1_ref, f0_ref, f1_ref, c0_front, c0_back, c1_front, c1_back, mm, mw, *refs, positions, head, later
):
    if later:
        left, refs = refs[0], refs[1 + 3 :]
        n_hbm, mo_hbm, wo_hbm, errors, approx, moment, weight, sem, bank_sem = refs
    else:
        n_hbm, mo_hbm, wo_hbm, left, errors, approx, moment, weight, sem, bank_sem = refs
    rank, width = v0_ref.shape[1:]
    blocks, rows = c0_front.shape[0] + c0_back.shape[0], c0_front.shape[1]
    per = rows // head
    if not later:
        for i, f_ref in enumerate((f0_ref, f1_ref)):
            high, middle, low = split3(f_ref[:, :rows].T)
            left[i] = jnp.concatenate([high, high, middle, high, low, middle], axis=1)
    units = [(k, p, i) for k, p in enumerate(positions) for i in range(2)]
    rights = []
    for k, p, i in units:
        f_ref, v_ref = ((f0_ref, v0_ref), (f1_ref, v1_ref))[i]
        high, middle, low = split3(dot(f_ref[:, rows : rows + rank], v_ref[k], TN))
        rights.append(jnp.concatenate([high, middle, high, low, high, middle], axis=0))
    stores = []
    for (k, p, i), right in zip(units, rights):
        m = place[0] if i == 0 else 1 - place[0]
        product = jnp.dot(left[i], right, preferred_element_type=f32)
        approx[k, i] = product
        part, at = within(p, blocks)
        errors[k, i] = ((c0_front, c0_back), (c1_front, c1_back))[i][part][at] - product
        columns = block_columns(place, i == 0, p, blocks, width)
        stores.append(pltpu.make_async_copy(errors.at[k, i], n_hbm.at[0, m, :, columns], sem.at[k, i]))
        stores[-1].start()
    bank_stores = []
    items = taken_items(place, owners, mm.shape[0])
    for k, p, i in units:
        m = place[0] if i == 0 else 1 - place[0]
        columns = block_columns(place, i == 0, p, blocks, width)
        for slot, item in enumerate(items):
            taken = (item >= m * per) & (item < (m + 1) * per)
            idle = (item < 0) | (item >= 2 * per)
            copies = (
                pltpu.make_async_copy(
                    moment.at[k, i, slot], mo_hbm.at[slot, :, columns], bank_sem.at[k, i, slot, 0]
                ),
                pltpu.make_async_copy(
                    weight.at[k, i, slot], wo_hbm.at[slot, :, columns], bank_sem.at[k, i, slot, 1]
                ),
            )

            @pl.when(taken)
            def _():
                at = pl.ds(pl.multiple_of((item - m * per) * head, head), head)
                new = 0.9 * mm[slot, :, columns] + approx[k, i, at, :]
                moment[k, i, slot] = new
                weight[k, i, slot] = mw[slot, :, columns] - 0.5 * new
                for copy in copies:
                    copy.start()

            writes = taken
            if i == 0:
                writes = taken | idle

                @pl.when(idle)
                def _():
                    moment[k, i, slot] = mm[slot, :, columns]
                    weight[k, i, slot] = mw[slot, :, columns]
                    for copy in copies:
                        copy.start()

            bank_stores.append((writes, copies))
    for store in stores:
        store.wait()
    for writes, copies in bank_stores:

        @pl.when(writes)
        def _():
            for copy in copies:
                copy.wait()


def finish(positions, left, outs, place, owners, own_v, other_v, own_f, other_f, own_c, other_c, shapes, mm, mw):
    n, rank, width = own_v.shape
    matrices, rows, cols = shapes[0][1:]
    slots, head = mm.shape[:2]
    later = len(outs) > 0
    inputs = 12 + len(left)
    first = [] if later else [pltpu.VMEM((2, rows, 6 * rank), jnp.bfloat16)]
    return call(
        functools.partial(finish_kernel, positions=positions, head=head, later=later),
        f"finish{positions[0]}",
        [SMEM, SMEM] + [VMEM] * (10 + len(left)) + [ANY] * len(outs),
        [ANY] * 3 + [VMEM] * len(first),
        [pltpu.HBM(s, f32) for s in shapes] + first,
        (place, owners, own_v, other_v, own_f, other_f, *own_c, *other_c, mm, mw, *left, *outs),
        mib=4 + 5 * n,
        flops=2 * n * matrices * rows * width * 6 * rank,
        nbytes=4 * n * width * (matrices * rows + 4 * slots * head),
        scratch=[
            pltpu.VMEM((n, 2, rows, width), f32),
            pltpu.VMEM((n, 2, rows, width), f32),
            pltpu.VMEM((n, 2, slots, head, width), f32),
            pltpu.VMEM((n, 2, slots, head, width), f32),
            pltpu.SemaphoreType.DMA((n, 2)),
            pltpu.SemaphoreType.DMA((n, 2, slots, 2)),
        ],
        aliases={inputs + i: i for i in range(len(outs))},
    )


def mirror(p, bits):
    return sum((p >> i & 1) << (bits - 1 - i) for i in range(bits))


def partner(kind, step):
    planes = (lax.axis_size("rep") // 2).bit_length() - 1
    depths = lax.axis_size("grp").bit_length() - 1

    def of(rep, grp):
        if kind == "core":
            return rep ^ 1, grp
        if kind == "plane":
            return rep ^ (2 << (step if rep % 2 == 0 else planes - 1 - step)), grp
        if kind == "depth":
            return rep, grp ^ step
        if kind == "place":
            return rep ^ 2 * (step if rep % 2 == 0 else mirror(step, planes)), grp
        return rep, grp ^ (1 << (step if rep % 2 == 0 else depths - 1 - step))

    return of


def exchange(a, kind, step=0):
    groups = lax.axis_size("grp")
    of = partner(kind, step)
    pairs = []
    for rep in range(lax.axis_size("rep")):
        for grp in range(groups):
            to_rep, to_grp = of(rep, grp)
            pairs.append((rep * groups + grp, to_rep * groups + to_grp))
    return lax.ppermute(a, ("rep", "grp"), pairs)


def hop(a, kind, step, work=None, *operands):
    if work is None:
        return a + exchange(a, kind, step)
    a, *operands = lax.optimization_barrier((a, *operands))
    steps = step if isinstance(step, list) else [step]
    arrived = [exchange(a, kind, each) for each in steps]
    done = work(*operands)
    arrived, done = lax.optimization_barrier((arrived, list(done)))
    return sum(arrived, a), *done


def local(grads, errors, warm_start, vec_grads, owners, mat_momentum, mat_weights, vec_momentum, vec_weights):
    reps, groups = lax.axis_size("rep"), lax.axis_size("grp")
    count = float(reps * groups)
    blocks = reps // 2
    bits = blocks.bit_length() - 1
    depths = groups.bit_length() - 1
    matrices, rows, cols = grads.shape[1:]
    rank = warm_start.shape[1]
    width = cols // blocks
    rep = lax.axis_index("rep")
    core, spot = rep % 2, rep // 2
    place = jnp.stack([core, spot, rep * groups + lax.axis_index("grp")]).astype(jnp.int32)
    head_items = matrices * (rows // mat_momentum.shape[1])

    grads, errors = in_hbm(grads), in_hbm(errors)
    mat_momentum, mat_weights = map(in_hbm, (mat_momentum, mat_weights))

    front, back = parted(blocks)
    other_front, other_back = combine(place, grads, errors, False, [front, back], blocks)
    arrived_front = in_vmem(exchange(other_front, "core"))
    (own_front,) = combine(place, grads, errors, True, [front], blocks)
    go = fold([[(own_front, i), (arrived_front, i)] for i in range(len(front))])
    ahead = front, 0, exchange(go, "plane", 0)
    later, go, leaves = lax.optimization_barrier((place, go, other_back))
    arrived_back = in_vmem(exchange(leaves, "core"))
    own_back, other_p, own_part = combine(
        later, grads, errors, True, [back], blocks, ((False, (front, back), True), (True, (front,), False)),
        (warm_start, vec_grads, other_front, other_back, own_front),
    )
    own_c, other_c = (own_front, own_back), (other_front, other_back)

    arrived_c = arrived_front, arrived_back
    terms = [[(c[part], at) for c in (own_c, arrived_c)] for part, at in (within(p, blocks) for p in range(blocks))]

    def send(goes, stage, after=()):
        return goes, stage, exchange(fold([terms[p] for p in goes], after), "plane", stage)

    def land(goes, stage, arrived):
        arrived = in_vmem(arrived)
        for i, p in enumerate(goes):
            terms[p ^ (1 << stage)].append((arrived, i))

    rest = [p for p in range(blocks) if p & 3 == 1]
    pending = [send(rest, 0)]

    own_p = own_factor(later, own_back, back, own_part, warm_start, vec_grads, blocks)
    packed = own_p + exchange(other_p, "core")
    land(*ahead)
    goes = [p for p in range(blocks) if p & 3 == 2]
    packed, mm, mw, go = hop(
        packed, "plane", bits - 1,
        lambda *x: [*banks(*x), fold([terms[p] for p in goes])], mat_momentum, mat_weights,
    )
    pending.append((goes, 1, exchange(go, "plane", 1)))
    for stage in range(2, bits):
        while pending:
            land(*pending.pop(0))
        goes = [p for p in range(blocks) if p >> stage & 1 and not p & ((1 << stage) - 1)]
        pending.append(send(goes, stage, (packed,)))
    for step in range(depths):
        packed = hop(packed, "z", step)
    for step in range(bits - 2, 0, -1):
        packed = hop(packed, "plane", step)
    land(*pending.pop(0))
    packed, keep = hop(packed, "plane", 0, lambda *x: [fold([list(zip(x, [at for _, at in terms[0]]))])],
                       *[a for a, _ in terms[0]])
    terms[0] = [(keep, 0)]
    while pending:
        land(*pending.pop(0))

    kept_sum, v = small_call(
        functools.partial(project_kernel, places=[at for _, at in terms[0]], count=count),
        "project", [(rows, width), (rank, width)], packed, *[a for a, _ in terms[0]],
    )
    square = (rank, rank)
    state = (3, rank, rank)
    depth = list(range(1, groups))
    v, first_state = hop(
        v, "depth", depth,
        lambda x: small_call(
            functools.partial(first_begin_kernel, rows=rows, count=count), "root1a", [state], x
        ), packed,
    )
    (u,) = small_call(functools.partial(lift_kernel, count=count), "lift", [(rank * rows // LANES, LANES)], v, kept_sum)
    u, first_root = hop(u, "depth", depth, lambda x: small_call(first_end_kernel, "root1b", [square], x), first_state)
    u, vec_momentum_out, vec_weights_out = hop(
        u, "place", list(range(1, blocks)),
        lambda x, y: gains(place, owners, x, y, vec_momentum, vec_weights, count, head_items),
        packed, exchange(packed, "core"),
    )
    (v,) = small_call(functools.partial(lower_kernel, count=count), "lower", [(rank, width)], u, kept_sum)
    def second(a, u):
        (begun,) = small_call(functools.partial(second_begin_kernel, rows=rows), "root2a", [state], a, u)
        return small_call(
            functools.partial(second_end_kernel, rows=rows), "root2b", [(rank, lanes(rows + rank))], begun, a, u
        )

    v, own_f = hop(v, "depth", depth, second, first_root, u)

    shapes = [errors.shape, mat_momentum.shape, mat_weights.shape]
    swapped = exchange(jnp.concatenate([v, own_f], axis=1), "core")
    other_v, other_f = swapped[None, :, :width], swapped[:, width:]
    v = v[None]
    arrived = [exchange(v, "place", p) for p in range(1, blocks)]
    *outs, left = finish(
        [0], (), (), place, owners, v, other_v, own_f, other_f, own_c, other_c, shapes, mm, mw
    )
    *arrived, left = lax.optimization_barrier((*arrived, left))
    v = jnp.concatenate(arrived, axis=0)
    outs = finish(
        list(range(1, blocks)), (left,), outs, place, owners, v, exchange(v, "core"), own_f, other_f, own_c, other_c,
        shapes, mm, mw,
    )
    new_errors, mat_momentum_out, mat_weights_out = outs
    return (new_errors, mat_momentum_out, mat_weights_out, vec_momentum_out, vec_weights_out)


def solution(mesh):
    both = ("rep", "grp")
    return jax.shard_map(
        local,
        mesh=mesh,
        in_specs=(
            P(both, None, None, None),
            P(both, None, None, None),
            P(),
            P(both, None, None),
            P(),
            P(both, None, None),
            P(both, None, None),
            P(both, None),
            P(both, None),
        ),
        out_specs=(
            P(both, None, None, None),
            P(both, None, None),
            P(both, None, None),
            P(both, None),
            P(both, None),
        ),
        check_vma=False,
    )
```

```python
import functools

import jax
import jax.numpy as jnp
from jax import lax
from jax.experimental import pallas as pl
from jax.experimental.pallas import tpu as pltpu
from jax.sharding import PartitionSpec as P

ROOT_ITERS = 12
LANES = 128
f32 = jnp.float32
NN = ((1,), (0,))
NT = ((1,), (1,))
TN = ((0,), (0,))
ANY = pl.BlockSpec(memory_space=pl.ANY)
VMEM = pl.BlockSpec(memory_space=pltpu.VMEM)
SMEM = pl.BlockSpec(memory_space=pltpu.SMEM)


def dot(a, b, dims=NN):
    return lax.dot_general(
        a, b, (dims, ((), ())), precision=lax.Precision.HIGHEST, preferred_element_type=f32
    )


def split3(a):
    high = a.astype(jnp.bfloat16)
    rest = a - high.astype(f32)
    middle = rest.astype(jnp.bfloat16)
    low = (rest - middle.astype(f32)).astype(jnp.bfloat16)
    return high, middle, low


def lanes(n):
    return -(-n // LANES) * LANES


def pack_factor(out, u):
    rank, rows = u.shape
    whole, left = divmod(rows, LANES)
    for i in range(whole):
        out[i * rank : (i + 1) * rank, :] = u[:, i * LANES : (i + 1) * LANES]
    if left:
        short = rank * left // LANES
        for i in range(LANES // left):
            out[whole * rank : whole * rank + short, i * left : (i + 1) * left] = u[
                i * short : (i + 1) * short, whole * LANES :
            ]


def unpack_factor(x, rank, rows):
    whole, left = divmod(rows, LANES)
    parts = [x[i * rank : (i + 1) * rank, :] for i in range(whole)]
    if left:
        short = rank * left // LANES
        tail = x[whole * rank : whole * rank + short, :]
        parts.append(jnp.concatenate([tail[:, i * left : (i + 1) * left] for i in range(LANES // left)], axis=0))
    return jnp.concatenate(parts, axis=1)


def in_hbm(a):
    return pltpu.with_memory_space_constraint(a, pltpu.HBM)


def in_vmem(a):
    return pltpu.with_memory_space_constraint(a, pltpu.VMEM)


def call(kernel, name, in_specs, out_specs, out_shape, operands, mib=4, flops=1, nbytes=1, scratch=(), aliases={}):
    return pl.pallas_call(
        kernel,
        in_specs=in_specs,
        out_specs=out_specs,
        out_shape=out_shape,
        scratch_shapes=scratch,
        input_output_aliases=aliases,
        compiler_params=pltpu.CompilerParams(vmem_limit_bytes=mib << 20),
        cost_estimate=pl.CostEstimate(flops=flops, bytes_accessed=nbytes, transcendentals=0),
        name=name,
    )(*operands)


def small_call(kernel, name, shapes, *operands):
    return call(
        kernel,
        name,
        [VMEM] * len(operands),
        [VMEM] * len(shapes),
        [jax.ShapeDtypeStruct(s, f32) for s in shapes],
        operands,
        flops=12_000_000,
        nbytes=4 * sum(o.size for o in operands),
    )


def block_columns(place, own, p, blocks, width):
    bits = blocks.bit_length() - 1
    core = place[0] if own else 1 - place[0]
    block = place[1] ^ jnp.where(core == 0, p, mirror(p, bits))
    return pl.ds(pl.multiple_of(block * width, width), width)


def part_of_factor(place, own, w_ref, part, places, blocks):
    _, rows, width = part.shape
    rank = w_ref.shape[1]
    m = place[0] if own else 1 - place[0]
    terms = jnp.zeros((rows, 3 * rank), f32)
    for i, p in enumerate(places):
        w_high, w_middle, w_low = split3(w_ref[m, :, block_columns(place, own, p, blocks, width)])
        high, middle, _ = split3(part[i])
        for piece, pieces in (
            (high, (w_high, w_middle, w_low)),
            (middle, (w_high, w_middle, jnp.zeros_like(w_low))),
        ):
            terms += lax.dot_general(
                piece, jnp.concatenate(pieces, axis=0), (NT, ((), ())), preferred_element_type=f32
            )
    return (terms[:, :rank] + terms[:, rank : 2 * rank] + terms[:, 2 * rank :]).T


def write_factor(out, place, own, factor, vec_ref):
    rank, rows = factor.shape
    pack_factor(out, factor)
    base = rank * rows // LANES
    mine = jnp.where((place[0] if own else 1 - place[0]) == 0, vec_ref[0, 0:1, :], vec_ref[0, 1:2, :])
    for i in range(vec_ref.shape[2] // LANES):
        out[base + i : base + i + 1, :] = mine[:, i * LANES : (i + 1) * LANES]


def factor_shape(rows, warm_start):
    _, rank, cols = warm_start.shape
    return jax.ShapeDtypeStruct(((rank * rows + cols) // LANES, LANES), f32)


def factor_kernel(place, w_ref, vec_ref, part, before, out, *, places, blocks):
    factor = before[...] + part_of_factor(place, True, w_ref, part, places, blocks)
    write_factor(out, place, True, factor, vec_ref)


def own_factor(place, part, places, before, warm_start, vec_grads, blocks):
    return call(
        functools.partial(factor_kernel, places=places, blocks=blocks),
        "factor",
        [SMEM] + [VMEM] * 4,
        VMEM,
        factor_shape(part.shape[1], warm_start),
        (place, warm_start, vec_grads, part, before),
    )


def combine_kernel(place, g_hbm, e_hbm, *refs, own, groups, blocks, sides):
    refs = list(refs)
    if sides:
        w_ref, vec_ref = refs.pop(0), refs.pop(0)
    ins = [[refs.pop(0) for _ in spots] for _, spots, _ in sides]
    outs = [refs.pop(0) for _ in groups]
    factors = [refs.pop(0) for _ in sides]
    g, e, sem = refs
    m = place[0] if own else 1 - place[0]
    loads = []
    for i, p in enumerate(sum(groups, [])):
        where = block_columns(place, own, p, blocks, g.shape[2])
        loads.append(
            (
                pltpu.make_async_copy(g_hbm.at[0, m, :, where], g.at[i], sem.at[i, 0]),
                pltpu.make_async_copy(e_hbm.at[0, m, :, where], e.at[i], sem.at[i, 1]),
            )
        )
        for load in loads[-1]:
            load.start()
    for (whose, spots, whole), parts, factor in zip(sides, ins, factors):
        value = sum(part_of_factor(place, whose, w_ref, part, at, blocks) for part, at in zip(parts, spots))
        if whole:
            write_factor(factor, place, whose, value, vec_ref)
        else:
            factor[...] = value
    i = 0
    for out in outs:
        for at in range(out.shape[0]):
            for load in loads[i]:
                load.wait()
            out[at] = g[i].astype(f32) + e[i]
            i += 1


def combine(place, grads, errors, own, groups, blocks, sides=(), extra=()):
    rows, cols = grads.shape[2:]
    width = cols // blocks
    shape = (sum(map(len, groups)), rows, width)
    shapes = [
        factor_shape(rows, extra[0]) if whole else jax.ShapeDtypeStruct((extra[0].shape[1], rows), f32)
        for _, _, whole in sides
    ]
    return call(
        functools.partial(combine_kernel, own=own, groups=groups, blocks=blocks, sides=sides),
        ("own" if own else "other") + str(len(sides)),
        [SMEM, ANY, ANY] + [VMEM] * len(extra),
        [VMEM] * (len(groups) + len(sides)),
        [pltpu.VMEM((len(group), rows, width), f32) for group in groups] + shapes,
        (place, grads, errors, *extra),
        mib=8,
        scratch=[
            pltpu.VMEM(shape, grads.dtype), pltpu.VMEM(shape, f32), pltpu.SemaphoreType.DMA((shape[0], 2))
        ],
    )


def parted(blocks):
    front = [p for p in range(blocks) if p & 3 == 3]
    return front, [p for p in range(blocks) if p & 3 == 1] + list(range(0, blocks, 2))


def within(p, blocks):
    front, back = parted(blocks)
    return (0, front.index(p)) if p in front else (1, back.index(p))


def fold_kernel(*refs, picks):
    for i, pick in enumerate(picks):
        refs[-1][i] = sum(refs[k][at] for k, at in pick)


def fold(terms, after=()):
    arrays, picks = [], []
    for pairs in terms:
        pick = []
        for a, at in pairs:
            if not any(a is b for b in arrays):
                arrays.append(a)
            pick.append((next(k for k, b in enumerate(arrays) if a is b), at))
        picks.append(pick)
    shape = (len(terms),) + arrays[0].shape[1:]
    return call(
        functools.partial(fold_kernel, picks=picks),
        "fold",
        [VMEM] * len(arrays) + [ANY] * len(after),
        VMEM,
        pltpu.VMEM(shape, f32),
        (*arrays, *after),
        nbytes=4 * len(picks[0]) * shape[0] * shape[1] * shape[2],
    )


def project_kernel(x_ref, *refs, places, count):
    parts, (s_ref, v_ref) = refs[:-2], refs[-2:]
    block = sum(part[at] for part, at in zip(parts, places))
    s_ref[...] = block
    v_ref[...] = dot(unpack_factor(x_ref[...], v_ref.shape[0], block.shape[0]) / count, block) / count


def lift_kernel(v_ref, s_ref, u_ref, *, count):
    pack_factor(u_ref, dot(v_ref[...], s_ref[...], NT) / count)


def lower_kernel(u_ref, s_ref, v_ref, *, count):
    v_ref[...] = dot(unpack_factor(u_ref[...], v_ref.shape[0], s_ref.shape[0]), s_ref[...]) / count


def identity(rank):
    return (
        lax.broadcasted_iota(jnp.int32, (rank, rank), 0)
        == lax.broadcasted_iota(jnp.int32, (rank, rank), 1)
    ).astype(f32)


def sweeps(left, right, first, last):
    eye = identity(left.shape[0])
    for sweep in range(first, last):
        middle = 1.5 * eye - 0.5 * (left if sweep == 0 else dot(right, left))
        right = middle if sweep == 0 else dot(middle, right)
        if sweep + 1 < ROOT_ITERS:
            left = dot(left, middle)
    return left, right


def root_begin(gram, state):
    spread = jnp.sqrt(jnp.sum(gram * gram, keepdims=True))
    left, right = sweeps(gram / spread, None, 0, ROOT_ITERS // 2)
    state[0], state[1] = left, right
    state[2] = jnp.broadcast_to(spread, gram.shape)


def root_end(state):
    _, right = sweeps(state[0], state[1], ROOT_ITERS // 2, ROOT_ITERS)
    return right / jnp.sqrt(state[2])


def first_begin_kernel(x_ref, state, *, rows, count):
    factor = unpack_factor(x_ref[...], state.shape[1], rows) / count
    root_begin(dot(factor, factor, NT), state)


def first_end_kernel(state, a_ref):
    a_ref[...] = root_end(state)


def second_begin_kernel(a_ref, u_ref, state, *, rows):
    a = a_ref[...]
    u = unpack_factor(u_ref[...], a.shape[0], rows)
    root_begin(dot(a, dot(dot(u, u, NT), a), TN), state)


def second_end_kernel(state, a_ref, u_ref, f_ref, *, rows):
    rank = a_ref.shape[0]
    u = unpack_factor(u_ref[...], rank, rows)
    both = dot(a_ref[...], root_end(state))
    f_ref[...] = jnp.zeros(f_ref.shape, f32)
    f_ref[:, :rows] = dot(both, u, TN)
    f_ref[:, rows : rows + rank] = both


def taken_items(place, owners, slots):
    items, before = [jnp.int32(-1)] * slots, jnp.int32(0)
    for item in range(owners.shape[0]):
        mine = owners[item] == place[2]
        items = [jnp.where(mine & (before == slot), item, old) for slot, old in enumerate(items)]
        before = before + jnp.where(mine, 1, 0)
    return items


def gains_kernel(place, owners, own_ref, other_ref, mv_ref, wv_ref, mo_ref, wo_ref, vec, *, count, first):
    for i in range(mv_ref.shape[1] // LANES):
        at = slice(i * LANES, (i + 1) * LANES)
        for k, ref in enumerate((own_ref, other_ref)):
            row = ref.shape[0] - mv_ref.shape[1] // LANES + i
            vec[k : k + 1, at] = ref[row : row + 1, :] / count
    for slot, item in enumerate(taken_items(place, owners, mv_ref.shape[0])):
        row = jnp.where(item - first == place[0], vec[0:1, :], vec[1:2, :])
        old, weight = mv_ref[slot : slot + 1, :], wv_ref[slot : slot + 1, :]
        new = 0.9 * old + row
        mo_ref[slot : slot + 1, :] = jnp.where(item >= first, new, old)
        wo_ref[slot : slot + 1, :] = jnp.where(item >= first, weight - 0.5 * new, weight)


def gains(place, owners, own, other, vec_momentum, vec_weights, count, first):
    return call(
        functools.partial(gains_kernel, count=count, first=first),
        "gains",
        [SMEM, SMEM] + [VMEM] * 4,
        [VMEM] * 2,
        [jax.ShapeDtypeStruct(vec_momentum.shape, f32)] * 2,
        (place, owners, own, other, vec_momentum, vec_weights),
        flops=10 * vec_momentum.size,
        nbytes=16 * vec_momentum.size,
        scratch=[pltpu.VMEM((2, vec_momentum.shape[1]), f32)],
    )


def banks_kernel(mm_hbm, mw_hbm, mm, mw, sem):
    loads = (pltpu.make_async_copy(mm_hbm, mm, sem.at[0]), pltpu.make_async_copy(mw_hbm, mw, sem.at[1]))
    for load in loads:
        load.start()
    for load in loads:
        load.wait()


def banks(mat_momentum, mat_weights):
    return call(
        banks_kernel,
        "banks",
        [ANY, ANY],
        [VMEM] * 2,
        [pltpu.VMEM(mat_momentum.shape, f32)] * 2,
        (mat_momentum, mat_weights),
        nbytes=8 * mat_momentum.size,
        scratch=[pltpu.SemaphoreType.DMA((2,))],
    )


def finish_kernel(
    place, owners, v0_ref, v1_ref, f0_ref, f1_ref, c0_front, c0_back, c1_front, c1_back, mm, mw, *refs, positions, head, later
):
    if later:
        left, refs = refs[0], refs[1 + 3 :]
        n_hbm, mo_hbm, wo_hbm, errors, approx, moment, weight, sem, bank_sem = refs
    else:
        n_hbm, mo_hbm, wo_hbm, left, errors, approx, moment, weight, sem, bank_sem = refs
    rank, width = v0_ref.shape[1:]
    blocks, rows = c0_front.shape[0] + c0_back.shape[0], c0_front.shape[1]
    per = rows // head
    if not later:
        for i, f_ref in enumerate((f0_ref, f1_ref)):
            high, middle, low = split3(f_ref[:, :rows].T)
            left[i] = jnp.concatenate([high, high, middle, high, low, middle], axis=1)
    units = [(k, p, i) for k, p in enumerate(positions) for i in range(2)]
    rights = []
    for k, p, i in units:
        f_ref, v_ref = ((f0_ref, v0_ref), (f1_ref, v1_ref))[i]
        high, middle, low = split3(dot(f_ref[:, rows : rows + rank], v_ref[k], TN))
        rights.append(jnp.concatenate([high, middle, high, low, high, middle], axis=0))
    stores = []
    for (k, p, i), right in zip(units, rights):
        m = place[0] if i == 0 else 1 - place[0]
        product = jnp.dot(left[i], right, preferred_element_type=f32)
        approx[k, i] = product
        part, at = within(p, blocks)
        errors[k, i] = ((c0_front, c0_back), (c1_front, c1_back))[i][part][at] - product
        columns = block_columns(place, i == 0, p, blocks, width)
        stores.append(pltpu.make_async_copy(errors.at[k, i], n_hbm.at[0, m, :, columns], sem.at[k, i]))
        stores[-1].start()
    bank_stores = []
    items = taken_items(place, owners, mm.shape[0])
    for k, p, i in units:
        m = place[0] if i == 0 else 1 - place[0]
        columns = block_columns(place, i == 0, p, blocks, width)
        for slot, item in enumerate(items):
            taken = (item >= m * per) & (item < (m + 1) * per)
            idle = (item < 0) | (item >= 2 * per)
            copies = (
                pltpu.make_async_copy(
                    moment.at[k, i, slot], mo_hbm.at[slot, :, columns], bank_sem.at[k, i, slot, 0]
                ),
                pltpu.make_async_copy(
                    weight.at[k, i, slot], wo_hbm.at[slot, :, columns], bank_sem.at[k, i, slot, 1]
                ),
            )

            @pl.when(taken)
            def _():
                at = pl.ds(pl.multiple_of((item - m * per) * head, head), head)
                new = 0.9 * mm[slot, :, columns] + approx[k, i, at, :]
                moment[k, i, slot] = new
                weight[k, i, slot] = mw[slot, :, columns] - 0.5 * new
                for copy in copies:
                    copy.start()

            writes = taken
            if i == 0:
                writes = taken | idle

                @pl.when(idle)
                def _():
                    moment[k, i, slot] = mm[slot, :, columns]
                    weight[k, i, slot] = mw[slot, :, columns]
                    for copy in copies:
                        copy.start()

            bank_stores.append((writes, copies))
    for store in stores:
        store.wait()
    for writes, copies in bank_stores:

        @pl.when(writes)
        def _():
            for copy in copies:
                copy.wait()


def finish(positions, left, outs, place, owners, own_v, other_v, own_f, other_f, own_c, other_c, shapes, mm, mw):
    n, rank, width = own_v.shape
    matrices, rows, cols = shapes[0][1:]
    slots, head = mm.shape[:2]
    later = len(outs) > 0
    inputs = 12 + len(left)
    first = [] if later else [pltpu.VMEM((2, rows, 6 * rank), jnp.bfloat16)]
    return call(
        functools.partial(finish_kernel, positions=positions, head=head, later=later),
        f"finish{positions[0]}",
        [SMEM, SMEM] + [VMEM] * (10 + len(left)) + [ANY] * len(outs),
        [ANY] * 3 + [VMEM] * len(first),
        [pltpu.HBM(s, f32) for s in shapes] + first,
        (place, owners, own_v, other_v, own_f, other_f, *own_c, *other_c, mm, mw, *left, *outs),
        mib=4 + 5 * n,
        flops=2 * n * matrices * rows * width * 6 * rank,
        nbytes=4 * n * width * (matrices * rows + 4 * slots * head),
        scratch=[
            pltpu.VMEM((n, 2, rows, width), f32),
            pltpu.VMEM((n, 2, rows, width), f32),
            pltpu.VMEM((n, 2, slots, head, width), f32),
            pltpu.VMEM((n, 2, slots, head, width), f32),
            pltpu.SemaphoreType.DMA((n, 2)),
            pltpu.SemaphoreType.DMA((n, 2, slots, 2)),
        ],
        aliases={inputs + i: i for i in range(len(outs))},
    )


def mirror(p, bits):
    return sum((p >> i & 1) << (bits - 1 - i) for i in range(bits))


def partner(kind, step):
    planes = (lax.axis_size("rep") // 2).bit_length() - 1
    depths = lax.axis_size("grp").bit_length() - 1

    def of(rep, grp):
        if kind == "core":
            return rep ^ 1, grp
        if kind == "plane":
            return rep ^ (2 << (step if rep % 2 == 0 else planes - 1 - step)), grp
        if kind == "depth":
            return rep, grp ^ step
        if kind == "place":
            return rep ^ 2 * (step if rep % 2 == 0 else mirror(step, planes)), grp
        return rep, grp ^ (1 << (step if rep % 2 == 0 else depths - 1 - step))

    return of


def rounds(places):
    return [1, *range(places - 1, 1, -1)]


def exchange(a, kind, step=0):
    groups = lax.axis_size("grp")
    of = partner(kind, step)
    pairs = []
    for rep in range(lax.axis_size("rep")):
        for grp in range(groups):
            to_rep, to_grp = of(rep, grp)
            pairs.append((rep * groups + grp, to_rep * groups + to_grp))
    return lax.ppermute(a, ("rep", "grp"), pairs)


def hop(a, kind, step, work=None, *operands):
    if work is None:
        return a + exchange(a, kind, step)
    a, *operands = lax.optimization_barrier((a, *operands))
    steps = step if isinstance(step, list) else [step]
    arrived = [exchange(a, kind, each) for each in steps]
    done = work(*operands)
    arrived, done = lax.optimization_barrier((arrived, list(done)))
    return sum(arrived, a), *done


def local(grads, errors, warm_start, vec_grads, owners, mat_momentum, mat_weights, vec_momentum, vec_weights):
    reps, groups = lax.axis_size("rep"), lax.axis_size("grp")
    count = float(reps * groups)
    blocks = reps // 2
    bits = blocks.bit_length() - 1
    depths = groups.bit_length() - 1
    matrices, rows, cols = grads.shape[1:]
    rank = warm_start.shape[1]
    width = cols // blocks
    rep = lax.axis_index("rep")
    core, spot = rep % 2, rep // 2
    place = jnp.stack([core, spot, rep * groups + lax.axis_index("grp")]).astype(jnp.int32)
    head_items = matrices * (rows // mat_momentum.shape[1])

    grads, errors = in_hbm(grads), in_hbm(errors)
    mat_momentum, mat_weights = map(in_hbm, (mat_momentum, mat_weights))

    front, back = parted(blocks)
    other_front, other_back = combine(place, grads, errors, False, [front, back], blocks)
    arrived_front = in_vmem(exchange(other_front, "core"))
    (own_front,) = combine(place, grads, errors, True, [front], blocks)
    go = fold([[(own_front, i), (arrived_front, i)] for i in range(len(front))])
    ahead = front, 0, exchange(go, "plane", 0)
    later, go, leaves = lax.optimization_barrier((place, go, other_back))
    arrived_back = in_vmem(exchange(leaves, "core"))
    own_back, other_p, own_part = combine(
        later, grads, errors, True, [back], blocks, ((False, (front, back), True), (True, (front,), False)),
        (warm_start, vec_grads, other_front, other_back, own_front),
    )
    own_c, other_c = (own_front, own_back), (other_front, other_back)

    arrived_c = arrived_front, arrived_back
    terms = [[(c[part], at) for c in (own_c, arrived_c)] for part, at in (within(p, blocks) for p in range(blocks))]

    def send(goes, stage, after=()):
        return goes, stage, exchange(fold([terms[p] for p in goes], after), "plane", stage)

    def land(goes, stage, arrived):
        arrived = in_vmem(arrived)
        for i, p in enumerate(goes):
            terms[p ^ (1 << stage)].append((arrived, i))

    rest = [p for p in range(blocks) if p & 3 == 1]
    pending = [send(rest, 0)]

    own_p = own_factor(later, own_back, back, own_part, warm_start, vec_grads, blocks)
    packed = own_p + exchange(other_p, "core")
    land(*ahead)
    goes = [p for p in range(blocks) if p & 3 == 2]
    packed, mm, mw, go = hop(
        packed, "plane", bits - 1,
        lambda *x: [*banks(*x), fold([terms[p] for p in goes])], mat_momentum, mat_weights,
    )
    pending.append((goes, 1, exchange(go, "plane", 1)))
    for stage in range(2, bits):
        while pending:
            land(*pending.pop(0))
        goes = [p for p in range(blocks) if p >> stage & 1 and not p & ((1 << stage) - 1)]
        pending.append(send(goes, stage, (packed,)))
    packed = packed + sum(exchange(packed, "depth", step) for step in rounds(groups))
    for step in range(bits - 2, 0, -1):
        packed = hop(packed, "plane", step)
    land(*pending.pop(0))
    packed, keep = hop(packed, "plane", 0, lambda *x: [fold([list(zip(x, [at for _, at in terms[0]]))])],
                       *[a for a, _ in terms[0]])
    terms[0] = [(keep, 0)]
    while pending:
        land(*pending.pop(0))

    kept_sum, v = small_call(
        functools.partial(project_kernel, places=[at for _, at in terms[0]], count=count),
        "project", [(rows, width), (rank, width)], packed, *[a for a, _ in terms[0]],
    )
    square = (rank, rank)
    state = (3, rank, rank)
    depth = rounds(groups)
    v, first_state = hop(
        v, "depth", depth,
        lambda x: small_call(
            functools.partial(first_begin_kernel, rows=rows, count=count), "root1a", [state], x
        ), packed,
    )
    (u,) = small_call(functools.partial(lift_kernel, count=count), "lift", [(rank * rows // LANES, LANES)], v, kept_sum)
    u, first_root = hop(u, "depth", depth, lambda x: small_call(first_end_kernel, "root1b", [square], x), first_state)
    u, vec_momentum_out, vec_weights_out = hop(
        u, "place", rounds(blocks),
        lambda x, y: gains(place, owners, x, y, vec_momentum, vec_weights, count, head_items),
        packed, exchange(packed, "core"),
    )
    (v,) = small_call(functools.partial(lower_kernel, count=count), "lower", [(rank, width)], u, kept_sum)
    def second(a, u):
        (begun,) = small_call(functools.partial(second_begin_kernel, rows=rows), "root2a", [state], a, u)
        return small_call(
            functools.partial(second_end_kernel, rows=rows), "root2b", [(rank, lanes(rows + rank))], begun, a, u
        )

    v, own_f = hop(v, "depth", depth, second, first_root, u)

    shapes = [errors.shape, mat_momentum.shape, mat_weights.shape]
    swapped = exchange(jnp.concatenate([v, own_f], axis=1), "core")
    other_v, other_f = swapped[None, :, :width], swapped[:, width:]
    v = v[None]
    arrived = {p: exchange(v, "place", p) for p in rounds(blocks)}
    arrived = [arrived[p] for p in range(1, blocks)]
    *outs, left = finish(
        [0], (), (), place, owners, v, other_v, own_f, other_f, own_c, other_c, shapes, mm, mw
    )
    *arrived, left = lax.optimization_barrier((*arrived, left))
    v = jnp.concatenate(arrived, axis=0)
    outs = finish(
        list(range(1, blocks)), (left,), outs, place, owners, v, exchange(v, "core"), own_f, other_f, own_c, other_c,
        shapes, mm, mw,
    )
    new_errors, mat_momentum_out, mat_weights_out = outs
    return (new_errors, mat_momentum_out, mat_weights_out, vec_momentum_out, vec_weights_out)


def solution(mesh):
    both = ("rep", "grp")
    return jax.shard_map(
        local,
        mesh=mesh,
        in_specs=(
            P(both, None, None, None),
            P(both, None, None, None),
            P(),
            P(both, None, None),
            P(),
            P(both, None, None),
            P(both, None, None),
            P(both, None),
            P(both, None),
        ),
        out_specs=(
            P(both, None, None, None),
            P(both, None, None),
            P(both, None, None),
            P(both, None),
            P(both, None),
        ),
        check_vma=False,
    )
```

```python
import functools

import jax
import jax.numpy as jnp
from jax import lax
from jax.experimental import pallas as pl
from jax.experimental.pallas import tpu as pltpu
from jax.sharding import PartitionSpec as P

ROOT_ITERS = 12
LANES = 128
f32 = jnp.float32
NN = ((1,), (0,))
NT = ((1,), (1,))
TN = ((0,), (0,))
ANY = pl.BlockSpec(memory_space=pl.ANY)
VMEM = pl.BlockSpec(memory_space=pltpu.VMEM)
SMEM = pl.BlockSpec(memory_space=pltpu.SMEM)


def dot(a, b, dims=NN):
    return lax.dot_general(
        a, b, (dims, ((), ())), precision=lax.Precision.HIGHEST, preferred_element_type=f32
    )


def split3(a):
    high = a.astype(jnp.bfloat16)
    rest = a - high.astype(f32)
    middle = rest.astype(jnp.bfloat16)
    low = (rest - middle.astype(f32)).astype(jnp.bfloat16)
    return high, middle, low


def lanes(n):
    return -(-n // LANES) * LANES


def pack_factor(out, u):
    rank, rows = u.shape
    whole, left = divmod(rows, LANES)
    for i in range(whole):
        out[i * rank : (i + 1) * rank, :] = u[:, i * LANES : (i + 1) * LANES]
    if left:
        short = rank * left // LANES
        for i in range(LANES // left):
            out[whole * rank : whole * rank + short, i * left : (i + 1) * left] = u[
                i * short : (i + 1) * short, whole * LANES :
            ]


def unpack_factor(x, rank, rows):
    whole, left = divmod(rows, LANES)
    parts = [x[i * rank : (i + 1) * rank, :] for i in range(whole)]
    if left:
        short = rank * left // LANES
        tail = x[whole * rank : whole * rank + short, :]
        parts.append(jnp.concatenate([tail[:, i * left : (i + 1) * left] for i in range(LANES // left)], axis=0))
    return jnp.concatenate(parts, axis=1)


def in_hbm(a):
    return pltpu.with_memory_space_constraint(a, pltpu.HBM)


def in_vmem(a):
    return pltpu.with_memory_space_constraint(a, pltpu.VMEM)


def call(kernel, name, in_specs, out_specs, out_shape, operands, mib=4, flops=1, nbytes=1, scratch=(), aliases={}):
    return pl.pallas_call(
        kernel,
        in_specs=in_specs,
        out_specs=out_specs,
        out_shape=out_shape,
        scratch_shapes=scratch,
        input_output_aliases=aliases,
        compiler_params=pltpu.CompilerParams(vmem_limit_bytes=mib << 20),
        cost_estimate=pl.CostEstimate(flops=flops, bytes_accessed=nbytes, transcendentals=0),
        name=name,
    )(*operands)


def small_call(kernel, name, shapes, *operands):
    return call(
        kernel,
        name,
        [VMEM] * len(operands),
        [VMEM] * len(shapes),
        [jax.ShapeDtypeStruct(s, f32) for s in shapes],
        operands,
        flops=12_000_000,
        nbytes=4 * sum(o.size for o in operands),
    )


def block_columns(place, own, p, blocks, width):
    bits = blocks.bit_length() - 1
    core = place[0] if own else 1 - place[0]
    block = place[1] ^ jnp.where(core == 0, p, mirror(p, bits))
    return pl.ds(pl.multiple_of(block * width, width), width)


def part_of_factor(place, own, w_ref, part, places, blocks):
    _, rows, width = part.shape
    rank = w_ref.shape[1]
    m = place[0] if own else 1 - place[0]
    terms = jnp.zeros((rows, 3 * rank), f32)
    for i, p in enumerate(places):
        w_high, w_middle, w_low = split3(w_ref[m, :, block_columns(place, own, p, blocks, width)])
        high, middle, _ = split3(part[i])
        for piece, pieces in (
            (high, (w_high, w_middle, w_low)),
            (middle, (w_high, w_middle, jnp.zeros_like(w_low))),
        ):
            terms += lax.dot_general(
                piece, jnp.concatenate(pieces, axis=0), (NT, ((), ())), preferred_element_type=f32
            )
    return (terms[:, :rank] + terms[:, rank : 2 * rank] + terms[:, 2 * rank :]).T


def write_factor(out, place, own, factor, vec_ref):
    rank, rows = factor.shape
    pack_factor(out, factor)
    base = rank * rows // LANES
    mine = jnp.where((place[0] if own else 1 - place[0]) == 0, vec_ref[0, 0:1, :], vec_ref[0, 1:2, :])
    for i in range(vec_ref.shape[2] // LANES):
        out[base + i : base + i + 1, :] = mine[:, i * LANES : (i + 1) * LANES]


def factor_shape(rows, warm_start):
    _, rank, cols = warm_start.shape
    return jax.ShapeDtypeStruct(((rank * rows + cols) // LANES, LANES), f32)


def factor_kernel(place, w_ref, vec_ref, part, before, out, *, places, blocks):
    factor = before[...] + part_of_factor(place, True, w_ref, part, places, blocks)
    write_factor(out, place, True, factor, vec_ref)


def own_factor(place, part, places, before, warm_start, vec_grads, blocks):
    return call(
        functools.partial(factor_kernel, places=places, blocks=blocks),
        "factor",
        [SMEM] + [VMEM] * 4,
        VMEM,
        factor_shape(part.shape[1], warm_start),
        (place, warm_start, vec_grads, part, before),
    )


def combine_kernel(place, g_hbm, e_hbm, *refs, own, groups, blocks, sides):
    refs = list(refs)
    if sides:
        w_ref, vec_ref = refs.pop(0), refs.pop(0)
    ins = [[refs.pop(0) for _ in spots] for _, spots, _ in sides]
    outs = [refs.pop(0) for _ in groups]
    factors = [refs.pop(0) for _ in sides]
    g, e, sem = refs
    m = place[0] if own else 1 - place[0]
    loads = []
    for i, p in enumerate(sum(groups, [])):
        where = block_columns(place, own, p, blocks, g.shape[2])
        loads.append(
            (
                pltpu.make_async_copy(g_hbm.at[0, m, :, where], g.at[i], sem.at[i, 0]),
                pltpu.make_async_copy(e_hbm.at[0, m, :, where], e.at[i], sem.at[i, 1]),
            )
        )
        for load in loads[-1]:
            load.start()
    for (whose, spots, whole), parts, factor in zip(sides, ins, factors):
        value = sum(part_of_factor(place, whose, w_ref, part, at, blocks) for part, at in zip(parts, spots))
        if whole:
            write_factor(factor, place, whose, value, vec_ref)
        else:
            factor[...] = value
    i = 0
    for out in outs:
        for at in range(out.shape[0]):
            for load in loads[i]:
                load.wait()
            out[at] = g[i].astype(f32) + e[i]
            i += 1


def combine(place, grads, errors, own, groups, blocks, sides=(), extra=()):
    rows, cols = grads.shape[2:]
    width = cols // blocks
    shape = (sum(map(len, groups)), rows, width)
    shapes = [
        factor_shape(rows, extra[0]) if whole else jax.ShapeDtypeStruct((extra[0].shape[1], rows), f32)
        for _, _, whole in sides
    ]
    return call(
        functools.partial(combine_kernel, own=own, groups=groups, blocks=blocks, sides=sides),
        ("own" if own else "other") + str(len(sides)),
        [SMEM, ANY, ANY] + [VMEM] * len(extra),
        [VMEM] * (len(groups) + len(sides)),
        [pltpu.VMEM((len(group), rows, width), f32) for group in groups] + shapes,
        (place, grads, errors, *extra),
        mib=8,
        scratch=[
            pltpu.VMEM(shape, grads.dtype), pltpu.VMEM(shape, f32), pltpu.SemaphoreType.DMA((shape[0], 2))
        ],
    )


def parted(blocks):
    front = [p for p in range(blocks) if p & 3 == 3]
    return front, [p for p in range(blocks) if p & 3 == 1] + list(range(0, blocks, 2))


def within(p, blocks):
    front, back = parted(blocks)
    return (0, front.index(p)) if p in front else (1, back.index(p))


def fold_kernel(*refs, picks):
    for i, pick in enumerate(picks):
        refs[-1][i] = sum(refs[k][at] for k, at in pick)


def fold(terms, after=()):
    arrays, picks = [], []
    for pairs in terms:
        pick = []
        for a, at in pairs:
            if not any(a is b for b in arrays):
                arrays.append(a)
            pick.append((next(k for k, b in enumerate(arrays) if a is b), at))
        picks.append(pick)
    shape = (len(terms),) + arrays[0].shape[1:]
    return call(
        functools.partial(fold_kernel, picks=picks),
        "fold",
        [VMEM] * len(arrays) + [ANY] * len(after),
        VMEM,
        pltpu.VMEM(shape, f32),
        (*arrays, *after),
        nbytes=4 * len(picks[0]) * shape[0] * shape[1] * shape[2],
    )


def project_kernel(x_ref, *refs, places, count):
    parts, (s_ref, v_ref) = refs[:-2], refs[-2:]
    block = sum(part[at] for part, at in zip(parts, places))
    s_ref[...] = block
    v_ref[...] = dot(unpack_factor(x_ref[...], v_ref.shape[0], block.shape[0]) / count, block) / count


def lift_kernel(v_ref, s_ref, u_ref, *, count):
    pack_factor(u_ref, dot(v_ref[...], s_ref[...], NT) / count)


def lower_kernel(u_ref, s_ref, v_ref, *, count):
    v_ref[...] = dot(unpack_factor(u_ref[...], v_ref.shape[0], s_ref.shape[0]), s_ref[...]) / count


def identity(rank):
    return (
        lax.broadcasted_iota(jnp.int32, (rank, rank), 0)
        == lax.broadcasted_iota(jnp.int32, (rank, rank), 1)
    ).astype(f32)


def sweeps(left, right, first, last):
    eye = identity(left.shape[0])
    for sweep in range(first, last):
        middle = 1.5 * eye - 0.5 * (left if sweep == 0 else dot(right, left))
        right = middle if sweep == 0 else dot(middle, right)
        if sweep + 1 < ROOT_ITERS:
            left = dot(left, middle)
    return left, right


def root_begin(gram, state):
    spread = jnp.sqrt(jnp.sum(gram * gram, keepdims=True))
    left, right = sweeps(gram / spread, None, 0, ROOT_ITERS // 2)
    state[0], state[1] = left, right
    state[2] = jnp.broadcast_to(spread, gram.shape)


def root_end(state):
    _, right = sweeps(state[0], state[1], ROOT_ITERS // 2, ROOT_ITERS)
    return right / jnp.sqrt(state[2])


def first_begin_kernel(x_ref, state, *, rows, count):
    factor = unpack_factor(x_ref[...], state.shape[1], rows) / count
    root_begin(dot(factor, factor, NT), state)


def first_end_kernel(state, a_ref):
    a_ref[...] = root_end(state)


def second_begin_kernel(a_ref, u_ref, state, *, rows):
    a = a_ref[...]
    u = unpack_factor(u_ref[...], a.shape[0], rows)
    root_begin(dot(a, dot(dot(u, u, NT), a), TN), state)


def second_end_kernel(state, a_ref, u_ref, f_ref, *, rows):
    rank = a_ref.shape[0]
    u = unpack_factor(u_ref[...], rank, rows)
    both = dot(a_ref[...], root_end(state))
    f_ref[...] = jnp.zeros(f_ref.shape, f32)
    f_ref[:, :rows] = dot(both, u, TN)
    f_ref[:, rows : rows + rank] = both


def taken_items(place, owners, slots):
    items, before = [jnp.int32(-1)] * slots, jnp.int32(0)
    for item in range(owners.shape[0]):
        mine = owners[item] == place[2]
        items = [jnp.where(mine & (before == slot), item, old) for slot, old in enumerate(items)]
        before = before + jnp.where(mine, 1, 0)
    return items


def gains_kernel(place, owners, own_ref, other_ref, mv_ref, wv_ref, mo_ref, wo_ref, vec, *, count, first):
    for i in range(mv_ref.shape[1] // LANES):
        at = slice(i * LANES, (i + 1) * LANES)
        for k, ref in enumerate((own_ref, other_ref)):
            row = ref.shape[0] - mv_ref.shape[1] // LANES + i
            vec[k : k + 1, at] = ref[row : row + 1, :] / count
    for slot, item in enumerate(taken_items(place, owners, mv_ref.shape[0])):
        row = jnp.where(item - first == place[0], vec[0:1, :], vec[1:2, :])
        old, weight = mv_ref[slot : slot + 1, :], wv_ref[slot : slot + 1, :]
        new = 0.9 * old + row
        mo_ref[slot : slot + 1, :] = jnp.where(item >= first, new, old)
        wo_ref[slot : slot + 1, :] = jnp.where(item >= first, weight - 0.5 * new, weight)


def gains(place, owners, own, other, vec_momentum, vec_weights, count, first):
    return call(
        functools.partial(gains_kernel, count=count, first=first),
        "gains",
        [SMEM, SMEM] + [VMEM] * 4,
        [VMEM] * 2,
        [jax.ShapeDtypeStruct(vec_momentum.shape, f32)] * 2,
        (place, owners, own, other, vec_momentum, vec_weights),
        flops=10 * vec_momentum.size,
        nbytes=16 * vec_momentum.size,
        scratch=[pltpu.VMEM((2, vec_momentum.shape[1]), f32)],
    )


def banks_kernel(mm_hbm, mw_hbm, mm, mw, sem):
    loads = (pltpu.make_async_copy(mm_hbm, mm, sem.at[0]), pltpu.make_async_copy(mw_hbm, mw, sem.at[1]))
    for load in loads:
        load.start()
    for load in loads:
        load.wait()


def banks(mat_momentum, mat_weights):
    return call(
        banks_kernel,
        "banks",
        [ANY, ANY],
        [VMEM] * 2,
        [pltpu.VMEM(mat_momentum.shape, f32)] * 2,
        (mat_momentum, mat_weights),
        nbytes=8 * mat_momentum.size,
        scratch=[pltpu.SemaphoreType.DMA((2,))],
    )


def turned(f_ref, v, rows):
    rank = v.shape[0]
    high, middle, low = split3(dot(f_ref[:, rows : rows + rank], v, TN))
    return jnp.concatenate([high, middle, high, low, high, middle], axis=0)


def ready_kernel(v_ref, f_ref, c_front, c_back, left, errors, approx, *, positions, blocks):
    rows = errors.shape[1]
    rights = [turned(f_ref, v_ref[k], rows) for k in range(len(positions))]
    for k, p in enumerate(positions):
        product = jnp.dot(left[0], rights[k], preferred_element_type=f32)
        part, at = within(p, blocks)
        approx[k] = product
        errors[k] = (c_front, c_back)[part][at] - product


def ready(positions, v, f, own_c, left, blocks):
    _, rows, width = own_c[0].shape
    shape = (len(positions), rows, width)
    return call(
        functools.partial(ready_kernel, positions=positions, blocks=blocks),
        "ready",
        [VMEM] * 5,
        [VMEM] * 2,
        [pltpu.VMEM(shape, f32)] * 2,
        (v, f, *own_c, left),
        mib=8,
    )


def finish_kernel(
    place, owners, v0_ref, v1_ref, f0_ref, f1_ref, c0_front, c0_back, c1_front, c1_back, mm, mw, *refs, positions, head, later
):
    if later:
        left, own_errors, own_approx, refs = refs[0], refs[1], refs[2], refs[3 + 3 :]
        n_hbm, mo_hbm, wo_hbm, errors, approx, moment, weight, sem, bank_sem = refs
    else:
        n_hbm, mo_hbm, wo_hbm, left, errors, approx, moment, weight, sem, bank_sem = refs
    rank, width = v0_ref.shape[1:]
    blocks, rows = c0_front.shape[0] + c0_back.shape[0], c0_front.shape[1]
    per = rows // head
    if not later:
        for i, f_ref in enumerate((f0_ref, f1_ref)):
            high, middle, low = split3(f_ref[:, :rows].T)
            left[i] = jnp.concatenate([high, high, middle, high, low, middle], axis=1)
    made = [(k, p, 0) for k, p in enumerate(positions)] if later else []
    units = [(k, p, i) for k, p in enumerate(positions) for i in range(2) if (k, p, i) not in made]
    items = taken_items(place, owners, mm.shape[0])
    stores, bank_stores = [], []

    def store(k, p, i, source):
        m = place[0] if i == 0 else 1 - place[0]
        columns = block_columns(place, i == 0, p, blocks, width)
        stores.append(pltpu.make_async_copy(source, n_hbm.at[0, m, :, columns], sem.at[k, i]))
        stores[-1].start()

    def step(k, p, i, source):
        m = place[0] if i == 0 else 1 - place[0]
        columns = block_columns(place, i == 0, p, blocks, width)
        for slot, item in enumerate(items):
            taken = (item >= m * per) & (item < (m + 1) * per)
            idle = (item < 0) | (item >= 2 * per)
            copies = (
                pltpu.make_async_copy(
                    moment.at[k, i, slot], mo_hbm.at[slot, :, columns], bank_sem.at[k, i, slot, 0]
                ),
                pltpu.make_async_copy(
                    weight.at[k, i, slot], wo_hbm.at[slot, :, columns], bank_sem.at[k, i, slot, 1]
                ),
            )

            @pl.when(taken)
            def _():
                at = pl.ds(pl.multiple_of((item - m * per) * head, head), head)
                new = 0.9 * mm[slot, :, columns] + source[at, :]
                moment[k, i, slot] = new
                weight[k, i, slot] = mw[slot, :, columns] - 0.5 * new
                for copy in copies:
                    copy.start()

            writes = taken
            if i == 0:
                writes = taken | idle

                @pl.when(idle)
                def _():
                    moment[k, i, slot] = mm[slot, :, columns]
                    weight[k, i, slot] = mw[slot, :, columns]
                    for copy in copies:
                        copy.start()

            bank_stores.append((writes, copies))

    for k, p, i in made:
        store(k, p, i, own_errors.at[k])
        step(k, p, i, own_approx.at[k])
    rights = [turned((f0_ref, f1_ref)[i], (v0_ref, v1_ref)[i][k], rows) for k, p, i in units]
    for (k, p, i), right in zip(units, rights):
        product = jnp.dot(left[i], right, preferred_element_type=f32)
        part, at = within(p, blocks)
        approx[k, i] = product
        errors[k, i] = ((c0_front, c0_back), (c1_front, c1_back))[i][part][at] - product
        store(k, p, i, errors.at[k, i])
    for k, p, i in units:
        step(k, p, i, approx.at[k, i])
    for copy in stores:
        copy.wait()
    for writes, copies in bank_stores:

        @pl.when(writes)
        def _():
            for copy in copies:
                copy.wait()


def finish(positions, left, outs, place, owners, own_v, other_v, own_f, other_f, own_c, other_c, shapes, mm, mw):
    n, rank, width = own_v.shape
    matrices, rows, cols = shapes[0][1:]
    slots, head = mm.shape[:2]
    later = len(outs) > 0
    inputs = 12 + len(left)
    first = [] if later else [pltpu.VMEM((2, rows, 6 * rank), jnp.bfloat16)]
    return call(
        functools.partial(finish_kernel, positions=positions, head=head, later=later),
        f"finish{positions[0]}",
        [SMEM, SMEM] + [VMEM] * (10 + len(left)) + [ANY] * len(outs),
        [ANY] * 3 + [VMEM] * len(first),
        [pltpu.HBM(s, f32) for s in shapes] + first,
        (place, owners, own_v, other_v, own_f, other_f, *own_c, *other_c, mm, mw, *left, *outs),
        mib=4 + 5 * n,
        flops=2 * n * matrices * rows * width * 6 * rank,
        nbytes=4 * n * width * (matrices * rows + 4 * slots * head),
        scratch=[
            pltpu.VMEM((n, 2, rows, width), f32),
            pltpu.VMEM((n, 2, rows, width), f32),
            pltpu.VMEM((n, 2, slots, head, width), f32),
            pltpu.VMEM((n, 2, slots, head, width), f32),
            pltpu.SemaphoreType.DMA((n, 2)),
            pltpu.SemaphoreType.DMA((n, 2, slots, 2)),
        ],
        aliases={inputs + i: i for i in range(len(outs))},
    )


def mirror(p, bits):
    return sum((p >> i & 1) << (bits - 1 - i) for i in range(bits))


def partner(kind, step):
    planes = (lax.axis_size("rep") // 2).bit_length() - 1
    depths = lax.axis_size("grp").bit_length() - 1

    def of(rep, grp):
        if kind == "core":
            return rep ^ 1, grp
        if kind == "plane":
            return rep ^ (2 << (step if rep % 2 == 0 else planes - 1 - step)), grp
        if kind == "depth":
            return rep, grp ^ step
        if kind == "place":
            return rep ^ 2 * (step if rep % 2 == 0 else mirror(step, planes)), grp
        return rep, grp ^ (1 << (step if rep % 2 == 0 else depths - 1 - step))

    return of


def rounds(places):
    return [1, *range(places - 1, 1, -1)]


def exchange(a, kind, step=0):
    groups = lax.axis_size("grp")
    of = partner(kind, step)
    pairs = []
    for rep in range(lax.axis_size("rep")):
        for grp in range(groups):
            to_rep, to_grp = of(rep, grp)
            pairs.append((rep * groups + grp, to_rep * groups + to_grp))
    return lax.ppermute(a, ("rep", "grp"), pairs)


def hop(a, kind, step, work=None, *operands):
    if work is None:
        return a + exchange(a, kind, step)
    a, *operands = lax.optimization_barrier((a, *operands))
    steps = step if isinstance(step, list) else [step]
    arrived = [exchange(a, kind, each) for each in steps]
    done = work(*operands)
    arrived, done = lax.optimization_barrier((arrived, list(done)))
    return sum(arrived, a), *done


def local(grads, errors, warm_start, vec_grads, owners, mat_momentum, mat_weights, vec_momentum, vec_weights):
    reps, groups = lax.axis_size("rep"), lax.axis_size("grp")
    count = float(reps * groups)
    blocks = reps // 2
    bits = blocks.bit_length() - 1
    depths = groups.bit_length() - 1
    matrices, rows, cols = grads.shape[1:]
    rank = warm_start.shape[1]
    width = cols // blocks
    rep = lax.axis_index("rep")
    core, spot = rep % 2, rep // 2
    place = jnp.stack([core, spot, rep * groups + lax.axis_index("grp")]).astype(jnp.int32)
    head_items = matrices * (rows // mat_momentum.shape[1])

    grads, errors = in_hbm(grads), in_hbm(errors)
    mat_momentum, mat_weights = map(in_hbm, (mat_momentum, mat_weights))

    front, back = parted(blocks)
    other_front, other_back = combine(place, grads, errors, False, [front, back], blocks)
    arrived_front = in_vmem(exchange(other_front, "core"))
    (own_front,) = combine(place, grads, errors, True, [front], blocks)
    go = fold([[(own_front, i), (arrived_front, i)] for i in range(len(front))])
    ahead = front, 0, exchange(go, "plane", 0)
    later, go, leaves = lax.optimization_barrier((place, go, other_back))
    arrived_back = in_vmem(exchange(leaves, "core"))
    own_back, other_p, own_part = combine(
        later, grads, errors, True, [back], blocks, ((False, (front, back), True), (True, (front,), False)),
        (warm_start, vec_grads, other_front, other_back, own_front),
    )
    own_c, other_c = (own_front, own_back), (other_front, other_back)

    arrived_c = arrived_front, arrived_back
    terms = [[(c[part], at) for c in (own_c, arrived_c)] for part, at in (within(p, blocks) for p in range(blocks))]

    def send(goes, stage, after=()):
        return goes, stage, exchange(fold([terms[p] for p in goes], after), "plane", stage)

    def land(goes, stage, arrived):
        arrived = in_vmem(arrived)
        for i, p in enumerate(goes):
            terms[p ^ (1 << stage)].append((arrived, i))

    rest = [p for p in range(blocks) if p & 3 == 1]
    pending = [send(rest, 0)]

    own_p = own_factor(later, own_back, back, own_part, warm_start, vec_grads, blocks)
    packed = own_p + exchange(other_p, "core")
    land(*ahead)
    goes = [p for p in range(blocks) if p & 3 == 2]
    packed, mm, mw, go = hop(
        packed, "plane", bits - 1,
        lambda *x: [*banks(*x), fold([terms[p] for p in goes])], mat_momentum, mat_weights,
    )
    pending.append((goes, 1, exchange(go, "plane", 1)))
    for stage in range(2, bits):
        while pending:
            land(*pending.pop(0))
        goes = [p for p in range(blocks) if p >> stage & 1 and not p & ((1 << stage) - 1)]
        pending.append(send(goes, stage, (packed,)))
    packed = packed + sum(exchange(packed, "depth", step) for step in rounds(groups))
    for step in range(bits - 2, 0, -1):
        packed = hop(packed, "plane", step)
    land(*pending.pop(0))
    packed, keep = hop(packed, "plane", 0, lambda *x: [fold([list(zip(x, [at for _, at in terms[0]]))])],
                       *[a for a, _ in terms[0]])
    terms[0] = [(keep, 0)]
    while pending:
        land(*pending.pop(0))

    kept_sum, v = small_call(
        functools.partial(project_kernel, places=[at for _, at in terms[0]], count=count),
        "project", [(rows, width), (rank, width)], packed, *[a for a, _ in terms[0]],
    )
    square = (rank, rank)
    state = (3, rank, rank)
    depth = rounds(groups)
    v, first_state = hop(
        v, "depth", depth,
        lambda x: small_call(
            functools.partial(first_begin_kernel, rows=rows, count=count), "root1a", [state], x
        ), packed,
    )
    (u,) = small_call(functools.partial(lift_kernel, count=count), "lift", [(rank * rows // LANES, LANES)], v, kept_sum)
    u, first_root = hop(u, "depth", depth, lambda x: small_call(first_end_kernel, "root1b", [square], x), first_state)
    u, vec_momentum_out, vec_weights_out = hop(
        u, "place", rounds(blocks),
        lambda x, y: gains(place, owners, x, y, vec_momentum, vec_weights, count, head_items),
        packed, exchange(packed, "core"),
    )
    (v,) = small_call(functools.partial(lower_kernel, count=count), "lower", [(rank, width)], u, kept_sum)
    def second(a, u):
        (begun,) = small_call(functools.partial(second_begin_kernel, rows=rows), "root2a", [state], a, u)
        return small_call(
            functools.partial(second_end_kernel, rows=rows), "root2b", [(rank, lanes(rows + rank))], begun, a, u
        )

    v, own_f = hop(v, "depth", depth, second, first_root, u)

    shapes = [errors.shape, mat_momentum.shape, mat_weights.shape]
    swapped = exchange(jnp.concatenate([v, own_f], axis=1), "core")
    other_v, other_f = swapped[None, :, :width], swapped[:, width:]
    v = v[None]
    arrived = {p: exchange(v, "place", p) for p in rounds(blocks)}
    arrived = [arrived[p] for p in range(1, blocks)]
    *outs, left = finish(
        [0], (), (), place, owners, v, other_v, own_f, other_f, own_c, other_c, shapes, mm, mw
    )
    *arrived, left = lax.optimization_barrier((*arrived, left))
    v = jnp.concatenate(arrived, axis=0)
    other_v = exchange(v, "core")
    others = list(range(1, blocks))
    left = (left, *ready(others, v, own_f, own_c, left, blocks))
    outs = finish(others, left, outs, place, owners, v, other_v, own_f, other_f, own_c, other_c, shapes, mm, mw)
    new_errors, mat_momentum_out, mat_weights_out = outs
    return (new_errors, mat_momentum_out, mat_weights_out, vec_momentum_out, vec_weights_out)


def solution(mesh):
    both = ("rep", "grp")
    return jax.shard_map(
        local,
        mesh=mesh,
        in_specs=(
            P(both, None, None, None),
            P(both, None, None, None),
            P(),
            P(both, None, None),
            P(),
            P(both, None, None),
            P(both, None, None),
            P(both, None),
            P(both, None),
        ),
        out_specs=(
            P(both, None, None, None),
            P(both, None, None),
            P(both, None, None),
            P(both, None),
            P(both, None),
        ),
        check_vma=False,
    )
```

```python
import functools

import jax
import jax.numpy as jnp
from jax import lax
from jax.experimental import pallas as pl
from jax.experimental.pallas import tpu as pltpu
from jax.sharding import PartitionSpec as P

ROOT_ITERS = 12
LANES = 128
f32 = jnp.float32
NN = ((1,), (0,))
NT = ((1,), (1,))
TN = ((0,), (0,))
ANY = pl.BlockSpec(memory_space=pl.ANY)
VMEM = pl.BlockSpec(memory_space=pltpu.VMEM)
SMEM = pl.BlockSpec(memory_space=pltpu.SMEM)


def dot(a, b, dims=NN):
    return lax.dot_general(
        a, b, (dims, ((), ())), precision=lax.Precision.HIGHEST, preferred_element_type=f32
    )


def split3(a):
    high = a.astype(jnp.bfloat16)
    rest = a - high.astype(f32)
    middle = rest.astype(jnp.bfloat16)
    low = (rest - middle.astype(f32)).astype(jnp.bfloat16)
    return high, middle, low


def lanes(n):
    return -(-n // LANES) * LANES


def pack_factor(out, u):
    rank, rows = u.shape
    whole, left = divmod(rows, LANES)
    for i in range(whole):
        out[i * rank : (i + 1) * rank, :] = u[:, i * LANES : (i + 1) * LANES]
    if left:
        short = rank * left // LANES
        for i in range(LANES // left):
            out[whole * rank : whole * rank + short, i * left : (i + 1) * left] = u[
                i * short : (i + 1) * short, whole * LANES :
            ]


def unpack_factor(x, rank, rows):
    whole, left = divmod(rows, LANES)
    parts = [x[i * rank : (i + 1) * rank, :] for i in range(whole)]
    if left:
        short = rank * left // LANES
        tail = x[whole * rank : whole * rank + short, :]
        parts.append(jnp.concatenate([tail[:, i * left : (i + 1) * left] for i in range(LANES // left)], axis=0))
    return jnp.concatenate(parts, axis=1)


def in_hbm(a):
    return pltpu.with_memory_space_constraint(a, pltpu.HBM)


def in_vmem(a):
    return pltpu.with_memory_space_constraint(a, pltpu.VMEM)


def call(kernel, name, in_specs, out_specs, out_shape, operands, mib=4, flops=1, nbytes=1, scratch=(), aliases={}):
    return pl.pallas_call(
        kernel,
        in_specs=in_specs,
        out_specs=out_specs,
        out_shape=out_shape,
        scratch_shapes=scratch,
        input_output_aliases=aliases,
        compiler_params=pltpu.CompilerParams(vmem_limit_bytes=mib << 20),
        cost_estimate=pl.CostEstimate(flops=flops, bytes_accessed=nbytes, transcendentals=0),
        name=name,
    )(*operands)


def small_call(kernel, name, shapes, *operands):
    return call(
        kernel,
        name,
        [VMEM] * len(operands),
        [VMEM] * len(shapes),
        [jax.ShapeDtypeStruct(s, f32) for s in shapes],
        operands,
        flops=12_000_000,
        nbytes=4 * sum(o.size for o in operands),
    )


def block_columns(place, own, p, blocks, width):
    bits = blocks.bit_length() - 1
    core = place[0] if own else 1 - place[0]
    block = place[1] ^ jnp.where(core == 0, p, mirror(p, bits))
    return pl.ds(pl.multiple_of(block * width, width), width)


def part_of_factor(place, own, w_ref, part, places, blocks):
    _, rows, width = part.shape
    rank = w_ref.shape[1]
    m = place[0] if own else 1 - place[0]
    terms = jnp.zeros((rows, 3 * rank), f32)
    for i, p in enumerate(places):
        w_high, w_middle, w_low = split3(w_ref[m, :, block_columns(place, own, p, blocks, width)])
        high, middle, _ = split3(part[i])
        for piece, pieces in (
            (high, (w_high, w_middle, w_low)),
            (middle, (w_high, w_middle, jnp.zeros_like(w_low))),
        ):
            terms += lax.dot_general(
                piece, jnp.concatenate(pieces, axis=0), (NT, ((), ())), preferred_element_type=f32
            )
    return (terms[:, :rank] + terms[:, rank : 2 * rank] + terms[:, 2 * rank :]).T


def write_factor(out, place, own, factor, vec_ref):
    rank, rows = factor.shape
    pack_factor(out, factor)
    base = rank * rows // LANES
    mine = jnp.where((place[0] if own else 1 - place[0]) == 0, vec_ref[0, 0:1, :], vec_ref[0, 1:2, :])
    for i in range(vec_ref.shape[2] // LANES):
        out[base + i : base + i + 1, :] = mine[:, i * LANES : (i + 1) * LANES]


def factor_shape(rows, warm_start):
    _, rank, cols = warm_start.shape
    return jax.ShapeDtypeStruct(((rank * rows + cols) // LANES, LANES), f32)


def factor_kernel(place, w_ref, vec_ref, part, before, out, *, places, blocks):
    factor = before[...] + part_of_factor(place, True, w_ref, part, places, blocks)
    write_factor(out, place, True, factor, vec_ref)


def own_factor(place, part, places, before, warm_start, vec_grads, blocks):
    return call(
        functools.partial(factor_kernel, places=places, blocks=blocks),
        "factor",
        [SMEM] + [VMEM] * 4,
        VMEM,
        factor_shape(part.shape[1], warm_start),
        (place, warm_start, vec_grads, part, before),
    )


def combine_kernel(place, g_hbm, e_hbm, *refs, own, groups, blocks, sides):
    refs = list(refs)
    if sides:
        w_ref, vec_ref = refs.pop(0), refs.pop(0)
    ins = [[refs.pop(0) for _ in spots] for _, spots, _ in sides]
    outs = [refs.pop(0) for _ in groups]
    factors = [refs.pop(0) for _ in sides]
    g, e, sem = refs
    m = place[0] if own else 1 - place[0]
    loads = []
    for i, p in enumerate(sum(groups, [])):
        where = block_columns(place, own, p, blocks, g.shape[2])
        loads.append(
            (
                pltpu.make_async_copy(g_hbm.at[0, m, :, where], g.at[i], sem.at[i, 0]),
                pltpu.make_async_copy(e_hbm.at[0, m, :, where], e.at[i], sem.at[i, 1]),
            )
        )
        for load in loads[-1]:
            load.start()
    for (whose, spots, whole), parts, factor in zip(sides, ins, factors):
        value = sum(part_of_factor(place, whose, w_ref, part, at, blocks) for part, at in zip(parts, spots))
        if whole:
            write_factor(factor, place, whose, value, vec_ref)
        else:
            factor[...] = value
    i = 0
    for out in outs:
        for at in range(out.shape[0]):
            for load in loads[i]:
                load.wait()
            out[at] = g[i].astype(f32) + e[i]
            i += 1


def combine(place, grads, errors, own, groups, blocks, sides=(), extra=()):
    rows, cols = grads.shape[2:]
    width = cols // blocks
    shape = (sum(map(len, groups)), rows, width)
    shapes = [
        factor_shape(rows, extra[0]) if whole else jax.ShapeDtypeStruct((extra[0].shape[1], rows), f32)
        for _, _, whole in sides
    ]
    return call(
        functools.partial(combine_kernel, own=own, groups=groups, blocks=blocks, sides=sides),
        ("own" if own else "other") + str(len(sides)),
        [SMEM, ANY, ANY] + [VMEM] * len(extra),
        [VMEM] * (len(groups) + len(sides)),
        [pltpu.VMEM((len(group), rows, width), f32) for group in groups] + shapes,
        (place, grads, errors, *extra),
        mib=8,
        scratch=[
            pltpu.VMEM(shape, grads.dtype), pltpu.VMEM(shape, f32), pltpu.SemaphoreType.DMA((shape[0], 2))
        ],
    )


def parted(blocks):
    front = [p for p in range(blocks) if p & 3 == 3]
    return front, [p for p in range(blocks) if p & 3 == 1] + list(range(0, blocks, 2))


def within(p, blocks):
    front, back = parted(blocks)
    return (0, front.index(p)) if p in front else (1, back.index(p))


def fold_kernel(*refs, picks):
    for i, pick in enumerate(picks):
        refs[-1][i] = sum(refs[k][at] for k, at in pick)


def fold(terms, after=()):
    arrays, picks = [], []
    for pairs in terms:
        pick = []
        for a, at in pairs:
            if not any(a is b for b in arrays):
                arrays.append(a)
            pick.append((next(k for k, b in enumerate(arrays) if a is b), at))
        picks.append(pick)
    shape = (len(terms),) + arrays[0].shape[1:]
    return call(
        functools.partial(fold_kernel, picks=picks),
        "fold",
        [VMEM] * len(arrays) + [ANY] * len(after),
        VMEM,
        pltpu.VMEM(shape, f32),
        (*arrays, *after),
        nbytes=4 * len(picks[0]) * shape[0] * shape[1] * shape[2],
    )


def project_kernel(x_ref, *refs, places, count):
    parts, (s_ref, v_ref) = refs[:-2], refs[-2:]
    block = sum(part[at] for part, at in zip(parts, places))
    s_ref[...] = block
    v_ref[...] = dot(unpack_factor(x_ref[...], v_ref.shape[0], block.shape[0]) / count, block) / count


def lift_kernel(v_ref, s_ref, u_ref, *, count):
    pack_factor(u_ref, dot(v_ref[...], s_ref[...], NT) / count)


def lower_kernel(u_ref, s_ref, v_ref, *, count):
    v_ref[...] = dot(unpack_factor(u_ref[...], v_ref.shape[0], s_ref.shape[0]), s_ref[...]) / count


def identity(rank):
    return (
        lax.broadcasted_iota(jnp.int32, (rank, rank), 0)
        == lax.broadcasted_iota(jnp.int32, (rank, rank), 1)
    ).astype(f32)


def sweeps(left, right, first, last):
    eye = identity(left.shape[0])
    for sweep in range(first, last):
        middle = 1.5 * eye - 0.5 * (left if sweep == 0 else dot(right, left))
        right = middle if sweep == 0 else dot(middle, right)
        if sweep + 1 < ROOT_ITERS:
            left = dot(left, middle)
    return left, right


def root_begin(gram, state):
    spread = jnp.sqrt(jnp.sum(gram * gram, keepdims=True))
    left, right = sweeps(gram / spread, None, 0, ROOT_ITERS // 2)
    state[0], state[1] = left, right
    state[2] = jnp.broadcast_to(spread, gram.shape)


def root_end(state):
    _, right = sweeps(state[0], state[1], ROOT_ITERS // 2, ROOT_ITERS)
    return right / jnp.sqrt(state[2])


def first_begin_kernel(x_ref, state, *, rows, count):
    factor = unpack_factor(x_ref[...], state.shape[1], rows) / count
    root_begin(dot(factor, factor, NT), state)


def first_end_kernel(state, a_ref):
    a_ref[...] = root_end(state)


def second_begin_kernel(a_ref, u_ref, state, *, rows):
    a = a_ref[...]
    u = unpack_factor(u_ref[...], a.shape[0], rows)
    root_begin(dot(a, dot(dot(u, u, NT), a), TN), state)


def second_end_kernel(state, a_ref, u_ref, f_ref, *, rows):
    rank = a_ref.shape[0]
    u = unpack_factor(u_ref[...], rank, rows)
    both = dot(a_ref[...], root_end(state))
    f_ref[...] = jnp.zeros(f_ref.shape, f32)
    f_ref[:, :rows] = dot(both, u, TN)
    f_ref[:, rows : rows + rank] = both


def taken_items(place, owners, slots):
    items, before = [jnp.int32(-1)] * slots, jnp.int32(0)
    for item in range(owners.shape[0]):
        mine = owners[item] == place[2]
        items = [jnp.where(mine & (before == slot), item, old) for slot, old in enumerate(items)]
        before = before + jnp.where(mine, 1, 0)
    return items


def gains_kernel(place, owners, own_ref, other_ref, mv_ref, wv_ref, mo_ref, wo_ref, vec, *, count, first):
    for i in range(mv_ref.shape[1] // LANES):
        at = slice(i * LANES, (i + 1) * LANES)
        for k, ref in enumerate((own_ref, other_ref)):
            row = ref.shape[0] - mv_ref.shape[1] // LANES + i
            vec[k : k + 1, at] = ref[row : row + 1, :] / count
    for slot, item in enumerate(taken_items(place, owners, mv_ref.shape[0])):
        row = jnp.where(item - first == place[0], vec[0:1, :], vec[1:2, :])
        old, weight = mv_ref[slot : slot + 1, :], wv_ref[slot : slot + 1, :]
        new = 0.9 * old + row
        mo_ref[slot : slot + 1, :] = jnp.where(item >= first, new, old)
        wo_ref[slot : slot + 1, :] = jnp.where(item >= first, weight - 0.5 * new, weight)


def gains(place, owners, own, other, vec_momentum, vec_weights, count, first):
    return call(
        functools.partial(gains_kernel, count=count, first=first),
        "gains",
        [SMEM, SMEM] + [VMEM] * 4,
        [VMEM] * 2,
        [jax.ShapeDtypeStruct(vec_momentum.shape, f32)] * 2,
        (place, owners, own, other, vec_momentum, vec_weights),
        flops=10 * vec_momentum.size,
        nbytes=16 * vec_momentum.size,
        scratch=[pltpu.VMEM((2, vec_momentum.shape[1]), f32)],
    )


def idle(item, items):
    return (item < 0) | (item >= items)


def banks_kernel(place, owners, mm_hbm, mw_hbm, mm, mw, mo_hbm, wo_hbm, sem, *, items):
    loads = (pltpu.make_async_copy(mm_hbm, mm, sem.at[0, 0]), pltpu.make_async_copy(mw_hbm, mw, sem.at[0, 1]))
    for load in loads:
        load.start()
    for load in loads:
        load.wait()
    stores = []
    for slot, item in enumerate(taken_items(place, owners, mm.shape[0])):
        copies = (
            pltpu.make_async_copy(mm.at[slot], mo_hbm.at[slot], sem.at[1 + slot, 0]),
            pltpu.make_async_copy(mw.at[slot], wo_hbm.at[slot], sem.at[1 + slot, 1]),
        )
        stores.append((idle(item, items), copies))

        @pl.when(stores[-1][0])
        def _():
            for copy in copies:
                copy.start()

    for writes, copies in stores:

        @pl.when(writes)
        def _():
            for copy in copies:
                copy.wait()


def banks(place, owners, mat_momentum, mat_weights, items):
    shape = mat_momentum.shape
    return call(
        functools.partial(banks_kernel, items=items),
        "banks",
        [SMEM, SMEM, ANY, ANY],
        [VMEM] * 2 + [ANY] * 2,
        [pltpu.VMEM(shape, f32)] * 2 + [pltpu.HBM(shape, f32)] * 2,
        (place, owners, mat_momentum, mat_weights),
        nbytes=8 * mat_momentum.size,
        scratch=[pltpu.SemaphoreType.DMA((1 + shape[0], 2))],
    )


def turned(f_ref, v, rows):
    rank = v.shape[0]
    high, middle, low = split3(dot(f_ref[:, rows : rows + rank], v, TN))
    return jnp.concatenate([high, middle, high, low, high, middle], axis=0)


def left_side(f_ref, rows):
    high, middle, low = split3(f_ref[:, :rows].T)
    return jnp.concatenate([high, high, middle, high, low, middle], axis=1)


def ready_kernel(v_ref, f_ref, c_front, c_back, errors, approx):
    blocks, rows, _ = errors.shape
    left = left_side(f_ref, rows)
    rights = [turned(f_ref, v_ref[p], rows) for p in range(blocks)]
    for p in range(blocks):
        product = jnp.dot(left, rights[p], preferred_element_type=f32)
        part, at = within(p, blocks)
        approx[p] = product
        errors[p] = (c_front, c_back)[part][at] - product


def ready(v, f, own_c):
    shape = (v.shape[0],) + own_c[0].shape[1:]
    return call(
        ready_kernel,
        "ready",
        [VMEM] * 4,
        [VMEM] * 2,
        [pltpu.VMEM(shape, f32)] * 2,
        (v, f, *own_c),
        mib=8,
    )


def finish_kernel(
    place, owners, v_ref, f_ref, c_front, c_back, own_errors, own_approx, mm, mw, _, __,
    n_hbm, mo_hbm, wo_hbm, errors, approx, moment, weight, sem, bank_sem, *, head
):
    blocks, rows, width = errors.shape
    per = rows // head
    items = taken_items(place, owners, mm.shape[0])
    stores, bank_stores = [], []

    def store(p, i, source):
        m = place[0] if i == 0 else 1 - place[0]
        columns = block_columns(place, i == 0, p, blocks, width)
        stores.append(pltpu.make_async_copy(source, n_hbm.at[0, m, :, columns], sem.at[p, i]))
        stores[-1].start()

    def step(p, i, source):
        m = place[0] if i == 0 else 1 - place[0]
        columns = block_columns(place, i == 0, p, blocks, width)
        for slot, item in enumerate(items):
            taken = (item >= m * per) & (item < (m + 1) * per)
            copies = (
                pltpu.make_async_copy(
                    moment.at[p, i, slot], mo_hbm.at[slot, :, columns], bank_sem.at[p, i, slot, 0]
                ),
                pltpu.make_async_copy(
                    weight.at[p, i, slot], wo_hbm.at[slot, :, columns], bank_sem.at[p, i, slot, 1]
                ),
            )

            @pl.when(taken)
            def _():
                at = pl.ds(pl.multiple_of((item - m * per) * head, head), head)
                new = 0.9 * mm[slot, :, columns] + source[at, :]
                moment[p, i, slot] = new
                weight[p, i, slot] = mw[slot, :, columns] - 0.5 * new
                for copy in copies:
                    copy.start()

            bank_stores.append((taken, copies))

    for p in range(blocks):
        store(p, 0, own_errors.at[p])
        step(p, 0, own_approx.at[p])
    left = left_side(f_ref, rows)
    rights = [turned(f_ref, v_ref[p], rows) for p in range(blocks)]
    for p in range(blocks):
        product = jnp.dot(left, rights[p], preferred_element_type=f32)
        part, at = within(p, blocks)
        approx[p] = product
        errors[p] = (c_front, c_back)[part][at] - product
        store(p, 1, errors.at[p])
    for p in range(blocks):
        step(p, 1, approx.at[p])
    for copy in stores:
        copy.wait()
    for writes, copies in bank_stores:

        @pl.when(writes)
        def _():
            for copy in copies:
                copy.wait()


def finish(place, owners, v, f, other_c, made, shapes, mm, mw, mo, wo):
    blocks, rank, width = v.shape
    rows = other_c[0].shape[1]
    slots, head = mm.shape[:2]
    block = pltpu.VMEM((blocks, rows, width), f32)
    rows_of_slots = pltpu.VMEM((blocks, 2, slots, head, width), f32)
    return call(
        functools.partial(finish_kernel, head=head),
        "finish",
        [SMEM, SMEM] + [VMEM] * 8 + [ANY] * 2,
        [ANY] * 3,
        [pltpu.HBM(shape, f32) for shape in shapes],
        (place, owners, v, f, *other_c, *made, mm, mw, mo, wo),
        mib=20,
        flops=2 * blocks * rows * width * 6 * rank,
        nbytes=8 * blocks * rows * width,
        scratch=[
            block,
            block,
            rows_of_slots,
            rows_of_slots,
            pltpu.SemaphoreType.DMA((blocks, 2)),
            pltpu.SemaphoreType.DMA((blocks, 2, slots, 2)),
        ],
        aliases={10: 1, 11: 2},
    )


def mirror(p, bits):
    return sum((p >> i & 1) << (bits - 1 - i) for i in range(bits))


def partner(kind, step):
    planes = (lax.axis_size("rep") // 2).bit_length() - 1
    depths = lax.axis_size("grp").bit_length() - 1

    def of(rep, grp):
        if kind == "core":
            return rep ^ 1, grp
        if kind == "plane":
            return rep ^ (2 << (step if rep % 2 == 0 else planes - 1 - step)), grp
        if kind == "depth":
            return rep, grp ^ step
        if kind == "place":
            return rep ^ 2 * (step if rep % 2 == 0 else mirror(step, planes)), grp
        return rep, grp ^ (1 << (step if rep % 2 == 0 else depths - 1 - step))

    return of


def rounds(places):
    return [1, *range(places - 1, 1, -1)]


def exchange(a, kind, step=0):
    groups = lax.axis_size("grp")
    of = partner(kind, step)
    pairs = []
    for rep in range(lax.axis_size("rep")):
        for grp in range(groups):
            to_rep, to_grp = of(rep, grp)
            pairs.append((rep * groups + grp, to_rep * groups + to_grp))
    return lax.ppermute(a, ("rep", "grp"), pairs)


def hop(a, kind, step, work=None, *operands):
    if work is None:
        return a + exchange(a, kind, step)
    a, *operands = lax.optimization_barrier((a, *operands))
    steps = step if isinstance(step, list) else [step]
    arrived = [exchange(a, kind, each) for each in steps]
    done = work(*operands)
    arrived, done = lax.optimization_barrier((arrived, list(done)))
    return sum(arrived, a), *done


def local(grads, errors, warm_start, vec_grads, owners, mat_momentum, mat_weights, vec_momentum, vec_weights):
    reps, groups = lax.axis_size("rep"), lax.axis_size("grp")
    count = float(reps * groups)
    blocks = reps // 2
    bits = blocks.bit_length() - 1
    depths = groups.bit_length() - 1
    matrices, rows, cols = grads.shape[1:]
    rank = warm_start.shape[1]
    width = cols // blocks
    rep = lax.axis_index("rep")
    core, spot = rep % 2, rep // 2
    place = jnp.stack([core, spot, rep * groups + lax.axis_index("grp")]).astype(jnp.int32)
    head_items = matrices * (rows // mat_momentum.shape[1])

    grads, errors = in_hbm(grads), in_hbm(errors)
    mat_momentum, mat_weights = map(in_hbm, (mat_momentum, mat_weights))

    front, back = parted(blocks)
    other_front, other_back = combine(place, grads, errors, False, [front, back], blocks)
    arrived_front = in_vmem(exchange(other_front, "core"))
    (own_front,) = combine(place, grads, errors, True, [front], blocks)
    go = fold([[(own_front, i), (arrived_front, i)] for i in range(len(front))])
    ahead = front, 0, exchange(go, "plane", 0)
    later, go, leaves = lax.optimization_barrier((place, go, other_back))
    arrived_back = in_vmem(exchange(leaves, "core"))
    own_back, other_p, own_part = combine(
        later, grads, errors, True, [back], blocks, ((False, (front, back), True), (True, (front,), False)),
        (warm_start, vec_grads, other_front, other_back, own_front),
    )
    own_c, other_c = (own_front, own_back), (other_front, other_back)

    arrived_c = arrived_front, arrived_back
    terms = [[(c[part], at) for c in (own_c, arrived_c)] for part, at in (within(p, blocks) for p in range(blocks))]

    def send(goes, stage, after=()):
        return goes, stage, exchange(fold([terms[p] for p in goes], after), "plane", stage)

    def land(goes, stage, arrived):
        arrived = in_vmem(arrived)
        for i, p in enumerate(goes):
            terms[p ^ (1 << stage)].append((arrived, i))

    rest = [p for p in range(blocks) if p & 3 == 1]

    own_p = own_factor(later, own_back, back, own_part, warm_start, vec_grads, blocks)
    packed = own_p + exchange(other_p, "core")
    pending = [send(rest, 0, (packed,))]
    land(*ahead)
    goes = [p for p in range(blocks) if p & 3 == 2]
    packed, mm, mw, mo, wo, go = hop(
        packed, "plane", bits - 1,
        lambda *x: [*banks(place, owners, *x, head_items), fold([terms[p] for p in goes])], mat_momentum, mat_weights,
    )
    pending.append((goes, 1, exchange(go, "plane", 1)))
    for stage in range(2, bits):
        while pending:
            land(*pending.pop(0))
        goes = [p for p in range(blocks) if p >> stage & 1 and not p & ((1 << stage) - 1)]
        pending.append(send(goes, stage, (packed,)))
    packed = packed + sum(exchange(packed, "depth", step) for step in rounds(groups))
    for step in range(bits - 2, 0, -1):
        packed = hop(packed, "plane", step)
    land(*pending.pop(0))
    packed, keep = hop(packed, "plane", 0, lambda *x: [fold([list(zip(x, [at for _, at in terms[0]]))])],
                       *[a for a, _ in terms[0]])
    terms[0] = [(keep, 0)]
    while pending:
        land(*pending.pop(0))

    kept_sum, v = small_call(
        functools.partial(project_kernel, places=[at for _, at in terms[0]], count=count),
        "project", [(rows, width), (rank, width)], packed, *[a for a, _ in terms[0]],
    )
    square = (rank, rank)
    state = (3, rank, rank)
    depth = rounds(groups)
    v, first_state = hop(
        v, "depth", depth,
        lambda x: small_call(
            functools.partial(first_begin_kernel, rows=rows, count=count), "root1a", [state], x
        ), packed,
    )
    (u,) = small_call(functools.partial(lift_kernel, count=count), "lift", [(rank * rows // LANES, LANES)], v, kept_sum)
    u, first_root = hop(u, "depth", depth, lambda x: small_call(first_end_kernel, "root1b", [square], x), first_state)
    u, vec_momentum_out, vec_weights_out = hop(
        u, "place", rounds(blocks),
        lambda x, y: gains(place, owners, x, y, vec_momentum, vec_weights, count, head_items),
        packed, exchange(packed, "core"),
    )
    (v,) = small_call(functools.partial(lower_kernel, count=count), "lower", [(rank, width)], u, kept_sum)
    v, second_state = hop(
        v, "depth", depth,
        lambda *x: small_call(functools.partial(second_begin_kernel, rows=rows), "root2a", [state], *x),
        first_root, u,
    )

    v, *tied = lax.optimization_barrier((v[None], second_state, first_root, u))
    arrived = {p: exchange(v, "place", p) for p in rounds(blocks)}
    arrived = [arrived[p] for p in range(1, blocks)]
    (own_f,) = small_call(
        functools.partial(second_end_kernel, rows=rows), "root2b", [(rank, lanes(rows + rank))], *tied
    )
    other_f = exchange(own_f, "core")
    arrived, own_f = lax.optimization_barrier((arrived, own_f))
    v = jnp.concatenate([v, *arrived], axis=0)
    other_v = exchange(v, "core")
    made = ready(v, own_f, own_c)
    shapes = [errors.shape, mat_momentum.shape, mat_weights.shape]
    outs = finish(place, owners, other_v, other_f, other_c, made, shapes, mm, mw, mo, wo)
    new_errors, mat_momentum_out, mat_weights_out = outs
    return (new_errors, mat_momentum_out, mat_weights_out, vec_momentum_out, vec_weights_out)


def solution(mesh):
    both = ("rep", "grp")
    return jax.shard_map(
        local,
        mesh=mesh,
        in_specs=(
            P(both, None, None, None),
            P(both, None, None, None),
            P(),
            P(both, None, None),
            P(),
            P(both, None, None),
            P(both, None, None),
            P(both, None),
            P(both, None),
        ),
        out_specs=(
            P(both, None, None, None),
            P(both, None, None),
            P(both, None, None),
            P(both, None),
            P(both, None),
        ),
        check_vma=False,
    )
```
